512 devices in a mesh: energy: 64 (over y_hi, z, core), pair: 8 (over x, y_lo).
Axes of the slice: x: 4, y: 4 (y_hi: 2, y_lo: 2; y = y_hi * 2 + y_lo), z: 16, core: 2. Of those that a mesh axis runs over, the one named last changes fastest.
Arguments:
- g_less: bfloat16 [2, 4096, 8192], P(None, 'energy', 'pair'), may hold values from -6 to 6
- g_greater: bfloat16 [2, 4096, 8192], P(None, 'energy', 'pair'), may hold values from -6 to 6
- pair_slot: int32 [8, 1024], P('pair'), may hold values from 0 to 1023, each once within a row
Outputs:
- pol_less: bfloat16 [2, 4096, 8192], P(None, 'energy', 'pair')
- pol_greater: bfloat16 [2, 4096, 8192], P(None, 'energy', 'pair')
The draws below stay inside these ranges and needn't reach their ends.
Inputs may be any that keep to these rules, and one draw needn't show every extreme that they name: Each row of pair_slot is a permutation of the slots; rows p and p xor 1 pair their elements as mirrors through equal entries.
All inputs are finite; a program needn't handle non-finite values.
Results may differ from the reference program's by a relative error of at most 0.011.
Values may be sent and summed in bfloat16 or wider, within the bound.
A program may use at most 64 MiB of HBM per device.

```python
import math
import jax
import jax.numpy as jnp
from jax import lax

NE = 4096
ELEM_DEV = 1024
GROUPS = 8
ELEMS = 8192


def levels(stream_key, shape, cuts, least, high):
    def one(axis_at, blocks):
        steps = jax.random.uniform(jax.random.fold_in(jax.random.fold_in(stream_key, 6), axis_at), (blocks,), jnp.float32, least / len(cuts), high / len(cuts))
        return jnp.repeat(jnp.exp(steps), shape[axis_at] // blocks).reshape((-1,) + (1,) * (len(shape) - axis_at - 1))

    factor_of = one(*cuts[0])
    for cut in cuts[1:]:
        factor_of = factor_of * one(*cut)
    return factor_of


def centred(stream_key, shape, deviation, limit, cuts=(), kind=jnp.bfloat16):
    entries = jax.random.normal(stream_key, shape, jnp.float32) * deviation
    if len(cuts) > 0:
        entries = levels(stream_key, shape, cuts, -0.22, 0.18) * entries
    return jnp.clip(entries, min=-limit, max=limit).astype(kind)


def setup_inputs(seed: int = 0) -> dict:
    splits = jax.random.split(jax.random.key(seed), 4)
    return {
        "g_less": centred(splits[0], (2, NE, ELEMS), 1.0, 6.0, ((1, 64), (2, 8))),
        "g_greater": centred(splits[1], (2, NE, ELEMS), 1.0, 6.0, ((1, 64), (2, 8))),
        "pair_slot": jax.vmap(lambda own: jax.random.permutation(own, ELEM_DEV))(jax.random.split(splits[2], GROUPS)).reshape((GROUPS, ELEM_DEV)).astype(jnp.int32),
    }


def correlate(first, second):
    length = 2 * NE
    spec_first = jnp.fft.fft(first, n=length, axis=0)
    spec_second = jnp.fft.ifft(second, n=length, axis=0) * length
    lagged = jnp.fft.ifft(spec_first * spec_second, axis=0)[:NE]
    value = -1j * lagged / math.sqrt(NE)
    return jnp.stack([jnp.real(value), jnp.imag(value)]).astype(jnp.bfloat16)

def to_complex(parts):
    return parts[0].astype(jnp.float32) + 1j * parts[1].astype(jnp.float32)

def reference(g_less, g_greater, pair_slot):
    groups = pair_slot.shape[0]
    per_group = pair_slot.shape[1]
    inverse = jnp.argsort(pair_slot, axis=1).astype(jnp.int32)
    partner = jnp.bitwise_xor(jnp.arange(groups, dtype=jnp.int32), 1)
    mirror_local = jnp.take_along_axis(inverse[partner], pair_slot, axis=1)
    mirror = (partner[:, None] * per_group + mirror_local).reshape(-1).astype(jnp.int32)
    mirror_less = jnp.take(g_less, mirror, axis=2)
    mirror_greater = jnp.take(g_greater, mirror, axis=2)
    total = g_less.shape[2]
    block = math.gcd(total, 256)
    count = total // block

    def split(array):
        return jnp.moveaxis(array.reshape(2, NE, count, block), 2, 0)

    def per_block(items):
        own_less, own_greater, other_less, other_greater = items
        result_less = correlate(to_complex(own_less), to_complex(other_greater))
        result_greater = correlate(to_complex(own_greater), to_complex(other_less))
        return (result_less, result_greater)
    out_less, out_greater = lax.map(per_block, (split(g_less), split(g_greater), split(mirror_less), split(mirror_greater)))

    def merge_back(array):
        return jnp.moveaxis(array, 0, 2).reshape(2, NE, total)
    return (merge_back(out_less), merge_back(out_greater))
```

```python
import functools
import math

import jax
import jax.numpy as jnp
import ml_dtypes
import numpy as np
from jax import lax
from jax.experimental import pallas as pl
from jax.experimental.pallas import tpu as pltpu
from jax.sharding import PartitionSpec as P

NE = 4096
N0 = 64
EDEV = 64
OWNERS = 2 * EDEV
SLOTS = 1024
MINE = SLOTS // OWNERS
ROWS = 2 * MINE
K0 = 128
K1 = 64
LENGTH = 2 * NE
F32 = jnp.float32
BF16 = jnp.bfloat16
MESH = pl.DeviceIdType.MESH


def upper_lower(table):
    upper = table.astype(ml_dtypes.bfloat16)
    lower = (table - upper.astype(np.float64)).astype(ml_dtypes.bfloat16)
    return upper, lower


def cos_sin(rows, cols, period):
    angle = (np.arange(rows)[:, None] * np.arange(cols)[None, :] % period) * (2.0 * math.pi / period)
    return np.cos(angle), np.sin(angle)


def tables():
    lanes = lambda *parts: np.concatenate(parts, axis=1)
    both = lambda table: np.concatenate(upper_lower(table))
    straight = lambda part: np.kron(np.eye(2), part)
    crossed = lambda part: np.kron(np.eye(2)[::-1], part)
    c, s = cos_sin(K0, EDEV, K0)
    first = [lanes(*upper_lower(lanes(c, s))), lanes(*upper_lower(lanes(c, -s)))]
    c, s = cos_sin(N0, K1, K1)
    own = both(np.block([[straight(c), -straight(s)], [straight(s), straight(c)]]))
    far = both(np.block([[crossed(c), crossed(s)], [-crossed(s), crossed(c)]]))
    ahead = both(np.block([[straight(c), straight(s)], [-straight(s), straight(c)]]))
    behind = both(np.block([[crossed(c), crossed(s)], [crossed(s), -crossed(c)]]))
    c, s = cos_sin(EDEV, K0, K0)
    last = both(np.block([[c, -s], [s, c]]))
    coarse = np.concatenate(first + [own, far, ahead, behind, last])
    c, s = cos_sin(K0, N0, LENGTH)
    scale = 1.0 / (math.sqrt(NE) * LENGTH)
    fine = np.stack([lanes(c, c), lanes(s, s), lanes(s, s) * scale, -lanes(c, c) * scale])
    return coarse.reshape(-1, 128, 256).astype(np.float32), fine.astype(np.float32)


def dot(left, right, dims=((1,), (0,))):
    return lax.dot_general(left, right, (dims, ((), ())), preferred_element_type=F32)


def split(value):
    upper = value.astype(BF16)
    return upper, (value - upper.astype(F32)).astype(BF16)


def correlate(recv, send, coarse, fine, flat, y_own, y_far):
    first, own, far, ahead, behind, last = 0, 2, 6, 10, 14, 18
    flat[...] = recv[...].astype(F32).reshape(OWNERS * ROWS, 128)

    def line(side, part, slot):
        return pl.ds(side * ROWS + part * MINE + slot, EDEV, stride=2 * ROWS)

    def spectrum(side, slot, into):
        re, im = flat[line(side, 0, slot), :], flat[line(side, 1, slot), :]
        top = jnp.concatenate([re, im], axis=1).astype(BF16)
        bottom = jnp.concatenate([im, -re], axis=1).astype(BF16)
        step = dot(coarse[first + side], jnp.concatenate([top, bottom, top, bottom], axis=0))
        re, im = step[:, :128], step[:, 128:]
        c, s = fine[0], fine[1]
        if side == 0:
            re, im = re * c + im * s, im * c - re * s
        else:
            re, im = re * c - im * s, im * c + re * s
        into[pl.ds(slot * K0, K0), :] = jnp.concatenate(split(jnp.concatenate([re, im], axis=1)), axis=1)

    def forward(step, carry):
        for member in range(2):
            spectrum(0, step * 2 + member, y_own)
            spectrum(1, step * 2 + member, y_far)
        return carry

    lax.fori_loop(0, MINE // 2, forward, 0)

    def triple(value, table):
        upper = coarse[table : table + 2].reshape(256, 256)
        lower = coarse[table + 2 : table + 4].reshape(256, 256)
        return dot(
            jnp.concatenate([value, value[:, :256]], axis=1), jnp.concatenate([upper, upper, lower], axis=0)
        )

    group = 4

    def product(step, carry):
        rows = pl.ds(step * (group * K0), group * K0)
        left, right = triple(y_own[rows, :], own), triple(y_far[rows, :], far)
        a, b, c, d = left[:, :128], left[:, 128:], right[:, :128], right[:, 128:]
        spec = jnp.concatenate(split(jnp.concatenate([a * c - b * d, a * d + b * c], axis=1)), axis=1)
        lags = (triple(spec, ahead), triple(spec, behind))
        for member in range(group):
            tops, bottoms = [], []
            for part in lags:
                re, im = part[member * K0 : (member + 1) * K0, :128], part[member * K0 : (member + 1) * K0, 128:]
                tops.append(re * fine[2] - im * fine[3])
                bottoms.append(re * fine[3] + im * fine[2])
            upper, lower = split(
                jnp.concatenate([jnp.concatenate(tops, axis=1), jnp.concatenate(bottoms, axis=1)], axis=0)
            )
            result = dot(
                jnp.concatenate([coarse[last], coarse[last], coarse[last + 1]], axis=1),
                jnp.concatenate([upper, lower, upper], axis=0),
            )
            slot = step * group + member
            flat[line(0, 0, slot), :] = result[:EDEV, :128]
            flat[line(0, 1, slot), :] = result[EDEV:, :128]
            flat[line(1, 0, slot), :] = -result[:EDEV, 128:]
            flat[line(1, 1, slot), :] = result[EDEV:, 128:]
        return carry

    lax.fori_loop(0, MINE // group, product, 0)
    send[...] = flat[...].reshape(OWNERS, ROWS, 128).astype(BF16)


def one_hot(slot):
    order = lax.broadcasted_iota(jnp.int32, (SLOTS, SLOTS), 0)
    return jnp.where(order == slot, 1.0, 0.0).astype(BF16)


def kernel(
    less_hbm, greater_hbm, slot_hbm, coarse_hbm, fine_hbm,
    recv_two,
    less, greater, slot, wide, coarse, fine,
    hot, send_one, recv_one, send_two, flat, y_own, y_far,
    sent, came, kept, fetched,
):
    e = lax.axis_index("energy")
    p = lax.axis_index("pair")
    core, z, x = lax.rem(e, 2), lax.rem(lax.div(e, 2), 16), lax.div(p, 2)
    y = lax.div(e, 32) * 2 + lax.rem(p, 2)
    me = e * 2 + lax.rem(p, 2)

    sources = (slot_hbm, less_hbm, greater_hbm, coarse_hbm, fine_hbm)
    places = (slot, less, greater, wide, fine)
    fetches = [pltpu.make_async_copy(a, b, fetched.at[i]) for i, (a, b) in enumerate(zip(sources, places))]
    for fetch in fetches:
        fetch.start()

    columns = []
    for dy in range(4):
        to_y = lax.rem(y + dy, 4)
        columns.append((lax.div(to_y, 2) * 32, lax.rem(to_y, 2)))

    def every_peer(act):
        for to_core in (1, 0):

            def along_z(t, carry):
                dz = 8 + (1 - 2 * lax.rem(t, 2)) * lax.div(t + 1, 2)
                low = lax.rem(z + dz, 16) * 2 + to_core
                for dy, (high, side) in enumerate(columns):
                    run = functools.partial(act, high + low, x * 2 + side, (high + low) * 2 + side)
                    if dy == 0:
                        pl.when(jnp.logical_or(t < 15, core != to_core))(run)
                    else:
                        run()
                return carry

            lax.fori_loop(0, 16, along_z, 0)

    barrier = pltpu.get_barrier_semaphore()

    def greet(to_e, to_p, to):
        pl.semaphore_signal(barrier, inc=1, device_id=(to_e, to_p), device_id_type=MESH)

    every_peer(greet)

    fetches[0].wait()
    hot[...] = one_hot(slot[...])
    fetches[1].wait()
    fetches[2].wait()
    halves = []
    for part in range(2):
        value = jnp.concatenate([less[part], greater[part]], axis=0)
        halves.append(dot(hot[...], value, ((1,), (1,))).reshape(OWNERS, MINE, 128))
    send_one[...] = jnp.concatenate(halves, axis=1).astype(BF16)

    pl.semaphore_wait(barrier, OWNERS - 1)

    def exchange(source, target, at, meanwhile=None):
        def start(to_e, to_p, to):
            pltpu.make_async_remote_copy(
                src_ref=source.at[to],
                dst_ref=target.at[me],
                send_sem=sent.at[at],
                recv_sem=came.at[at],
                device_id=(to_e, to_p),
                device_id_type=MESH,
            ).start()

        every_peer(start)
        stay = pltpu.make_async_copy(source.at[me], target.at[me], kept)
        stay.start()
        stay.wait()
        if meanwhile is not None:
            meanwhile()
        others = pl.ds(0, OWNERS - 1)
        pltpu.make_async_copy(target.at[others], target.at[others], came.at[at]).wait()

    def drain(source, at):
        others = pl.ds(0, OWNERS - 1)
        pltpu.make_async_copy(source.at[others], source.at[others], sent.at[at]).wait()

    def narrow():
        fetches[3].wait()
        fetches[4].wait()
        coarse[...] = wide[...].astype(BF16)

    exchange(send_one, recv_one, 0, narrow)
    correlate(recv_one, send_two, coarse, fine, flat, y_own, y_far)
    exchange(send_two, recv_two, 1)

    drain(send_one, 0)
    drain(send_two, 1)


def reorder(back_hbm, slot_hbm, out_less, out_greater, back, slot, fetched):
    fetches = [
        pltpu.make_async_copy(slot_hbm, slot, fetched.at[0]),
        pltpu.make_async_copy(back_hbm, back, fetched.at[1]),
    ]
    for fetch in fetches:
        fetch.start()
    fetches[0].wait()
    hot = one_hot(slot[...])
    fetches[1].wait()
    value = back[...].astype(F32)
    for part in range(2):
        ordered = value[:, part * MINE : (part + 1) * MINE].reshape(SLOTS, 128).astype(BF16)
        result = dot(ordered, hot, ((0,), (0,))).astype(BF16)
        out_less[part] = result[:N0]
        out_greater[part] = result[N0:]


def per_device(g_less, g_greater, pair_slot):
    coarse, fine = tables()
    vmem, hbm = pl.BlockSpec(memory_space=pltpu.VMEM), pl.BlockSpec(memory_space=pltpu.HBM)
    grant = 60 * 1024 * 1024
    packets = pltpu.VMEM((OWNERS, ROWS, 128), BF16)
    back = pl.pallas_call(
        kernel,
        out_shape=jax.ShapeDtypeStruct((OWNERS, ROWS, 128), BF16),
        in_specs=[hbm] * 5,
        out_specs=hbm,
        scratch_shapes=[
            pltpu.VMEM((2, N0, SLOTS), BF16),
            pltpu.VMEM((2, N0, SLOTS), BF16),
            pltpu.VMEM((1, SLOTS), jnp.int32),
            pltpu.VMEM(coarse.shape, F32),
            pltpu.VMEM(coarse.shape, BF16),
            pltpu.VMEM(fine.shape, F32),
            pltpu.VMEM((SLOTS, SLOTS), BF16),
            packets,
            packets,
            packets,
            pltpu.VMEM((OWNERS * ROWS, 128), F32),
            pltpu.VMEM((MINE * K0, 512), BF16),
            pltpu.VMEM((MINE * K0, 512), BF16),
            pltpu.SemaphoreType.DMA((2,)),
            pltpu.SemaphoreType.DMA((2,)),
            pltpu.SemaphoreType.DMA,
            pltpu.SemaphoreType.DMA((5,)),
        ],
        compiler_params=pltpu.CompilerParams(collective_id=0, has_side_effects=True, vmem_limit_bytes=grant),
        cost_estimate=pl.CostEstimate(flops=4 * 10**9, bytes_accessed=4 * 10**6, transcendentals=0),
    )(g_less, g_greater, pair_slot, jnp.asarray(coarse), jnp.asarray(fine))
    shape = jax.ShapeDtypeStruct((2, N0, SLOTS), BF16)
    return pl.pallas_call(
        reorder,
        out_shape=(shape, shape),
        in_specs=[hbm, hbm],
        out_specs=(vmem, vmem),
        scratch_shapes=[packets, pltpu.VMEM((1, SLOTS), jnp.int32), pltpu.SemaphoreType.DMA((2,))],
        compiler_params=pltpu.CompilerParams(vmem_limit_bytes=grant),
        cost_estimate=pl.CostEstimate(flops=10**9, bytes_accessed=10**6, transcendentals=0),
    )(back, pair_slot)


def solution(mesh):
    placed = (P(None, "energy", "pair"), P(None, "energy", "pair"), P("pair", None))
    return jax.shard_map(
        per_device,
        mesh=mesh,
        in_specs=placed,
        out_specs=(P(None, "energy", "pair"), P(None, "energy", "pair")),
        check_vma=False,
    )
```

```python
import functools
import math

import jax
import jax.numpy as jnp
import ml_dtypes
import numpy as np
from jax import lax
from jax.experimental import pallas as pl
from jax.experimental.pallas import tpu as pltpu
from jax.sharding import PartitionSpec as P

NE = 4096
N0 = 64
EDEV = 64
OWNERS = 2 * EDEV
SLOTS = 1024
MINE = SLOTS // OWNERS
ROWS = 2 * MINE
K0 = 128
K1 = 64
LENGTH = 2 * NE
F32 = jnp.float32
BF16 = jnp.bfloat16
MESH = pl.DeviceIdType.MESH


def upper_lower(table):
    upper = table.astype(ml_dtypes.bfloat16)
    lower = (table - upper.astype(np.float64)).astype(ml_dtypes.bfloat16)
    return upper, lower


def cos_sin(rows, cols, period):
    angle = (np.arange(rows)[:, None] * np.arange(cols)[None, :] % period) * (2.0 * math.pi / period)
    return np.cos(angle), np.sin(angle)


def tables():
    lanes = lambda *parts: np.concatenate(parts, axis=1)
    both = lambda table: np.concatenate(upper_lower(table))
    straight = lambda part: np.kron(np.eye(2), part)
    crossed = lambda part: np.kron(np.eye(2)[::-1], part)
    c, s = cos_sin(K0, EDEV, K0)
    first = [lanes(*upper_lower(lanes(c, s))), lanes(*upper_lower(lanes(c, -s)))]
    c, s = cos_sin(N0, K1, K1)
    own = both(np.block([[straight(c), -straight(s)], [straight(s), straight(c)]]))
    far = both(np.block([[crossed(c), crossed(s)], [-crossed(s), crossed(c)]]))
    ahead = both(np.block([[straight(c), straight(s)], [-straight(s), straight(c)]]))
    behind = both(np.block([[crossed(c), crossed(s)], [crossed(s), -crossed(c)]]))
    c, s = cos_sin(EDEV, K0, K0)
    last = both(np.block([[c, -s], [s, c]]))
    coarse = np.concatenate(first + [own, far, ahead, behind, last])
    c, s = cos_sin(K0, N0, LENGTH)
    scale = 1.0 / (math.sqrt(NE) * LENGTH)
    fine = np.stack([lanes(c, c), lanes(s, s), lanes(s, s) * scale, -lanes(c, c) * scale])
    return coarse.reshape(-1, 128, 256).astype(np.float32), fine.astype(np.float32)


def dot(left, right, dims=((1,), (0,))):
    return lax.dot_general(left, right, (dims, ((), ())), preferred_element_type=F32)


def split(value):
    upper = value.astype(BF16)
    return upper, (value - upper.astype(F32)).astype(BF16)


def correlate(recv, send, coarse, fine, flat, y_own, y_far):
    first, own, far, ahead, behind, last = 0, 2, 6, 10, 14, 18
    flat[...] = recv[...].astype(F32).reshape(OWNERS * ROWS, 128)

    def line(side, part, slot):
        return pl.ds(side * ROWS + part * MINE + slot, EDEV, stride=2 * ROWS)

    def spectrum(side, slot, into):
        re, im = flat[line(side, 0, slot), :], flat[line(side, 1, slot), :]
        top = jnp.concatenate([re, im], axis=1).astype(BF16)
        bottom = jnp.concatenate([im, -re], axis=1).astype(BF16)
        step = dot(coarse[first + side], jnp.concatenate([top, bottom, top, bottom], axis=0))
        re, im = step[:, :128], step[:, 128:]
        c, s = fine[0], fine[1]
        if side == 0:
            re, im = re * c + im * s, im * c - re * s
        else:
            re, im = re * c - im * s, im * c + re * s
        into[pl.ds(slot * K0, K0), :] = jnp.concatenate(split(jnp.concatenate([re, im], axis=1)), axis=1)

    def forward(step, carry):
        for member in range(2):
            spectrum(0, step * 2 + member, y_own)
            spectrum(1, step * 2 + member, y_far)
        return carry

    lax.fori_loop(0, MINE // 2, forward, 0)

    def triple(value, table):
        upper = coarse[table : table + 2].reshape(256, 256)
        lower = coarse[table + 2 : table + 4].reshape(256, 256)
        return dot(
            jnp.concatenate([value, value[:, :256]], axis=1), jnp.concatenate([upper, upper, lower], axis=0)
        )

    group = 4

    def product(step, carry):
        rows = pl.ds(step * (group * K0), group * K0)
        left, right = triple(y_own[rows, :], own), triple(y_far[rows, :], far)
        a, b, c, d = left[:, :128], left[:, 128:], right[:, :128], right[:, 128:]
        spec = jnp.concatenate(split(jnp.concatenate([a * c - b * d, a * d + b * c], axis=1)), axis=1)
        lags = (triple(spec, ahead), triple(spec, behind))
        for member in range(group):
            tops, bottoms = [], []
            for part in lags:
                re, im = part[member * K0 : (member + 1) * K0, :128], part[member * K0 : (member + 1) * K0, 128:]
                tops.append(re * fine[2] - im * fine[3])
                bottoms.append(re * fine[3] + im * fine[2])
            upper, lower = split(
                jnp.concatenate([jnp.concatenate(tops, axis=1), jnp.concatenate(bottoms, axis=1)], axis=0)
            )
            result = dot(
                jnp.concatenate([coarse[last], coarse[last], coarse[last + 1]], axis=1),
                jnp.concatenate([upper, lower, upper], axis=0),
            )
            slot = step * group + member
            flat[line(0, 0, slot), :] = result[:EDEV, :128]
            flat[line(0, 1, slot), :] = result[EDEV:, :128]
            flat[line(1, 0, slot), :] = -result[:EDEV, 128:]
            flat[line(1, 1, slot), :] = result[EDEV:, 128:]
        return carry

    lax.fori_loop(0, MINE // group, product, 0)
    send[...] = flat[...].reshape(OWNERS, ROWS, 128).astype(BF16)


def one_hot(slot):
    order = lax.broadcasted_iota(jnp.int32, (SLOTS, SLOTS), 0)
    return jnp.where(order == slot, 1.0, 0.0).astype(BF16)


def kernel(
    less_hbm, greater_hbm, slot_hbm, coarse_hbm, fine_hbm,
    recv_two,
    less, greater, slot, wide, coarse, fine,
    hot, send_one, recv_one, send_two, flat, y_own, y_far,
    sent, came, kept, fetched,
):
    e = lax.axis_index("energy")
    p = lax.axis_index("pair")
    core, z, x = lax.rem(e, 2), lax.rem(lax.div(e, 2), 16), lax.div(p, 2)
    y = lax.div(e, 32) * 2 + lax.rem(p, 2)
    me = e * 2 + lax.rem(p, 2)

    sources = (slot_hbm, less_hbm, greater_hbm, coarse_hbm, fine_hbm)
    places = (slot, less, greater, wide, fine)
    fetches = [pltpu.make_async_copy(a, b, fetched.at[i]) for i, (a, b) in enumerate(zip(sources, places))]
    for fetch in fetches:
        fetch.start()

    columns = []
    for dy in range(4):
        to_y = lax.rem(y + dy, 4)
        columns.append((lax.div(to_y, 2) * 32, lax.rem(to_y, 2)))

    def every_peer(act):
        for to_core in (1, 0):

            def at(dz, columns):
                to_z = jnp.where(z + dz >= 16, z + dz - 16, z + dz)
                for high, side in columns:
                    to_e = high + to_z * 2 + to_core
                    act(to_e, x * 2 + side, to_e * 2 + side)

            def both_ways(near, carry):
                at(7 - near, columns)
                at(9 + near, columns)
                return carry

            at(8, columns)
            lax.fori_loop(0, 7, both_ways, 0)
            at(0, columns[1:])
            pl.when(core != to_core)(functools.partial(at, 0, columns[:1]))

    barrier = pltpu.get_barrier_semaphore()

    def greet(to_e, to_p, to):
        pl.semaphore_signal(barrier, inc=1, device_id=(to_e, to_p), device_id_type=MESH)

    every_peer(greet)

    fetches[0].wait()
    hot[...] = one_hot(slot[...])
    fetches[1].wait()
    fetches[2].wait()
    halves = []
    for part in range(2):
        value = jnp.concatenate([less[part], greater[part]], axis=0)
        halves.append(dot(hot[...], value, ((1,), (1,))).reshape(OWNERS, MINE, 128))
    send_one[...] = jnp.concatenate(halves, axis=1).astype(BF16)

    pl.semaphore_wait(barrier, OWNERS - 1)

    def exchange(source, target, at, meanwhile=None):
        def start(to_e, to_p, to):
            pltpu.make_async_remote_copy(
                src_ref=source.at[to],
                dst_ref=target.at[me],
                send_sem=sent.at[at],
                recv_sem=came.at[at],
                device_id=(to_e, to_p),
                device_id_type=MESH,
            ).start()

        every_peer(start)
        stay = pltpu.make_async_copy(source.at[me], target.at[me], kept)
        stay.start()
        stay.wait()
        if meanwhile is not None:
            meanwhile()
        others = pl.ds(0, OWNERS - 1)
        pltpu.make_async_copy(target.at[others], target.at[others], came.at[at]).wait()

    def drain(source, at):
        others = pl.ds(0, OWNERS - 1)
        pltpu.make_async_copy(source.at[others], source.at[others], sent.at[at]).wait()

    def narrow():
        fetches[3].wait()
        fetches[4].wait()
        coarse[...] = wide[...].astype(BF16)

    exchange(send_one, recv_one, 0, narrow)
    correlate(recv_one, send_two, coarse, fine, flat, y_own, y_far)
    exchange(send_two, recv_two, 1)

    drain(send_one, 0)
    drain(send_two, 1)


def reorder(back_hbm, slot_hbm, out_less, out_greater, back, slot, fetched):
    fetches = [
        pltpu.make_async_copy(slot_hbm, slot, fetched.at[0]),
        pltpu.make_async_copy(back_hbm, back, fetched.at[1]),
    ]
    for fetch in fetches:
        fetch.start()
    fetches[0].wait()
    hot = one_hot(slot[...])
    fetches[1].wait()
    value = back[...].astype(F32)
    for part in range(2):
        ordered = value[:, part * MINE : (part + 1) * MINE].reshape(SLOTS, 128).astype(BF16)
        result = dot(ordered, hot, ((0,), (0,))).astype(BF16)
        out_less[part] = result[:N0]
        out_greater[part] = result[N0:]


def per_device(g_less, g_greater, pair_slot):
    coarse, fine = tables()
    vmem, hbm = pl.BlockSpec(memory_space=pltpu.VMEM), pl.BlockSpec(memory_space=pltpu.HBM)
    grant = 60 * 1024 * 1024
    packets = pltpu.VMEM((OWNERS, ROWS, 128), BF16)
    back = pl.pallas_call(
        kernel,
        out_shape=jax.ShapeDtypeStruct((OWNERS, ROWS, 128), BF16),
        in_specs=[hbm] * 5,
        out_specs=hbm,
        scratch_shapes=[
            pltpu.VMEM((2, N0, SLOTS), BF16),
            pltpu.VMEM((2, N0, SLOTS), BF16),
            pltpu.VMEM((1, SLOTS), jnp.int32),
            pltpu.VMEM(coarse.shape, F32),
            pltpu.VMEM(coarse.shape, BF16),
            pltpu.VMEM(fine.shape, F32),
            pltpu.VMEM((SLOTS, SLOTS), BF16),
            packets,
            packets,
            packets,
            pltpu.VMEM((OWNERS * ROWS, 128), F32),
            pltpu.VMEM((MINE * K0, 512), BF16),
            pltpu.VMEM((MINE * K0, 512), BF16),
            pltpu.SemaphoreType.DMA((2,)),
            pltpu.SemaphoreType.DMA((2,)),
            pltpu.SemaphoreType.DMA,
            pltpu.SemaphoreType.DMA((5,)),
        ],
        compiler_params=pltpu.CompilerParams(collective_id=0, has_side_effects=True, vmem_limit_bytes=grant),
        cost_estimate=pl.CostEstimate(flops=4 * 10**9, bytes_accessed=4 * 10**6, transcendentals=0),
    )(g_less, g_greater, pair_slot, jnp.asarray(coarse), jnp.asarray(fine))
    shape = jax.ShapeDtypeStruct((2, N0, SLOTS), BF16)
    return pl.pallas_call(
        reorder,
        out_shape=(shape, shape),
        in_specs=[hbm, hbm],
        out_specs=(vmem, vmem),
        scratch_shapes=[packets, pltpu.VMEM((1, SLOTS), jnp.int32), pltpu.SemaphoreType.DMA((2,))],
        compiler_params=pltpu.CompilerParams(vmem_limit_bytes=grant),
        cost_estimate=pl.CostEstimate(flops=10**9, bytes_accessed=10**6, transcendentals=0),
    )(back, pair_slot)


def solution(mesh):
    placed = (P(None, "energy", "pair"), P(None, "energy", "pair"), P("pair", None))
    return jax.shard_map(
        per_device,
        mesh=mesh,
        in_specs=placed,
        out_specs=(P(None, "energy", "pair"), P(None, "energy", "pair")),
        check_vma=False,
    )
```

```python
import functools
import math

import jax
import jax.numpy as jnp
import ml_dtypes
import numpy as np
from jax import lax
from jax.experimental import pallas as pl
from jax.experimental.pallas import tpu as pltpu
from jax.sharding import PartitionSpec as P

NE = 4096
N0 = 64
EDEV = 64
OWNERS = 2 * EDEV
SLOTS = 1024
MINE = SLOTS // OWNERS
ROWS = 2 * MINE
K0 = 128
K1 = 64
LENGTH = 2 * NE
F32 = jnp.float32
BF16 = jnp.bfloat16
MESH = pl.DeviceIdType.MESH


def upper_lower(table):
    upper = table.astype(ml_dtypes.bfloat16)
    lower = (table - upper.astype(np.float64)).astype(ml_dtypes.bfloat16)
    return upper, lower


def cos_sin(rows, cols, period):
    angle = (np.arange(rows)[:, None] * np.arange(cols)[None, :] % period) * (2.0 * math.pi / period)
    return np.cos(angle), np.sin(angle)


def tables():
    lanes = lambda *parts: np.concatenate(parts, axis=1)
    both = lambda table: np.concatenate(upper_lower(table))
    straight = lambda part: np.kron(np.eye(2), part)
    crossed = lambda part: np.kron(np.eye(2)[::-1], part)
    c, s = cos_sin(K0, EDEV, K0)
    first = [lanes(*upper_lower(lanes(c, s))), lanes(*upper_lower(lanes(c, -s)))]
    c, s = cos_sin(N0, K1, K1)
    own = both(np.block([[straight(c), -straight(s)], [straight(s), straight(c)]]))
    far = both(np.block([[crossed(c), crossed(s)], [-crossed(s), crossed(c)]]))
    ahead = both(np.block([[straight(c), straight(s)], [-straight(s), straight(c)]]))
    behind = both(np.block([[crossed(c), crossed(s)], [crossed(s), -crossed(c)]]))
    c, s = cos_sin(EDEV, K0, K0)
    last = both(np.block([[c, -s], [s, c]]))
    coarse = np.concatenate(first + [own, far, ahead, behind, last])
    c, s = cos_sin(K0, N0, LENGTH)
    scale = 1.0 / (math.sqrt(NE) * LENGTH)
    fine = np.stack([lanes(c, c), lanes(s, s), lanes(s, s) * scale, -lanes(c, c) * scale])
    return coarse.reshape(-1, 128, 256).astype(np.float32), fine.astype(np.float32)


def dot(left, right, dims=((1,), (0,))):
    return lax.dot_general(left, right, (dims, ((), ())), preferred_element_type=F32)


def split(value):
    upper = value.astype(BF16)
    return upper, (value - upper.astype(F32)).astype(BF16)


def correlate(recv, send, coarse, fine, flat, y_own, y_far):
    first, own, far, ahead, behind, last = 0, 2, 6, 10, 14, 18
    flat[...] = recv[...].astype(F32).reshape(OWNERS * ROWS, 128)

    def line(side, part, slot):
        return pl.ds(side * ROWS + part * MINE + slot, EDEV, stride=2 * ROWS)

    def spectrum(side, slot, into):
        re, im = flat[line(side, 0, slot), :], flat[line(side, 1, slot), :]
        top = jnp.concatenate([re, im], axis=1).astype(BF16)
        bottom = jnp.concatenate([im, -re], axis=1).astype(BF16)
        step = dot(coarse[first + side], jnp.concatenate([top, bottom, top, bottom], axis=0))
        re, im = step[:, :128], step[:, 128:]
        c, s = fine[0], fine[1]
        if side == 0:
            re, im = re * c + im * s, im * c - re * s
        else:
            re, im = re * c - im * s, im * c + re * s
        into[pl.ds(slot * K0, K0), :] = jnp.concatenate(split(jnp.concatenate([re, im], axis=1)), axis=1)

    def forward(step, carry):
        for member in range(2):
            spectrum(0, step * 2 + member, y_own)
            spectrum(1, step * 2 + member, y_far)
        return carry

    lax.fori_loop(0, MINE // 2, forward, 0)

    def triple(value, table):
        upper = coarse[table : table + 2].reshape(256, 256)
        lower = coarse[table + 2 : table + 4].reshape(256, 256)
        return dot(
            jnp.concatenate([value, value[:, :256]], axis=1), jnp.concatenate([upper, upper, lower], axis=0)
        )

    group = 4

    def product(step, carry):
        rows = pl.ds(step * (group * K0), group * K0)
        left, right = triple(y_own[rows, :], own), triple(y_far[rows, :], far)
        a, b, c, d = left[:, :128], left[:, 128:], right[:, :128], right[:, 128:]
        spec = jnp.concatenate(split(jnp.concatenate([a * c - b * d, a * d + b * c], axis=1)), axis=1)
        lags = (triple(spec, ahead), triple(spec, behind))
        for member in range(group):
            tops, bottoms = [], []
            for part in lags:
                re, im = part[member * K0 : (member + 1) * K0, :128], part[member * K0 : (member + 1) * K0, 128:]
                tops.append(re * fine[2] - im * fine[3])
                bottoms.append(re * fine[3] + im * fine[2])
            upper, lower = split(
                jnp.concatenate([jnp.concatenate(tops, axis=1), jnp.concatenate(bottoms, axis=1)], axis=0)
            )
            result = dot(
                jnp.concatenate([coarse[last], coarse[last], coarse[last + 1]], axis=1),
                jnp.concatenate([upper, lower, upper], axis=0),
            )
            slot = step * group + member
            flat[line(0, 0, slot), :] = result[:EDEV, :128]
            flat[line(0, 1, slot), :] = result[EDEV:, :128]
            flat[line(1, 0, slot), :] = -result[:EDEV, 128:]
            flat[line(1, 1, slot), :] = result[EDEV:, 128:]
        return carry

    lax.fori_loop(0, MINE // group, product, 0)
    send[...] = flat[...].reshape(OWNERS, ROWS, 128).astype(BF16)


def one_hot(slot, begin, rows):
    order = lax.broadcasted_iota(jnp.int32, (rows, SLOTS), 0) + begin
    return jnp.where(order == slot, 1.0, 0.0).astype(BF16)


def kernel(
    less_hbm, greater_hbm, slot_hbm, coarse_hbm, fine_hbm,
    recv_two,
    less, greater, slot, wide, coarse, fine,
    hot, send_one, recv_one, send_two, flat, y_own, y_far,
    sent, came, kept, fetched,
):
    e = lax.axis_index("energy")
    p = lax.axis_index("pair")
    core, z, x = lax.rem(e, 2), lax.rem(lax.div(e, 2), 16), lax.div(p, 2)
    side = lax.rem(p, 2)
    y = lax.div(e, 32) * 2 + side
    place = e * 2 + side
    owner = (1 - core) * EDEV + lax.div(e, 2) * 2 + side

    sources = (slot_hbm, less_hbm, greater_hbm, coarse_hbm, fine_hbm)
    places = (slot, less, greater, wide, fine)
    fetches = [pltpu.make_async_copy(a, b, fetched.at[i]) for i, (a, b) in enumerate(zip(sources, places))]
    for fetch in fetches:
        fetch.start()

    columns = []
    for dy in range(4):
        to_y = lax.rem(y + dy, 4)
        columns.append((lax.div(to_y, 2) * 16, lax.rem(to_y, 2)))

    def at(dz, to_core, columns, act):
        to_z = jnp.where(z + dz >= 16, z + dz - 16, z + dz)
        for high, to_side in columns:
            chip = high + to_z
            act(
                chip * 2 + to_core,
                x * 2 + to_side,
                (chip * 2 + to_core) * 2 + to_side,
                (1 - to_core) * EDEV + chip * 2 + to_side,
            )

    def peers(cores, act):
        def both_ways(near, carry):
            for to_core in cores:
                at(7 - near, to_core, columns, act)
                at(9 + near, to_core, columns, act)
            return carry

        for to_core in cores:
            at(8, to_core, columns, act)
        lax.fori_loop(0, 7, both_ways, 0)
        for to_core in cores:
            at(0, to_core, columns[1:], act)
            pl.when(core != to_core)(functools.partial(at, 0, to_core, columns[:1], act))

    def some_peers(to_core, odd, act):
        even = 1 - lax.rem(odd + z, 2)

        def both_ways(near, carry):
            at(7 + even - 2 * near, to_core, columns, act)
            at(9 + even + 2 * near, to_core, columns, act)
            return carry

        lax.fori_loop(0, 3, both_ways, 0)
        at(1 + even, to_core, columns, act)
        at(15 + even, to_core, columns[1:], act)
        pl.when(jnp.logical_or(even == 0, core != to_core))(
            functools.partial(at, 15 + even, to_core, columns[:1], act)
        )

    barrier = pltpu.get_barrier_semaphore()

    def greet(to_e, to_p, to_place, to_owner):
        pl.semaphore_signal(barrier, inc=1, device_id=(to_e, to_p), device_id_type=MESH)

    peers((1, 0), greet)
    fetches[0].wait()
    hot[...] = one_hot(slot[...], 0, SLOTS)

    def remote(src, dst, turn, to_e, to_p):
        pltpu.make_async_remote_copy(
            src_ref=src,
            dst_ref=dst,
            send_sem=sent.at[turn],
            recv_sem=came.at[turn],
            device_id=(to_e, to_p),
            device_id_type=MESH,
        ).start()

    def out(to_e, to_p, to_place, to_owner):
        remote(send_one.at[to_owner], recv_one.at[place], 0, to_e, to_p)

    def back(to_e, to_p, to_place, to_owner):
        remote(send_two.at[to_place], recv_two.at[owner], 1, to_e, to_p)

    others = pl.ds(0, OWNERS - 1)

    def arrive(src, dst, target, turn):
        stay = pltpu.make_async_copy(src, dst, kept)
        stay.start()
        stay.wait()
        pltpu.make_async_copy(target.at[others], target.at[others], came.at[turn]).wait()

    fetches[1].wait()
    fetches[2].wait()
    value = jnp.concatenate([less[0], greater[0], less[1], greater[1]], axis=0)
    for to_core in (1, 0):
        half = SLOTS // 2
        ordered = dot(hot[(1 - to_core) * half : (2 - to_core) * half, :], value, ((1,), (1,)))
        parts = [ordered[:, part * 128 : (part + 1) * 128].reshape(EDEV, MINE, 128) for part in range(2)]
        send_one[(1 - to_core) * EDEV : (2 - to_core) * EDEV] = jnp.concatenate(parts, axis=1).astype(BF16)
        if to_core == 1:
            pl.semaphore_wait(barrier, OWNERS - 1)
        for odd in (1, 0):
            some_peers(to_core, odd, out)

    fetches[3].wait()
    fetches[4].wait()
    coarse[...] = wide[...].astype(BF16)
    arrive(send_one.at[owner], recv_one.at[place], recv_one, 0)
    correlate(recv_one, send_two, coarse, fine, flat, y_own, y_far)
    for to_core in (1, 0):
        peers((to_core,), back)
    arrive(send_two.at[place], recv_two.at[owner], recv_two, 1)

    for turn, source in enumerate((send_one, send_two)):
        pltpu.make_async_copy(source.at[others], source.at[others], sent.at[turn]).wait()


def reorder(back_hbm, slot_hbm, less_hbm, greater_hbm, back, slot, less, greater, fetched, stored):
    fetches = [
        pltpu.make_async_copy(slot_hbm, slot, fetched.at[0]),
        pltpu.make_async_copy(back_hbm, back, fetched.at[1]),
    ]
    for fetch in fetches:
        fetch.start()
    fetches[0].wait()
    hot = one_hot(slot[...], 0, SLOTS)
    fetches[1].wait()
    value = back[...].astype(F32)
    ordered = jnp.concatenate(
        [value[:, part * MINE : (part + 1) * MINE].reshape(SLOTS, 128) for part in range(2)], axis=1
    )
    result = dot(ordered.astype(BF16), hot, ((0,), (0,))).astype(BF16)
    stores = []
    for part in range(2):
        for array, (kept, result_hbm) in enumerate(((less, less_hbm), (greater, greater_hbm))):
            kept[part] = result[(part * 2 + array) * N0 : (part * 2 + array + 1) * N0]
            stores.append(pltpu.make_async_copy(kept.at[part], result_hbm.at[part], stored.at[part, array]))
            stores[-1].start()
    for store in stores:
        store.wait()


def per_device(g_less, g_greater, pair_slot):
    coarse, fine = tables()
    hbm = pl.BlockSpec(memory_space=pltpu.HBM)
    grant = 60 * 1024 * 1024
    packets = pltpu.VMEM((OWNERS, ROWS, 128), BF16)
    back = pl.pallas_call(
        kernel,
        out_shape=jax.ShapeDtypeStruct((OWNERS, ROWS, 128), BF16),
        in_specs=[hbm] * 5,
        out_specs=hbm,
        scratch_shapes=[
            pltpu.VMEM((2, N0, SLOTS), BF16),
            pltpu.VMEM((2, N0, SLOTS), BF16),
            pltpu.VMEM((1, SLOTS), jnp.int32),
            pltpu.VMEM(coarse.shape, F32),
            pltpu.VMEM(coarse.shape, BF16),
            pltpu.VMEM(fine.shape, F32),
            pltpu.VMEM((SLOTS, SLOTS), BF16),
            packets,
            packets,
            packets,
            pltpu.VMEM((OWNERS * ROWS, 128), F32),
            pltpu.VMEM((MINE * K0, 512), BF16),
            pltpu.VMEM((MINE * K0, 512), BF16),
            pltpu.SemaphoreType.DMA((2,)),
            pltpu.SemaphoreType.DMA((2,)),
            pltpu.SemaphoreType.DMA,
            pltpu.SemaphoreType.DMA((5,)),
        ],
        compiler_params=pltpu.CompilerParams(collective_id=0, has_side_effects=True, vmem_limit_bytes=grant),
        cost_estimate=pl.CostEstimate(flops=4 * 10**9, bytes_accessed=4 * 10**6, transcendentals=0),
    )(g_less, g_greater, pair_slot, jnp.asarray(coarse), jnp.asarray(fine))
    shape = jax.ShapeDtypeStruct((2, N0, SLOTS), BF16)
    return pl.pallas_call(
        reorder,
        out_shape=(shape, shape),
        in_specs=[hbm, hbm],
        out_specs=(hbm, hbm),
        scratch_shapes=[
            packets,
            pltpu.VMEM((1, SLOTS), jnp.int32),
            pltpu.VMEM(shape.shape, BF16),
            pltpu.VMEM(shape.shape, BF16),
            pltpu.SemaphoreType.DMA((2,)),
            pltpu.SemaphoreType.DMA((2, 2)),
        ],
        compiler_params=pltpu.CompilerParams(vmem_limit_bytes=grant),
        cost_estimate=pl.CostEstimate(flops=10**9, bytes_accessed=10**6, transcendentals=0),
    )(back, pair_slot)


def solution(mesh):
    placed = (P(None, "energy", "pair"), P(None, "energy", "pair"), P("pair", None))
    return jax.shard_map(
        per_device,
        mesh=mesh,
        in_specs=placed,
        out_specs=(P(None, "energy", "pair"), P(None, "energy", "pair")),
        check_vma=False,
    )
```

```python
import functools
import math

import jax
import jax.numpy as jnp
import ml_dtypes
import numpy as np
from jax import lax
from jax.experimental import pallas as pl
from jax.experimental.pallas import tpu as pltpu
from jax.sharding import PartitionSpec as P

NE = 4096
N0 = 64
EDEV = 64
OWNERS = 2 * EDEV
SLOTS = 1024
MINE = SLOTS // OWNERS
ROWS = 2 * MINE
K0 = 128
K1 = 64
LENGTH = 2 * NE
F32 = jnp.float32
BF16 = jnp.bfloat16
MESH = pl.DeviceIdType.MESH


def upper_lower(table):
    upper = table.astype(ml_dtypes.bfloat16)
    lower = (table - upper.astype(np.float64)).astype(ml_dtypes.bfloat16)
    return upper, lower


def cos_sin(rows, cols, period):
    angle = (np.arange(rows)[:, None] * np.arange(cols)[None, :] % period) * (2.0 * math.pi / period)
    return np.cos(angle), np.sin(angle)


def tables():
    lanes = lambda *parts: np.concatenate(parts, axis=1)
    both = lambda table: np.concatenate(upper_lower(table))
    straight = lambda part: np.kron(np.eye(2), part)
    crossed = lambda part: np.kron(np.eye(2)[::-1], part)
    c, s = cos_sin(K0, EDEV, K0)
    first = [lanes(*upper_lower(lanes(c, s))), lanes(*upper_lower(lanes(c, -s)))]
    c, s = cos_sin(N0, K1, K1)
    own = both(np.block([[straight(c), -straight(s)], [straight(s), straight(c)]]))
    far = both(np.block([[crossed(c), crossed(s)], [-crossed(s), crossed(c)]]))
    ahead = both(np.block([[straight(c), straight(s)], [-straight(s), straight(c)]]))
    behind = both(np.block([[crossed(c), crossed(s)], [crossed(s), -crossed(c)]]))
    c, s = cos_sin(EDEV, K0, K0)
    last = both(np.block([[c, -s], [s, c]]))
    coarse = np.concatenate(first + [own, far, ahead, behind, last])
    c, s = cos_sin(K0, N0, LENGTH)
    scale = 1.0 / (math.sqrt(NE) * LENGTH)
    fine = np.stack([lanes(c, c), lanes(s, s), lanes(s, s) * scale, -lanes(c, c) * scale])
    return coarse.reshape(-1, 128, 256).astype(np.float32), fine.astype(np.float32)


def dot(left, right, dims=((1,), (0,))):
    return lax.dot_general(left, right, (dims, ((), ())), preferred_element_type=F32)


def split(value):
    upper = value.astype(BF16)
    return upper, (value - upper.astype(F32)).astype(BF16)


def correlate(recv, send, coarse, fine, flat, y_own, y_far):
    first, own, far, ahead, behind, last = 0, 2, 6, 10, 14, 18
    flat[...] = recv[...].astype(F32).reshape(OWNERS * ROWS, 128)

    def line(side, part, slot):
        return pl.ds(side * ROWS + part * MINE + slot, EDEV, stride=2 * ROWS)

    def spectrum(side, slot, into):
        re, im = flat[line(side, 0, slot), :], flat[line(side, 1, slot), :]
        top = jnp.concatenate([re, im], axis=1).astype(BF16)
        bottom = jnp.concatenate([im, -re], axis=1).astype(BF16)
        step = dot(coarse[first + side], jnp.concatenate([top, bottom, top, bottom], axis=0))
        re, im = step[:, :128], step[:, 128:]
        c, s = fine[0], fine[1]
        if side == 0:
            re, im = re * c + im * s, im * c - re * s
        else:
            re, im = re * c - im * s, im * c + re * s
        into[pl.ds(slot * K0, K0), :] = jnp.concatenate(split(jnp.concatenate([re, im], axis=1)), axis=1)

    for slot in range(MINE):
        spectrum(0, slot, y_own)
        spectrum(1, slot, y_far)

    def triple(value, table):
        upper = coarse[table : table + 2].reshape(256, 256)
        lower = coarse[table + 2 : table + 4].reshape(256, 256)
        return dot(
            jnp.concatenate([value, value[:, :256]], axis=1), jnp.concatenate([upper, upper, lower], axis=0)
        )

    group = 4
    for step in range(MINE // group):
        rows = pl.ds(step * (group * K0), group * K0)
        left, right = triple(y_own[rows, :], own), triple(y_far[rows, :], far)
        a, b, c, d = left[:, :128], left[:, 128:], right[:, :128], right[:, 128:]
        spec = jnp.concatenate(split(jnp.concatenate([a * c - b * d, a * d + b * c], axis=1)), axis=1)
        lags = (triple(spec, ahead), triple(spec, behind))
        for member in range(group):
            tops, bottoms = [], []
            for part in lags:
                re, im = part[member * K0 : (member + 1) * K0, :128], part[member * K0 : (member + 1) * K0, 128:]
                tops.append(re * fine[2] - im * fine[3])
                bottoms.append(re * fine[3] + im * fine[2])
            upper, lower = split(
                jnp.concatenate([jnp.concatenate(tops, axis=1), jnp.concatenate(bottoms, axis=1)], axis=0)
            )
            both = dot(coarse[last : last + 2].reshape(256, 256), upper)
            result = both[:128] + both[128:] + dot(coarse[last], lower)
            slot = step * group + member
            flat[line(0, 0, slot), :] = result[:EDEV, :128]
            flat[line(0, 1, slot), :] = result[EDEV:, :128]
            flat[line(1, 0, slot), :] = -result[:EDEV, 128:]
            flat[line(1, 1, slot), :] = result[EDEV:, 128:]

    send[...] = flat[...].reshape(OWNERS, ROWS, 128).astype(BF16)


def one_hot(slot, begin, rows):
    order = lax.broadcasted_iota(jnp.int32, (rows, SLOTS), 0) + begin
    return jnp.where(order == slot, 1.0, 0.0).astype(BF16)


def kernel(
    less_hbm, greater_hbm, slot_hbm, coarse_hbm, fine_hbm,
    recv_two,
    less, greater, slot, wide, coarse, fine,
    hot, send_one, recv_one, send_two, flat, y_own, y_far,
    sent, came, kept, fetched,
):
    e = lax.axis_index("energy")
    p = lax.axis_index("pair")
    core, z, x = lax.rem(e, 2), lax.rem(lax.div(e, 2), 16), lax.div(p, 2)
    side = lax.rem(p, 2)
    y = lax.div(e, 32) * 2 + side
    place = e * 2 + side
    owner = (1 - core) * EDEV + lax.div(e, 2) * 2 + side

    sources = (slot_hbm, less_hbm, greater_hbm, coarse_hbm, fine_hbm)
    places = (slot, less, greater, wide, fine)
    fetches = [pltpu.make_async_copy(a, b, fetched.at[i]) for i, (a, b) in enumerate(zip(sources, places))]
    for fetch in fetches:
        fetch.start()

    columns = []
    for dy in range(4):
        to_y = lax.rem(y + dy, 4)
        columns.append((lax.div(to_y, 2) * 16, lax.rem(to_y, 2)))

    def at(dz, to_core, columns, act):
        to_z = jnp.where(z + dz >= 16, z + dz - 16, z + dz)
        for high, to_side in columns:
            chip = high + to_z
            act(
                chip * 2 + to_core,
                x * 2 + to_side,
                (chip * 2 + to_core) * 2 + to_side,
                (1 - to_core) * EDEV + chip * 2 + to_side,
            )

    def peers(cores, act):
        def both_ways(near, carry):
            for to_core in cores:
                at(7 - near, to_core, columns, act)
                at(9 + near, to_core, columns, act)
            return carry

        for to_core in cores:
            at(8, to_core, columns, act)
        lax.fori_loop(0, 7, both_ways, 0)
        for to_core in cores:
            at(0, to_core, columns[1:], act)
            pl.when(core != to_core)(functools.partial(at, 0, to_core, columns[:1], act))

    def some_peers(to_core, odd, act):
        even = 1 - lax.rem(odd + z, 2)

        def both_ways(near, carry):
            at(7 + even - 2 * near, to_core, columns, act)
            at(9 + even + 2 * near, to_core, columns, act)
            return carry

        lax.fori_loop(0, 3, both_ways, 0)
        at(1 + even, to_core, columns, act)
        at(15 + even, to_core, columns[1:], act)
        pl.when(jnp.logical_or(even == 0, core != to_core))(
            functools.partial(at, 15 + even, to_core, columns[:1], act)
        )

    barrier = pltpu.get_barrier_semaphore()

    def greet(to_e, to_p, to_place, to_owner):
        pl.semaphore_signal(barrier, inc=1, device_id=(to_e, to_p), device_id_type=MESH)

    peers((1, 0), greet)
    fetches[0].wait()
    hot[...] = one_hot(slot[...], 0, SLOTS)

    def remote(src, dst, turn, to_e, to_p):
        pltpu.make_async_remote_copy(
            src_ref=src,
            dst_ref=dst,
            send_sem=sent.at[turn],
            recv_sem=came.at[turn],
            device_id=(to_e, to_p),
            device_id_type=MESH,
        ).start()

    def out(to_e, to_p, to_place, to_owner):
        remote(send_one.at[to_owner], recv_one.at[place], 0, to_e, to_p)

    def back(to_e, to_p, to_place, to_owner):
        remote(send_two.at[to_place], recv_two.at[owner], 1, to_e, to_p)

    others = pl.ds(0, OWNERS - 1)

    def arrive(src, dst, target, turn):
        stay = pltpu.make_async_copy(src, dst, kept)
        stay.start()
        stay.wait()
        pltpu.make_async_copy(target.at[others], target.at[others], came.at[turn]).wait()

    fetches[1].wait()
    fetches[2].wait()
    value = jnp.concatenate([less[0], greater[0], less[1], greater[1]], axis=0)
    for to_core in (1, 0):
        half = SLOTS // 2
        ordered = dot(hot[(1 - to_core) * half : (2 - to_core) * half, :], value, ((1,), (1,)))
        parts = [ordered[:, part * 128 : (part + 1) * 128].reshape(EDEV, MINE, 128) for part in range(2)]
        send_one[(1 - to_core) * EDEV : (2 - to_core) * EDEV] = jnp.concatenate(parts, axis=1).astype(BF16)
        if to_core == 1:
            pl.semaphore_wait(barrier, OWNERS - 1)
        for odd in (1, 0):
            some_peers(to_core, odd, out)

    fetches[3].wait()
    fetches[4].wait()
    coarse[...] = wide[...].astype(BF16)
    arrive(send_one.at[owner], recv_one.at[place], recv_one, 0)
    correlate(recv_one, send_two, coarse, fine, flat, y_own, y_far)
    for to_core in (1, 0):
        peers((to_core,), back)
    arrive(send_two.at[place], recv_two.at[owner], recv_two, 1)

    for turn, source in enumerate((send_one, send_two)):
        pltpu.make_async_copy(source.at[others], source.at[others], sent.at[turn]).wait()


def reorder(back_hbm, slot_hbm, less_hbm, greater_hbm, back, slot, less, greater, fetched, stored):
    fetches = [
        pltpu.make_async_copy(slot_hbm, slot, fetched.at[0]),
        pltpu.make_async_copy(back_hbm, back, fetched.at[1]),
    ]
    for fetch in fetches:
        fetch.start()
    fetches[0].wait()
    hot = one_hot(slot[...], 0, SLOTS)
    fetches[1].wait()
    value = back[...].astype(F32)
    ordered = jnp.concatenate(
        [value[:, part * MINE : (part + 1) * MINE].reshape(SLOTS, 128) for part in range(2)], axis=1
    )
    result = dot(ordered.astype(BF16), hot, ((0,), (0,))).astype(BF16)
    stores = []
    for part in range(2):
        for array, (kept, result_hbm) in enumerate(((less, less_hbm), (greater, greater_hbm))):
            kept[part] = result[(part * 2 + array) * N0 : (part * 2 + array + 1) * N0]
            stores.append(pltpu.make_async_copy(kept.at[part], result_hbm.at[part], stored.at[part, array]))
            stores[-1].start()
    for store in stores:
        store.wait()


def per_device(g_less, g_greater, pair_slot):
    coarse, fine = tables()
    hbm = pl.BlockSpec(memory_space=pltpu.HBM)
    grant = 60 * 1024 * 1024
    packets = pltpu.VMEM((OWNERS, ROWS, 128), BF16)
    back = pl.pallas_call(
        kernel,
        out_shape=jax.ShapeDtypeStruct((OWNERS, ROWS, 128), BF16),
        in_specs=[hbm] * 5,
        out_specs=hbm,
        scratch_shapes=[
            pltpu.VMEM((2, N0, SLOTS), BF16),
            pltpu.VMEM((2, N0, SLOTS), BF16),
            pltpu.VMEM((1, SLOTS), jnp.int32),
            pltpu.VMEM(coarse.shape, F32),
            pltpu.VMEM(coarse.shape, BF16),
            pltpu.VMEM(fine.shape, F32),
            pltpu.VMEM((SLOTS, SLOTS), BF16),
            packets,
            packets,
            packets,
            pltpu.VMEM((OWNERS * ROWS, 128), F32),
            pltpu.VMEM((MINE * K0, 512), BF16),
            pltpu.VMEM((MINE * K0, 512), BF16),
            pltpu.SemaphoreType.DMA((2,)),
            pltpu.SemaphoreType.DMA((2,)),
            pltpu.SemaphoreType.DMA,
            pltpu.SemaphoreType.DMA((5,)),
        ],
        compiler_params=pltpu.CompilerParams(collective_id=0, has_side_effects=True, vmem_limit_bytes=grant),
        cost_estimate=pl.CostEstimate(flops=4 * 10**9, bytes_accessed=4 * 10**6, transcendentals=0),
    )(g_less, g_greater, pair_slot, jnp.asarray(coarse), jnp.asarray(fine))
    shape = jax.ShapeDtypeStruct((2, N0, SLOTS), BF16)
    return pl.pallas_call(
        reorder,
        out_shape=(shape, shape),
        in_specs=[hbm, hbm],
        out_specs=(hbm, hbm),
        scratch_shapes=[
            packets,
            pltpu.VMEM((1, SLOTS), jnp.int32),
            pltpu.VMEM(shape.shape, BF16),
            pltpu.VMEM(shape.shape, BF16),
            pltpu.SemaphoreType.DMA((2,)),
            pltpu.SemaphoreType.DMA((2, 2)),
        ],
        compiler_params=pltpu.CompilerParams(vmem_limit_bytes=grant),
        cost_estimate=pl.CostEstimate(flops=10**9, bytes_accessed=10**6, transcendentals=0),
    )(back, pair_slot)


def solution(mesh):
    placed = (P(None, "energy", "pair"), P(None, "energy", "pair"), P("pair", None))
    return jax.shard_map(
        per_device,
        mesh=mesh,
        in_specs=placed,
        out_specs=(P(None, "energy", "pair"), P(None, "energy", "pair")),
        check_vma=False,
    )
```

```python
import functools
import math

import jax
import jax.numpy as jnp
import ml_dtypes
import numpy as np
from jax import lax
from jax.experimental import pallas as pl
from jax.experimental.pallas import tpu as pltpu
from jax.sharding import PartitionSpec as P

NE = 4096
N0 = 64
EDEV = 64
OWNERS = 2 * EDEV
SLOTS = 1024
MINE = SLOTS // OWNERS
ROWS = 2 * MINE
EARLY_Z = 2
K0 = 128
K1 = 64
LENGTH = 2 * NE
F32 = jnp.float32
BF16 = jnp.bfloat16
MESH = pl.DeviceIdType.MESH


def upper_lower(table):
    upper = table.astype(ml_dtypes.bfloat16)
    lower = (table - upper.astype(np.float64)).astype(ml_dtypes.bfloat16)
    return upper, lower


def cos_sin(rows, cols, period):
    angle = (np.arange(rows)[:, None] * np.arange(cols)[None, :] % period) * (2.0 * math.pi / period)
    return np.cos(angle), np.sin(angle)


def tables():
    lanes = lambda *parts: np.concatenate(parts, axis=1)
    both = lambda table: np.concatenate(upper_lower(table))
    straight = lambda part: np.kron(np.eye(2), part)
    crossed = lambda part: np.kron(np.eye(2)[::-1], part)
    c, s = cos_sin(K0, EDEV, K0)
    first = [lanes(*upper_lower(lanes(c, s))), lanes(*upper_lower(lanes(c, -s)))]
    c, s = cos_sin(N0, K1, K1)
    own = both(np.block([[straight(c), -straight(s)], [straight(s), straight(c)]]))
    far = both(np.block([[crossed(c), crossed(s)], [-crossed(s), crossed(c)]]))
    ahead = both(np.block([[straight(c), straight(s)], [-straight(s), straight(c)]]))
    behind = both(np.block([[crossed(c), crossed(s)], [crossed(s), -crossed(c)]]))
    c, s = cos_sin(EDEV, K0, K0)
    last = both(np.block([[c, -s], [s, c]]))
    coarse = np.concatenate(first + [own, far, ahead, behind, last])
    c, s = cos_sin(K0, N0, LENGTH)
    scale = 1.0 / (math.sqrt(NE) * LENGTH)
    fine = np.stack([lanes(c, c), lanes(s, s), lanes(s, s) * scale, -lanes(c, c) * scale])
    return coarse.reshape(-1, 128, 256).astype(np.float32), fine.astype(np.float32)


def dot(left, right, dims=((1,), (0,))):
    return lax.dot_general(left, right, (dims, ((), ())), preferred_element_type=F32)


def split(value):
    upper = value.astype(BF16)
    return upper, (value - upper.astype(F32)).astype(BF16)


def correlate(recv, send, coarse, fine, flat, y_own, y_far):
    first, own, far, ahead, behind, last = 0, 2, 6, 10, 14, 18
    flat[...] = recv[...].astype(F32).reshape(OWNERS * ROWS, 128)

    def line(side, part, slot):
        return pl.ds(side * ROWS + part * MINE + slot, EDEV, stride=2 * ROWS)

    def spectrum(side, slot, into):
        re, im = flat[line(side, 0, slot), :], flat[line(side, 1, slot), :]
        top = jnp.concatenate([re, im], axis=1).astype(BF16)
        bottom = jnp.concatenate([im, -re], axis=1).astype(BF16)
        step = dot(coarse[first + side], jnp.concatenate([top, bottom, top, bottom], axis=0))
        re, im = step[:, :128], step[:, 128:]
        c, s = fine[0], fine[1]
        if side == 0:
            re, im = re * c + im * s, im * c - re * s
        else:
            re, im = re * c - im * s, im * c + re * s
        into[pl.ds(slot * K0, K0), :] = jnp.concatenate(split(jnp.concatenate([re, im], axis=1)), axis=1)

    for slot in range(MINE):
        spectrum(0, slot, y_own)
        spectrum(1, slot, y_far)

    def triple(value, table):
        upper = coarse[table : table + 2].reshape(256, 256)
        lower = coarse[table + 2 : table + 4].reshape(256, 256)
        return dot(
            jnp.concatenate([value, value[:, :256]], axis=1), jnp.concatenate([upper, upper, lower], axis=0)
        )

    group = 4
    for step in range(MINE // group):
        rows = pl.ds(step * (group * K0), group * K0)
        left, right = triple(y_own[rows, :], own), triple(y_far[rows, :], far)
        a, b, c, d = left[:, :128], left[:, 128:], right[:, :128], right[:, 128:]
        spec = jnp.concatenate(split(jnp.concatenate([a * c - b * d, a * d + b * c], axis=1)), axis=1)
        lags = (triple(spec, ahead), triple(spec, behind))
        for member in range(group):
            tops, bottoms = [], []
            for part in lags:
                re, im = part[member * K0 : (member + 1) * K0, :128], part[member * K0 : (member + 1) * K0, 128:]
                tops.append(re * fine[2] - im * fine[3])
                bottoms.append(re * fine[3] + im * fine[2])
            upper, lower = split(
                jnp.concatenate([jnp.concatenate(tops, axis=1), jnp.concatenate(bottoms, axis=1)], axis=0)
            )
            both = dot(coarse[last : last + 2].reshape(256, 256), upper)
            result = both[:128] + both[128:] + dot(coarse[last], lower)
            slot = step * group + member
            flat[line(0, 0, slot), :] = result[:EDEV, :128]
            flat[line(0, 1, slot), :] = result[EDEV:, :128]
            flat[line(1, 0, slot), :] = -result[:EDEV, 128:]
            flat[line(1, 1, slot), :] = result[EDEV:, 128:]

    send[...] = flat[...].reshape(OWNERS, ROWS, 128).astype(BF16)


def one_hot(slot, begin, rows):
    order = lax.broadcasted_iota(jnp.int32, (rows, SLOTS), 0) + begin
    return jnp.where(order == slot, 1.0, 0.0).astype(BF16)


def kernel(
    less_hbm, greater_hbm, slot_hbm, coarse_hbm, fine_hbm,
    recv_two,
    less, greater, slot, wide, coarse, fine,
    hot, send_one, recv_one, send_two, flat, y_own, y_far,
    sent, came, kept, fetched,
):
    e = lax.axis_index("energy")
    p = lax.axis_index("pair")
    core, z, x = lax.rem(e, 2), lax.rem(lax.div(e, 2), 16), lax.div(p, 2)
    side = lax.rem(p, 2)
    y = lax.div(e, 32) * 2 + side
    place = e * 2 + side
    owner = (1 - core) * EDEV + lax.div(e, 2) * 2 + side

    sources = (slot_hbm, less_hbm, greater_hbm, coarse_hbm, fine_hbm)
    places = (slot, less, greater, wide, fine)
    fetches = [pltpu.make_async_copy(a, b, fetched.at[i]) for i, (a, b) in enumerate(zip(sources, places))]
    for fetch in fetches:
        fetch.start()

    columns = []
    for dy in range(4):
        to_y = lax.rem(y + dy, 4)
        columns.append((lax.div(to_y, 2) * 16, lax.rem(to_y, 2)))

    def at_z(to_z, to_core, columns, act):
        for high, to_side in columns:
            chip = high + to_z
            act(
                chip * 2 + to_core,
                x * 2 + to_side,
                (chip * 2 + to_core) * 2 + to_side,
                (1 - to_core) * EDEV + chip * 2 + to_side,
            )

    def at(dz, to_core, columns, act):
        at_z(jnp.where(z + dz >= 16, z + dz - 16, z + dz), to_core, columns, act)

    def peers(cores, act, visit=at):
        def both_ways(near, carry):
            for to_core in cores:
                visit(7 - near, to_core, columns, act)
                visit(9 + near, to_core, columns, act)
            return carry

        for to_core in cores:
            visit(8, to_core, columns, act)
        lax.fori_loop(0, 7, both_ways, 0)
        for to_core in cores:
            visit(0, to_core, columns[1:], act)
            pl.when(core != to_core)(functools.partial(visit, 0, to_core, columns[:1], act))

    def some_peers(to_core, odd, act):
        even = 1 - lax.rem(odd + z, 2)

        def both_ways(near, carry):
            at(7 + even - 2 * near, to_core, columns, act)
            at(9 + even + 2 * near, to_core, columns, act)
            return carry

        lax.fori_loop(0, 3, both_ways, 0)
        at(1 + even, to_core, columns, act)
        at(15 + even, to_core, columns[1:], act)
        pl.when(jnp.logical_or(even == 0, core != to_core))(
            functools.partial(at, 15 + even, to_core, columns[:1], act)
        )

    barrier = pltpu.get_barrier_semaphore()

    def greet(to_e, to_p, to_place, to_owner):
        pl.semaphore_signal(barrier, inc=1, device_id=(to_e, to_p), device_id_type=MESH)

    peers((1, 0), greet)
    fetches[0].wait()
    hot[...] = one_hot(slot[...], 0, SLOTS)

    def remote(src, dst, turn, to_e, to_p):
        pltpu.make_async_remote_copy(
            src_ref=src,
            dst_ref=dst,
            send_sem=sent.at[turn],
            recv_sem=came.at[turn],
            device_id=(to_e, to_p),
            device_id_type=MESH,
        ).start()

    def out(to_e, to_p, to_place, to_owner):
        remote(send_one.at[to_owner], recv_one.at[place], 0, to_e, to_p)

    def back(to_e, to_p, to_place, to_owner):
        remote(send_two.at[to_place], recv_two.at[owner], 1, to_e, to_p)

    others = pl.ds(0, OWNERS - 1)

    def arrive(src, dst, target, turn):
        stay = pltpu.make_async_copy(src, dst, kept)
        stay.start()
        stay.wait()
        pltpu.make_async_copy(target.at[others], target.at[others], came.at[turn]).wait()

    fetches[1].wait()
    fetches[2].wait()
    value = jnp.concatenate([less[0], greater[0], less[1], greater[1]], axis=0)
    for to_core in (1, 0):
        half = SLOTS // 2
        ordered = dot(hot[(1 - to_core) * half : (2 - to_core) * half, :], value, ((1,), (1,)))
        parts = [ordered[:, part * 128 : (part + 1) * 128].reshape(EDEV, MINE, 128) for part in range(2)]
        send_one[(1 - to_core) * EDEV : (2 - to_core) * EDEV] = jnp.concatenate(parts, axis=1).astype(BF16)
        if to_core == 1:
            pl.semaphore_wait(barrier, OWNERS - 1)
        for odd in (1, 0):
            some_peers(to_core, odd, out)

    fetches[3].wait()
    fetches[4].wait()
    coarse[...] = wide[...].astype(BF16)
    arrive(send_one.at[owner], recv_one.at[place], recv_one, 0)
    correlate(recv_one, send_two, coarse, fine, flat, y_own, y_far)
    peers((1,), back)
    for to_z in range(EARLY_Z):
        at_z(to_z, 0, columns[1:], back)
        pl.when(jnp.logical_or(z != to_z, core != 0))(functools.partial(at_z, to_z, 0, columns[:1], back))

    def later(dz, to_core, columns, act):
        to_z = jnp.where(z + dz >= 16, z + dz - 16, z + dz)
        pl.when(to_z >= EARLY_Z)(functools.partial(at_z, to_z, to_core, columns, act))

    peers((0,), back, later)
    arrive(send_two.at[place], recv_two.at[owner], recv_two, 1)

    for turn, source in enumerate((send_one, send_two)):
        pltpu.make_async_copy(source.at[others], source.at[others], sent.at[turn]).wait()


def reorder(back_hbm, slot_hbm, less_hbm, greater_hbm, back, slot, less, greater, fetched, stored):
    fetches = [
        pltpu.make_async_copy(slot_hbm, slot, fetched.at[0]),
        pltpu.make_async_copy(back_hbm, back, fetched.at[1]),
    ]
    for fetch in fetches:
        fetch.start()
    fetches[0].wait()
    hot = one_hot(slot[...], 0, SLOTS)
    fetches[1].wait()
    value = back[...].astype(F32)
    ordered = jnp.concatenate(
        [value[:, part * MINE : (part + 1) * MINE].reshape(SLOTS, 128) for part in range(2)], axis=1
    )
    result = dot(ordered.astype(BF16), hot, ((0,), (0,))).astype(BF16)
    stores = []
    for part in range(2):
        for array, (kept, result_hbm) in enumerate(((less, less_hbm), (greater, greater_hbm))):
            kept[part] = result[(part * 2 + array) * N0 : (part * 2 + array + 1) * N0]
            stores.append(pltpu.make_async_copy(kept.at[part], result_hbm.at[part], stored.at[part, array]))
            stores[-1].start()
    for store in stores:
        store.wait()


def per_device(g_less, g_greater, pair_slot):
    coarse, fine = tables()
    hbm = pl.BlockSpec(memory_space=pltpu.HBM)
    grant = 60 * 1024 * 1024
    packets = pltpu.VMEM((OWNERS, ROWS, 128), BF16)
    back = pl.pallas_call(
        kernel,
        out_shape=jax.ShapeDtypeStruct((OWNERS, ROWS, 128), BF16),
        in_specs=[hbm] * 5,
        out_specs=hbm,
        scratch_shapes=[
            pltpu.VMEM((2, N0, SLOTS), BF16),
            pltpu.VMEM((2, N0, SLOTS), BF16),
            pltpu.VMEM((1, SLOTS), jnp.int32),
            pltpu.VMEM(coarse.shape, F32),
            pltpu.VMEM(coarse.shape, BF16),
            pltpu.VMEM(fine.shape, F32),
            pltpu.VMEM((SLOTS, SLOTS), BF16),
            packets,
            packets,
            packets,
            pltpu.VMEM((OWNERS * ROWS, 128), F32),
            pltpu.VMEM((MINE * K0, 512), BF16),
            pltpu.VMEM((MINE * K0, 512), BF16),
            pltpu.SemaphoreType.DMA((2,)),
            pltpu.SemaphoreType.DMA((2,)),
            pltpu.SemaphoreType.DMA,
            pltpu.SemaphoreType.DMA((5,)),
        ],
        compiler_params=pltpu.CompilerParams(collective_id=0, has_side_effects=True, vmem_limit_bytes=grant),
        cost_estimate=pl.CostEstimate(flops=4 * 10**9, bytes_accessed=4 * 10**6, transcendentals=0),
    )(g_less, g_greater, pair_slot, jnp.asarray(coarse), jnp.asarray(fine))
    shape = jax.ShapeDtypeStruct((2, N0, SLOTS), BF16)
    return pl.pallas_call(
        reorder,
        out_shape=(shape, shape),
        in_specs=[hbm, hbm],
        out_specs=(hbm, hbm),
        scratch_shapes=[
            packets,
            pltpu.VMEM((1, SLOTS), jnp.int32),
            pltpu.VMEM(shape.shape, BF16),
            pltpu.VMEM(shape.shape, BF16),
            pltpu.SemaphoreType.DMA((2,)),
            pltpu.SemaphoreType.DMA((2, 2)),
        ],
        compiler_params=pltpu.CompilerParams(vmem_limit_bytes=grant),
        cost_estimate=pl.CostEstimate(flops=10**9, bytes_accessed=10**6, transcendentals=0),
    )(back, pair_slot)


def solution(mesh):
    placed = (P(None, "energy", "pair"), P(None, "energy", "pair"), P("pair", None))
    return jax.shard_map(
        per_device,
        mesh=mesh,
        in_specs=placed,
        out_specs=(P(None, "energy", "pair"), P(None, "energy", "pair")),
        check_vma=False,
    )
```

```python
import functools
import math

import jax
import jax.numpy as jnp
import ml_dtypes
import numpy as np
from jax import lax
from jax.experimental import pallas as pl
from jax.experimental.pallas import tpu as pltpu
from jax.sharding import PartitionSpec as P

NE = 4096
N0 = 64
EDEV = 64
OWNERS = 2 * EDEV
SLOTS = 1024
MINE = SLOTS // OWNERS
ROWS = 2 * MINE
EARLY_Z = 2
K0 = 128
K1 = 64
LENGTH = 2 * NE
F32 = jnp.float32
BF16 = jnp.bfloat16
MESH = pl.DeviceIdType.MESH


def upper_lower(table):
    upper = table.astype(ml_dtypes.bfloat16)
    lower = (table - upper.astype(np.float64)).astype(ml_dtypes.bfloat16)
    return upper, lower


def cos_sin(rows, cols, period):
    angle = (np.arange(rows)[:, None] * np.arange(cols)[None, :] % period) * (2.0 * math.pi / period)
    return np.cos(angle), np.sin(angle)


def tables():
    lanes = lambda *parts: np.concatenate(parts, axis=1)
    both = lambda table: np.concatenate(upper_lower(table))
    straight = lambda part: np.kron(np.eye(2), part)
    crossed = lambda part: np.kron(np.eye(2)[::-1], part)
    c, s = cos_sin(K0, EDEV, K0)
    first = [lanes(*upper_lower(lanes(c, s))), lanes(*upper_lower(lanes(c, -s)))]
    c, s = cos_sin(N0, K1, K1)
    own = both(np.block([[straight(c), -straight(s)], [straight(s), straight(c)]]))
    far = both(np.block([[crossed(c), crossed(s)], [-crossed(s), crossed(c)]]))
    ahead = both(np.block([[straight(c), straight(s)], [-straight(s), straight(c)]]))
    behind = both(np.block([[crossed(c), crossed(s)], [crossed(s), -crossed(c)]]))
    c, s = cos_sin(EDEV, K0, K0)
    last = both(np.block([[c, -s], [s, c]]))
    coarse = np.concatenate(first + [own, far, ahead, behind, last])
    c, s = cos_sin(K0, N0, LENGTH)
    scale = 1.0 / (math.sqrt(NE) * LENGTH)
    fine = np.stack([lanes(c, c), lanes(s, s), lanes(s, s) * scale, -lanes(c, c) * scale])
    return coarse.reshape(-1, 128, 256).astype(np.float32), fine.astype(np.float32)


def dot(left, right, dims=((1,), (0,))):
    return lax.dot_general(left, right, (dims, ((), ())), preferred_element_type=F32)


def split(value):
    upper = value.astype(BF16)
    return upper, (value - upper.astype(F32)).astype(BF16)


def correlate(recv, send, coarse, fine, flat, y_own, y_far):
    first, own, far, ahead, behind, last = 0, 2, 6, 10, 14, 18
    flat[...] = recv[...].astype(F32).reshape(OWNERS * ROWS, 128)

    def line(side, part, slot):
        return pl.ds(side * ROWS + part * MINE + slot, EDEV, stride=2 * ROWS)

    def spectrum(side, slot, into):
        re, im = flat[line(side, 0, slot), :], flat[line(side, 1, slot), :]
        top = jnp.concatenate([re, im], axis=1).astype(BF16)
        bottom = jnp.concatenate([im, -re], axis=1).astype(BF16)
        step = dot(coarse[first + side], jnp.concatenate([top, bottom, top, bottom], axis=0))
        re, im = step[:, :128], step[:, 128:]
        c, s = fine[0], fine[1]
        if side == 0:
            re, im = re * c + im * s, im * c - re * s
        else:
            re, im = re * c - im * s, im * c + re * s
        into[pl.ds(slot * K0, K0), :] = jnp.concatenate(split(jnp.concatenate([re, im], axis=1)), axis=1)

    for slot in range(MINE):
        spectrum(0, slot, y_own)
        spectrum(1, slot, y_far)

    def triple(value, table):
        upper = coarse[table : table + 2].reshape(256, 256)
        lower = coarse[table + 2 : table + 4].reshape(256, 256)
        return dot(
            jnp.concatenate([value, value[:, :256]], axis=1), jnp.concatenate([upper, upper, lower], axis=0)
        )

    group = 4
    for step in range(MINE // group):
        rows = pl.ds(step * (group * K0), group * K0)
        left, right = triple(y_own[rows, :], own), triple(y_far[rows, :], far)
        a, b, c, d = left[:, :128], left[:, 128:], right[:, :128], right[:, 128:]
        spec = jnp.concatenate(split(jnp.concatenate([a * c - b * d, a * d + b * c], axis=1)), axis=1)
        lags = (triple(spec, ahead), triple(spec, behind))
        for member in range(group):
            tops, bottoms = [], []
            for part in lags:
                re, im = part[member * K0 : (member + 1) * K0, :128], part[member * K0 : (member + 1) * K0, 128:]
                tops.append(re * fine[2] - im * fine[3])
                bottoms.append(re * fine[3] + im * fine[2])
            upper, lower = split(
                jnp.concatenate([jnp.concatenate(tops, axis=1), jnp.concatenate(bottoms, axis=1)], axis=0)
            )
            both = dot(coarse[last : last + 2].reshape(256, 256), upper)
            result = both[:128] + both[128:] + dot(coarse[last], lower)
            slot = step * group + member
            flat[line(0, 0, slot), :] = result[:EDEV, :128]
            flat[line(0, 1, slot), :] = result[EDEV:, :128]
            flat[line(1, 0, slot), :] = -result[:EDEV, 128:]
            flat[line(1, 1, slot), :] = result[EDEV:, 128:]

    send[...] = flat[...].reshape(OWNERS, ROWS, 128).astype(BF16)


def one_hot(slot, begin, rows):
    order = lax.broadcasted_iota(jnp.int32, (rows, SLOTS), 0) + begin
    return jnp.where(order == slot, 1.0, 0.0).astype(BF16)


def kernel(
    less_hbm, greater_hbm, slot_hbm, coarse_hbm, fine_hbm,
    recv_two,
    less, greater, slot, wide, coarse, fine,
    hot, send_one, recv_one, send_two, flat, y_own, y_far,
    sent, came, kept, fetched,
):
    e = lax.axis_index("energy")
    p = lax.axis_index("pair")
    core, z, x = lax.rem(e, 2), lax.rem(lax.div(e, 2), 16), lax.div(p, 2)
    side = lax.rem(p, 2)
    y = lax.div(e, 32) * 2 + side
    place = e * 2 + side
    owner = (1 - core) * EDEV + lax.div(e, 2) * 2 + side

    sources = (slot_hbm, less_hbm, greater_hbm, coarse_hbm, fine_hbm)
    places = (slot, less, greater, wide, fine)
    fetches = [pltpu.make_async_copy(a, b, fetched.at[i]) for i, (a, b) in enumerate(zip(sources, places))]
    for fetch in fetches:
        fetch.start()

    columns = []
    for dy in range(4):
        to_y = lax.rem(y + dy, 4)
        columns.append((lax.div(to_y, 2) * 16, lax.rem(to_y, 2)))

    def at_z(to_z, to_core, columns, act):
        for high, to_side in columns:
            chip = high + to_z
            act(
                chip * 2 + to_core,
                x * 2 + to_side,
                (chip * 2 + to_core) * 2 + to_side,
                (1 - to_core) * EDEV + chip * 2 + to_side,
            )

    def at(dz, to_core, columns, act):
        at_z(jnp.where(z + dz >= 16, z + dz - 16, z + dz), to_core, columns, act)

    def peers(cores, act, visit=at):
        def both_ways(near, carry):
            for to_core in cores:
                for column in columns:
                    visit(7 - near, to_core, [column], act)
                    visit(9 + near, to_core, [column], act)
            return carry

        for to_core in cores:
            visit(8, to_core, columns, act)
        lax.fori_loop(0, 7, both_ways, 0)
        for to_core in cores:
            visit(0, to_core, columns[1:], act)
            pl.when(core != to_core)(functools.partial(visit, 0, to_core, columns[:1], act))

    def some_peers(to_core, odd, act):
        even = 1 - lax.rem(odd + z, 2)

        def both_ways(near, carry):
            for column in columns:
                at(7 + even - 2 * near, to_core, [column], act)
                at(9 + even + 2 * near, to_core, [column], act)
            return carry

        lax.fori_loop(0, 3, both_ways, 0)
        at(1 + even, to_core, columns[:1], act)
        for column in columns[1:]:
            at(1 + even, to_core, [column], act)
            at(15 + even, to_core, [column], act)
        pl.when(jnp.logical_or(even == 0, core != to_core))(
            functools.partial(at, 15 + even, to_core, columns[:1], act)
        )

    barrier = pltpu.get_barrier_semaphore()

    def greet(to_e, to_p, to_place, to_owner):
        pl.semaphore_signal(barrier, inc=1, device_id=(to_e, to_p), device_id_type=MESH)

    peers((1, 0), greet)
    fetches[0].wait()
    hot[...] = one_hot(slot[...], 0, SLOTS)

    def remote(src, dst, turn, to_e, to_p):
        pltpu.make_async_remote_copy(
            src_ref=src,
            dst_ref=dst,
            send_sem=sent.at[turn],
            recv_sem=came.at[turn],
            device_id=(to_e, to_p),
            device_id_type=MESH,
        ).start()

    def out(to_e, to_p, to_place, to_owner):
        remote(send_one.at[to_owner], recv_one.at[place], 0, to_e, to_p)

    def back(to_e, to_p, to_place, to_owner):
        remote(send_two.at[to_place], recv_two.at[owner], 1, to_e, to_p)

    others = pl.ds(0, OWNERS - 1)

    def arrive(src, dst, target, turn):
        stay = pltpu.make_async_copy(src, dst, kept)
        stay.start()
        stay.wait()
        pltpu.make_async_copy(target.at[others], target.at[others], came.at[turn]).wait()

    fetches[1].wait()
    fetches[2].wait()
    value = jnp.concatenate([less[0], greater[0], less[1], greater[1]], axis=0)
    for to_core in (1, 0):
        half = SLOTS // 2
        ordered = dot(hot[(1 - to_core) * half : (2 - to_core) * half, :], value, ((1,), (1,)))
        parts = [ordered[:, part * 128 : (part + 1) * 128].reshape(EDEV, MINE, 128) for part in range(2)]
        send_one[(1 - to_core) * EDEV : (2 - to_core) * EDEV] = jnp.concatenate(parts, axis=1).astype(BF16)
        if to_core == 1:
            pl.semaphore_wait(barrier, OWNERS - 1)
        for odd in (1, 0):
            some_peers(to_core, odd, out)

    fetches[3].wait()
    fetches[4].wait()
    coarse[...] = wide[...].astype(BF16)
    arrive(send_one.at[owner], recv_one.at[place], recv_one, 0)
    correlate(recv_one, send_two, coarse, fine, flat, y_own, y_far)
    for to_z in range(EARLY_Z):
        at_z(to_z, 0, columns[1:], back)
        pl.when(jnp.logical_or(z != to_z, core != 0))(functools.partial(at_z, to_z, 0, columns[:1], back))
    peers((1,), back)

    def later(dz, to_core, columns, act):
        to_z = jnp.where(z + dz >= 16, z + dz - 16, z + dz)
        pl.when(to_z >= EARLY_Z)(functools.partial(at_z, to_z, to_core, columns, act))

    peers((0,), back, later)
    arrive(send_two.at[place], recv_two.at[owner], recv_two, 1)

    for turn, source in enumerate((send_one, send_two)):
        pltpu.make_async_copy(source.at[others], source.at[others], sent.at[turn]).wait()


def reorder(back_hbm, slot_hbm, less_hbm, greater_hbm, back, slot, less, greater, fetched, stored):
    fetches = [
        pltpu.make_async_copy(slot_hbm, slot, fetched.at[0]),
        pltpu.make_async_copy(back_hbm, back, fetched.at[1]),
    ]
    for fetch in fetches:
        fetch.start()
    fetches[0].wait()
    hot = one_hot(slot[...], 0, SLOTS)
    fetches[1].wait()
    value = back[...].astype(F32)
    ordered = jnp.concatenate(
        [value[:, part * MINE : (part + 1) * MINE].reshape(SLOTS, 128) for part in range(2)], axis=1
    )
    result = dot(ordered.astype(BF16), hot, ((0,), (0,))).astype(BF16)
    stores = []
    for part in range(2):
        for array, (kept, result_hbm) in enumerate(((less, less_hbm), (greater, greater_hbm))):
            kept[part] = result[(part * 2 + array) * N0 : (part * 2 + array + 1) * N0]
            stores.append(pltpu.make_async_copy(kept.at[part], result_hbm.at[part], stored.at[part, array]))
            stores[-1].start()
    for store in stores:
        store.wait()


def per_device(g_less, g_greater, pair_slot):
    coarse, fine = tables()
    hbm = pl.BlockSpec(memory_space=pltpu.HBM)
    grant = 60 * 1024 * 1024
    packets = pltpu.VMEM((OWNERS, ROWS, 128), BF16)
    back = pl.pallas_call(
        kernel,
        out_shape=jax.ShapeDtypeStruct((OWNERS, ROWS, 128), BF16),
        in_specs=[hbm] * 5,
        out_specs=hbm,
        scratch_shapes=[
            pltpu.VMEM((2, N0, SLOTS), BF16),
            pltpu.VMEM((2, N0, SLOTS), BF16),
            pltpu.VMEM((1, SLOTS), jnp.int32),
            pltpu.VMEM(coarse.shape, F32),
            pltpu.VMEM(coarse.shape, BF16),
            pltpu.VMEM(fine.shape, F32),
            pltpu.VMEM((SLOTS, SLOTS), BF16),
            packets,
            packets,
            packets,
            pltpu.VMEM((OWNERS * ROWS, 128), F32),
            pltpu.VMEM((MINE * K0, 512), BF16),
            pltpu.VMEM((MINE * K0, 512), BF16),
            pltpu.SemaphoreType.DMA((2,)),
            pltpu.SemaphoreType.DMA((2,)),
            pltpu.SemaphoreType.DMA,
            pltpu.SemaphoreType.DMA((5,)),
        ],
        compiler_params=pltpu.CompilerParams(collective_id=0, has_side_effects=True, vmem_limit_bytes=grant),
        cost_estimate=pl.CostEstimate(flops=4 * 10**9, bytes_accessed=4 * 10**6, transcendentals=0),
    )(g_less, g_greater, pair_slot, jnp.asarray(coarse), jnp.asarray(fine))
    shape = jax.ShapeDtypeStruct((2, N0, SLOTS), BF16)
    return pl.pallas_call(
        reorder,
        out_shape=(shape, shape),
        in_specs=[hbm, hbm],
        out_specs=(hbm, hbm),
        scratch_shapes=[
            packets,
            pltpu.VMEM((1, SLOTS), jnp.int32),
            pltpu.VMEM(shape.shape, BF16),
            pltpu.VMEM(shape.shape, BF16),
            pltpu.SemaphoreType.DMA((2,)),
            pltpu.SemaphoreType.DMA((2, 2)),
        ],
        compiler_params=pltpu.CompilerParams(vmem_limit_bytes=grant),
        cost_estimate=pl.CostEstimate(flops=10**9, bytes_accessed=10**6, transcendentals=0),
    )(back, pair_slot)


def solution(mesh):
    placed = (P(None, "energy", "pair"), P(None, "energy", "pair"), P("pair", None))
    return jax.shard_map(
        per_device,
        mesh=mesh,
        in_specs=placed,
        out_specs=(P(None, "energy", "pair"), P(None, "energy", "pair")),
        check_vma=False,
    )
```

```python
import functools
import math

import jax
import jax.numpy as jnp
import ml_dtypes
import numpy as np
from jax import lax
from jax.experimental import pallas as pl
from jax.experimental.pallas import tpu as pltpu
from jax.sharding import PartitionSpec as P

NE = 4096
N0 = 64
EDEV = 64
OWNERS = 2 * EDEV
SLOTS = 1024
ROUNDS = 2
MINE = SLOTS // OWNERS // ROUNDS
ROWS = 2 * MINE
K0 = 128
K1 = 64
LENGTH = 2 * NE
F32 = jnp.float32
BF16 = jnp.bfloat16
MESH = pl.DeviceIdType.MESH


def upper_lower(table):
    upper = table.astype(ml_dtypes.bfloat16)
    lower = (table - upper.astype(np.float64)).astype(ml_dtypes.bfloat16)
    return upper, lower


def cos_sin(rows, cols, period):
    angle = (np.arange(rows)[:, None] * np.arange(cols)[None, :] % period) * (2.0 * math.pi / period)
    return np.cos(angle), np.sin(angle)


def tables():
    lanes = lambda *parts: np.concatenate(parts, axis=1)
    both = lambda table: np.concatenate(upper_lower(table))
    straight = lambda part: np.kron(np.eye(2), part)
    crossed = lambda part: np.kron(np.eye(2)[::-1], part)
    c, s = cos_sin(K0, EDEV, K0)
    first = [lanes(*upper_lower(lanes(c, s))), lanes(*upper_lower(lanes(c, -s)))]
    c, s = cos_sin(N0, K1, K1)
    own = both(np.block([[straight(c), -straight(s)], [straight(s), straight(c)]]))
    far = both(np.block([[crossed(c), crossed(s)], [-crossed(s), crossed(c)]]))
    ahead = both(np.block([[straight(c), straight(s)], [-straight(s), straight(c)]]))
    behind = both(np.block([[crossed(c), crossed(s)], [crossed(s), -crossed(c)]]))
    c, s = cos_sin(EDEV, K0, K0)
    last = both(np.block([[c, -s], [s, c]]))
    coarse = np.concatenate(first + [own, far, ahead, behind, last])
    c, s = cos_sin(K0, N0, LENGTH)
    scale = 1.0 / (math.sqrt(NE) * LENGTH)
    fine = np.stack([lanes(c, c), lanes(s, s), lanes(s, s) * scale, -lanes(c, c) * scale])
    return coarse.reshape(-1, 128, 256).astype(np.float32), fine.astype(np.float32)


def dot(left, right, dims=((1,), (0,))):
    return lax.dot_general(left, right, (dims, ((), ())), preferred_element_type=F32)


def split(value):
    upper = value.astype(BF16)
    return upper, (value - upper.astype(F32)).astype(BF16)


def correlate(recv, send, coarse, fine, flat, y_own, y_far):
    first, own, far, ahead, behind, last = 0, 2, 6, 10, 14, 18
    flat[...] = recv[...].astype(F32).reshape(OWNERS * ROWS, 128)

    def line(side, part, slot):
        return pl.ds(side * ROWS + part * MINE + slot, EDEV, stride=2 * ROWS)

    def spectrum(side, slot, into):
        re, im = flat[line(side, 0, slot), :], flat[line(side, 1, slot), :]
        top = jnp.concatenate([re, im], axis=1).astype(BF16)
        bottom = jnp.concatenate([im, -re], axis=1).astype(BF16)
        step = dot(coarse[first + side], jnp.concatenate([top, bottom, top, bottom], axis=0))
        re, im = step[:, :128], step[:, 128:]
        c, s = fine[0], fine[1]
        if side == 0:
            re, im = re * c + im * s, im * c - re * s
        else:
            re, im = re * c - im * s, im * c + re * s
        into[pl.ds(slot * K0, K0), :] = jnp.concatenate(split(jnp.concatenate([re, im], axis=1)), axis=1)

    for slot in range(MINE):
        spectrum(0, slot, y_own)
        spectrum(1, slot, y_far)

    def triple(value, table):
        upper = coarse[table : table + 2].reshape(256, 256)
        lower = coarse[table + 2 : table + 4].reshape(256, 256)
        return dot(
            jnp.concatenate([value, value[:, :256]], axis=1), jnp.concatenate([upper, upper, lower], axis=0)
        )

    group = MINE
    for step in range(MINE // group):
        rows = pl.ds(step * (group * K0), group * K0)
        left, right = triple(y_own[rows, :], own), triple(y_far[rows, :], far)
        a, b, c, d = left[:, :128], left[:, 128:], right[:, :128], right[:, 128:]
        spec = jnp.concatenate(split(jnp.concatenate([a * c - b * d, a * d + b * c], axis=1)), axis=1)
        lags = (triple(spec, ahead), triple(spec, behind))
        for member in range(group):
            tops, bottoms = [], []
            for part in lags:
                re, im = part[member * K0 : (member + 1) * K0, :128], part[member * K0 : (member + 1) * K0, 128:]
                tops.append(re * fine[2] - im * fine[3])
                bottoms.append(re * fine[3] + im * fine[2])
            upper, lower = split(
                jnp.concatenate([jnp.concatenate(tops, axis=1), jnp.concatenate(bottoms, axis=1)], axis=0)
            )
            both = dot(coarse[last : last + 2].reshape(256, 256), upper)
            result = both[:128] + both[128:] + dot(coarse[last], lower)
            slot = step * group + member
            flat[line(0, 0, slot), :] = result[:EDEV, :128]
            flat[line(0, 1, slot), :] = result[EDEV:, :128]
            flat[line(1, 0, slot), :] = -result[:EDEV, 128:]
            flat[line(1, 1, slot), :] = result[EDEV:, 128:]

    send[...] = flat[...].reshape(OWNERS, ROWS, 128).astype(BF16)


def one_hot(slot, rounds):
    owners = (len(rounds) * OWNERS, SLOTS)
    first = (lax.broadcasted_iota(jnp.int32, owners, 0) + rounds[0] * OWNERS) * MINE
    hits = [jnp.where(first == slot - mine, 1.0, 0.0) for mine in range(MINE)]
    return jnp.concatenate(hits, axis=0).astype(BF16)


def kernel(
    less_hbm, greater_hbm, slot_hbm, coarse_hbm, fine_hbm,
    recv_two,
    less, greater, slot, wide, coarse, fine,
    send_one, recv_one, send_two, flat, y_own, y_far,
    sent, came, kept, fetched,
):
    e = lax.axis_index("energy")
    p = lax.axis_index("pair")
    core, z, x = lax.rem(e, 2), lax.rem(lax.div(e, 2), 16), lax.div(p, 2)
    side = lax.rem(p, 2)
    y = lax.div(e, 32) * 2 + side
    me = e * 2 + side

    sources = (slot_hbm, less_hbm, greater_hbm, coarse_hbm, fine_hbm)
    places = (slot, less, greater, wide, fine)
    fetches = [pltpu.make_async_copy(a, b, fetched.at[i]) for i, (a, b) in enumerate(zip(sources, places))]
    for fetch in fetches:
        fetch.start()

    columns = []
    for dy in range(4):
        to_y = lax.rem(y + dy, 4)
        columns.append((lax.div(to_y, 2) * 16, lax.rem(to_y, 2)))

    def peers(act):
        def at(dz, to_core, columns):
            to_z = jnp.where(z + dz >= 16, z + dz - 16, z + dz)
            for high, to_side in columns:
                to_e = (high + to_z) * 2 + to_core
                act(to_e, x * 2 + to_side, to_e * 2 + to_side)

        def both_ways(near, carry):
            for to_core in (1, 0):
                at(7 - near, to_core, columns)
                at(9 + near, to_core, columns)
            return carry

        for to_core in (1, 0):
            at(8, to_core, columns)
        lax.fori_loop(0, 7, both_ways, 0)
        for to_core in (1, 0):
            at(0, to_core, columns[1:])
            pl.when(core != to_core)(functools.partial(at, 0, to_core, columns[:1]))

    barrier = pltpu.get_barrier_semaphore()

    def greet(to_e, to_p, to):
        pl.semaphore_signal(barrier, inc=1, device_id=(to_e, to_p), device_id_type=MESH)

    peers(greet)

    others = pl.ds(0, OWNERS - 1)

    def depart(source, target, turn, part):
        def start(to_e, to_p, to):
            pltpu.make_async_remote_copy(
                src_ref=source.at[to],
                dst_ref=target.at[me],
                send_sem=sent.at[turn, part],
                recv_sem=came.at[turn, part],
                device_id=(to_e, to_p),
                device_id_type=MESH,
            ).start()

        peers(start)

    def arrive(source, target, turn, part):
        stay = pltpu.make_async_copy(source.at[me], target.at[me], kept)
        stay.start()
        stay.wait()
        pltpu.make_async_copy(target.at[others], target.at[others], came.at[turn, part]).wait()

    fetches[0].wait()
    for part in range(ROUNDS):
        hot = one_hot(slot[...], (part,))
        if part == 0:
            fetches[1].wait()
            fetches[2].wait()
        value = jnp.concatenate([less[0], greater[0], less[1], greater[1]], axis=0)
        ordered = dot(hot, value, ((1,), (1,)))
        for mine in range(MINE):
            for half in range(2):
                flat[pl.ds(half * MINE + mine, OWNERS, stride=ROWS), :] = ordered[
                    mine * OWNERS : (mine + 1) * OWNERS, half * 128 : (half + 1) * 128
                ]
        send_one[part] = flat[...].reshape(OWNERS, ROWS, 128).astype(BF16)
        if part == 0:
            pl.semaphore_wait(barrier, OWNERS - 1)
        depart(send_one.at[part], recv_one.at[part], 0, part)

    fetches[3].wait()
    fetches[4].wait()
    coarse[...] = wide[...].astype(BF16)
    for part in range(ROUNDS):
        arrive(send_one.at[part], recv_one.at[part], 0, part)
        correlate(recv_one.at[part], send_two.at[part], coarse, fine, flat, y_own, y_far)
        depart(send_two.at[part], recv_two.at[part], 1, part)
    for part in range(ROUNDS):
        arrive(send_two.at[part], recv_two.at[part], 1, part)

    for turn, source in enumerate((send_one, send_two)):
        for part in range(ROUNDS):
            done = source.at[part].at[others]
            pltpu.make_async_copy(done, done, sent.at[turn, part]).wait()


def reorder(back_hbm, slot_hbm, less_hbm, greater_hbm, back, slot, flat, less, greater, fetched, stored):
    fetches = [
        pltpu.make_async_copy(slot_hbm, slot, fetched.at[0]),
        pltpu.make_async_copy(back_hbm, back, fetched.at[1]),
    ]
    for fetch in fetches:
        fetch.start()
    fetches[0].wait()
    hot = one_hot(slot[...], tuple(range(ROUNDS)))
    fetches[1].wait()
    count = ROUNDS * OWNERS
    flat[...] = back[...].astype(F32).reshape(count * ROWS, 128)
    ordered = jnp.concatenate(
        [
            jnp.concatenate(
                [flat[pl.ds(part * MINE + mine, count, stride=ROWS), :] for mine in range(MINE)], axis=0
            )
            for part in range(2)
        ],
        axis=1,
    )
    result = dot(ordered.astype(BF16), hot, ((0,), (0,))).astype(BF16)
    stores = []
    for part in range(2):
        for array, (kept, result_hbm) in enumerate(((less, less_hbm), (greater, greater_hbm))):
            kept[part] = result[(part * 2 + array) * N0 : (part * 2 + array + 1) * N0]
            stores.append(pltpu.make_async_copy(kept.at[part], result_hbm.at[part], stored.at[part, array]))
            stores[-1].start()
    for store in stores:
        store.wait()


def per_device(g_less, g_greater, pair_slot):
    coarse, fine = tables()
    hbm = pl.BlockSpec(memory_space=pltpu.HBM)
    grant = 60 * 1024 * 1024
    packets = pltpu.VMEM((ROUNDS, OWNERS, ROWS, 128), BF16)
    back = pl.pallas_call(
        kernel,
        out_shape=jax.ShapeDtypeStruct(packets.shape, BF16),
        in_specs=[hbm] * 5,
        out_specs=hbm,
        scratch_shapes=[
            pltpu.VMEM((2, N0, SLOTS), BF16),
            pltpu.VMEM((2, N0, SLOTS), BF16),
            pltpu.VMEM((1, SLOTS), jnp.int32),
            pltpu.VMEM(coarse.shape, F32),
            pltpu.VMEM(coarse.shape, BF16),
            pltpu.VMEM(fine.shape, F32),
            packets,
            packets,
            packets,
            pltpu.VMEM((OWNERS * ROWS, 128), F32),
            pltpu.VMEM((MINE * K0, 512), BF16),
            pltpu.VMEM((MINE * K0, 512), BF16),
            pltpu.SemaphoreType.DMA((2, ROUNDS)),
            pltpu.SemaphoreType.DMA((2, ROUNDS)),
            pltpu.SemaphoreType.DMA,
            pltpu.SemaphoreType.DMA((5,)),
        ],
        compiler_params=pltpu.CompilerParams(collective_id=0, has_side_effects=True, vmem_limit_bytes=grant),
        cost_estimate=pl.CostEstimate(flops=4 * 10**9, bytes_accessed=4 * 10**6, transcendentals=0),
    )(g_less, g_greater, pair_slot, jnp.asarray(coarse), jnp.asarray(fine))
    shape = jax.ShapeDtypeStruct((2, N0, SLOTS), BF16)
    return pl.pallas_call(
        reorder,
        out_shape=(shape, shape),
        in_specs=[hbm, hbm],
        out_specs=(hbm, hbm),
        scratch_shapes=[
            packets,
            pltpu.VMEM((1, SLOTS), jnp.int32),
            pltpu.VMEM((ROUNDS * OWNERS * ROWS, 128), F32),
            pltpu.VMEM(shape.shape, BF16),
            pltpu.VMEM(shape.shape, BF16),
            pltpu.SemaphoreType.DMA((2,)),
            pltpu.SemaphoreType.DMA((2, 2)),
        ],
        compiler_params=pltpu.CompilerParams(vmem_limit_bytes=grant),
        cost_estimate=pl.CostEstimate(flops=10**9, bytes_accessed=10**6, transcendentals=0),
    )(back, pair_slot)


def solution(mesh):
    placed = (P(None, "energy", "pair"), P(None, "energy", "pair"), P("pair", None))
    return jax.shard_map(
        per_device,
        mesh=mesh,
        in_specs=placed,
        out_specs=(P(None, "energy", "pair"), P(None, "energy", "pair")),
        check_vma=False,
    )
```

```python
import functools
import math

import jax
import jax.numpy as jnp
import ml_dtypes
import numpy as np
from jax import lax
from jax.experimental import pallas as pl
from jax.experimental.pallas import tpu as pltpu
from jax.sharding import PartitionSpec as P

NE = 4096
N0 = 64
EDEV = 64
OWNERS = 2 * EDEV
SLOTS = 1024
MINE = SLOTS // OWNERS
ROWS = 2 * MINE
EARLY_Z = 3
K0 = 128
K1 = 64
LENGTH = 2 * NE
F32 = jnp.float32
BF16 = jnp.bfloat16
MESH = pl.DeviceIdType.MESH


def upper_lower(table):
    upper = table.astype(ml_dtypes.bfloat16)
    lower = (table - upper.astype(np.float64)).astype(ml_dtypes.bfloat16)
    return upper, lower


def cos_sin(rows, cols, period):
    angle = (np.arange(rows)[:, None] * np.arange(cols)[None, :] % period) * (2.0 * math.pi / period)
    return np.cos(angle), np.sin(angle)


def tables():
    lanes = lambda *parts: np.concatenate(parts, axis=1)
    both = lambda table: np.concatenate(upper_lower(table))
    straight = lambda part: np.kron(np.eye(2), part)
    crossed = lambda part: np.kron(np.eye(2)[::-1], part)
    c, s = cos_sin(K0, EDEV, K0)
    first = [lanes(*upper_lower(lanes(c, s))), lanes(*upper_lower(lanes(c, -s)))]
    c, s = cos_sin(N0, K1, K1)
    own = both(np.block([[straight(c), -straight(s)], [straight(s), straight(c)]]))
    far = both(np.block([[crossed(c), crossed(s)], [-crossed(s), crossed(c)]]))
    ahead = both(np.block([[straight(c), straight(s)], [-straight(s), straight(c)]]))
    behind = both(np.block([[crossed(c), crossed(s)], [crossed(s), -crossed(c)]]))
    c, s = cos_sin(EDEV, K0, K0)
    last = both(np.block([[c, -s], [s, c]]))
    coarse = np.concatenate(first + [own, far, ahead, behind, last])
    c, s = cos_sin(K0, N0, LENGTH)
    scale = 1.0 / (math.sqrt(NE) * LENGTH)
    fine = np.stack([lanes(c, c), lanes(s, s), lanes(s, s) * scale, -lanes(c, c) * scale])
    return coarse.reshape(-1, 128, 256).astype(np.float32), fine.astype(np.float32)


def dot(left, right, dims=((1,), (0,))):
    return lax.dot_general(left, right, (dims, ((), ())), preferred_element_type=F32)


def split(value):
    upper = value.astype(BF16)
    return upper, (value - upper.astype(F32)).astype(BF16)


def correlate(recv, send, coarse, fine, flat, y_own, y_far):
    first, own, far, ahead, behind, last = 0, 2, 6, 10, 14, 18
    flat[...] = recv[...].astype(F32).reshape(OWNERS * ROWS, 128)

    def line(side, part, slot):
        return pl.ds(side * ROWS + part * MINE + slot, EDEV, stride=2 * ROWS)

    def spectrum(side, slot, into):
        re, im = flat[line(side, 0, slot), :], flat[line(side, 1, slot), :]
        top = jnp.concatenate([re, im], axis=1).astype(BF16)
        bottom = jnp.concatenate([im, -re], axis=1).astype(BF16)
        step = dot(coarse[first + side], jnp.concatenate([top, bottom, top, bottom], axis=0))
        re, im = step[:, :128], step[:, 128:]
        c, s = fine[0], fine[1]
        if side == 0:
            re, im = re * c + im * s, im * c - re * s
        else:
            re, im = re * c - im * s, im * c + re * s
        into[pl.ds(slot * K0, K0), :] = jnp.concatenate(split(jnp.concatenate([re, im], axis=1)), axis=1)

    for slot in range(MINE):
        spectrum(0, slot, y_own)
        spectrum(1, slot, y_far)

    def triple(value, table):
        upper = coarse[table : table + 2].reshape(256, 256)
        lower = coarse[table + 2 : table + 4].reshape(256, 256)
        return dot(
            jnp.concatenate([value, value[:, :256]], axis=1), jnp.concatenate([upper, upper, lower], axis=0)
        )

    group = 4
    for step in range(MINE // group):
        rows = pl.ds(step * (group * K0), group * K0)
        left, right = triple(y_own[rows, :], own), triple(y_far[rows, :], far)
        a, b, c, d = left[:, :128], left[:, 128:], right[:, :128], right[:, 128:]
        spec = jnp.concatenate(split(jnp.concatenate([a * c - b * d, a * d + b * c], axis=1)), axis=1)
        lags = (triple(spec, ahead), triple(spec, behind))
        for member in range(group):
            tops, bottoms = [], []
            for part in lags:
                re, im = part[member * K0 : (member + 1) * K0, :128], part[member * K0 : (member + 1) * K0, 128:]
                tops.append(re * fine[2] - im * fine[3])
                bottoms.append(re * fine[3] + im * fine[2])
            upper, lower = split(
                jnp.concatenate([jnp.concatenate(tops, axis=1), jnp.concatenate(bottoms, axis=1)], axis=0)
            )
            both = dot(coarse[last : last + 2].reshape(256, 256), upper)
            result = both[:128] + both[128:] + dot(coarse[last], lower)
            slot = step * group + member
            flat[line(0, 0, slot), :] = result[:EDEV, :128]
            flat[line(0, 1, slot), :] = result[EDEV:, :128]
            flat[line(1, 0, slot), :] = -result[:EDEV, 128:]
            flat[line(1, 1, slot), :] = result[EDEV:, 128:]

    send[...] = flat[...].reshape(OWNERS, ROWS, 128).astype(BF16)


def one_hot(slot, begin, rows):
    order = lax.broadcasted_iota(jnp.int32, (rows, SLOTS), 0) + begin
    return jnp.where(order == slot, 1.0, 0.0).astype(BF16)


def kernel(
    less_hbm, greater_hbm, slot_hbm, coarse_hbm, fine_hbm,
    recv_two,
    less, greater, slot, wide, coarse, fine,
    hot, send_one, recv_one, send_two, flat, y_own, y_far,
    sent, came, kept, fetched,
):
    e = lax.axis_index("energy")
    p = lax.axis_index("pair")
    core, z, x = lax.rem(e, 2), lax.rem(lax.div(e, 2), 16), lax.div(p, 2)
    side = lax.rem(p, 2)
    y = lax.div(e, 32) * 2 + side
    place = e * 2 + side
    owner = (1 - core) * EDEV + lax.div(e, 2) * 2 + side

    sources = (slot_hbm, less_hbm, greater_hbm, coarse_hbm, fine_hbm)
    places = (slot, less, greater, wide, fine)
    fetches = [pltpu.make_async_copy(a, b, fetched.at[i]) for i, (a, b) in enumerate(zip(sources, places))]
    for fetch in fetches:
        fetch.start()

    columns = []
    for dy in range(4):
        to_y = lax.rem(y + dy, 4)
        columns.append((lax.div(to_y, 2) * 16, lax.rem(to_y, 2)))

    def at_z(to_z, to_core, columns, act):
        for high, to_side in columns:
            chip = high + to_z
            act(
                chip * 2 + to_core,
                x * 2 + to_side,
                (chip * 2 + to_core) * 2 + to_side,
                (1 - to_core) * EDEV + chip * 2 + to_side,
            )

    def at(dz, to_core, columns, act):
        at_z(jnp.where(z + dz >= 16, z + dz - 16, z + dz), to_core, columns, act)

    def peers(cores, act, visit=at):
        def both_ways(near, carry):
            for to_core in cores:
                visit(7 - near, to_core, columns, act)
                visit(9 + near, to_core, columns, act)
            return carry

        for to_core in cores:
            visit(8, to_core, columns, act)
        lax.fori_loop(0, 7, both_ways, 0)
        for to_core in cores:
            visit(0, to_core, columns[1:], act)
            pl.when(core != to_core)(functools.partial(visit, 0, to_core, columns[:1], act))

    def some_peers(to_core, odd, act):
        even = 1 - lax.rem(odd + z, 2)

        def both_ways(near, carry):
            at(7 + even - 2 * near, to_core, columns, act)
            at(9 + even + 2 * near, to_core, columns, act)
            return carry

        lax.fori_loop(0, 3, both_ways, 0)
        at(1 + even, to_core, columns, act)
        at(15 + even, to_core, columns[1:], act)
        pl.when(jnp.logical_or(even == 0, core != to_core))(
            functools.partial(at, 15 + even, to_core, columns[:1], act)
        )

    barrier = pltpu.get_barrier_semaphore()

    def greet(to_e, to_p, to_place, to_owner):
        pl.semaphore_signal(barrier, inc=1, device_id=(to_e, to_p), device_id_type=MESH)

    peers((1, 0), greet)
    fetches[0].wait()
    hot[...] = one_hot(slot[...], 0, SLOTS)

    def remote(src, dst, turn, to_e, to_p):
        pltpu.make_async_remote_copy(
            src_ref=src,
            dst_ref=dst,
            send_sem=sent.at[turn],
            recv_sem=came.at[turn],
            device_id=(to_e, to_p),
            device_id_type=MESH,
        ).start()

    def out(to_e, to_p, to_place, to_owner):
        remote(send_one.at[to_owner], recv_one.at[place], 0, to_e, to_p)

    def back(to_e, to_p, to_place, to_owner):
        remote(send_two.at[to_place], recv_two.at[owner], 1, to_e, to_p)

    others = pl.ds(0, OWNERS - 1)

    def arrive(src, dst, target, turn):
        stay = pltpu.make_async_copy(src, dst, kept)
        stay.start()
        stay.wait()
        pltpu.make_async_copy(target.at[others], target.at[others], came.at[turn]).wait()

    fetches[1].wait()
    fetches[2].wait()
    value = jnp.concatenate([less[0], greater[0], less[1], greater[1]], axis=0)
    for to_core in (1, 0):
        half = SLOTS // 2
        ordered = dot(hot[(1 - to_core) * half : (2 - to_core) * half, :], value, ((1,), (1,)))
        parts = [ordered[:, part * 128 : (part + 1) * 128].reshape(EDEV, MINE, 128) for part in range(2)]
        send_one[(1 - to_core) * EDEV : (2 - to_core) * EDEV] = jnp.concatenate(parts, axis=1).astype(BF16)
        if to_core == 1:
            pl.semaphore_wait(barrier, OWNERS - 1)
        for odd in (1, 0):
            some_peers(to_core, odd, out)

    fetches[3].wait()
    fetches[4].wait()
    coarse[...] = wide[...].astype(BF16)
    arrive(send_one.at[owner], recv_one.at[place], recv_one, 0)
    correlate(recv_one, send_two, coarse, fine, flat, y_own, y_far)
    def sooner(dz, to_core, columns, act):
        to_z = jnp.where(z + dz >= 16, z + dz - 16, z + dz)
        if to_core == 1:
            at_z(to_z, to_core, columns, act)
        else:
            pl.when(to_z < EARLY_Z)(functools.partial(at_z, to_z, to_core, columns, act))

    def later(dz, to_core, columns, act):
        to_z = jnp.where(z + dz >= 16, z + dz - 16, z + dz)
        pl.when(to_z >= EARLY_Z)(functools.partial(at_z, to_z, to_core, columns, act))

    peers((0, 1), back, sooner)
    peers((0,), back, later)
    arrive(send_two.at[place], recv_two.at[owner], recv_two, 1)

    for turn, source in enumerate((send_one, send_two)):
        pltpu.make_async_copy(source.at[others], source.at[others], sent.at[turn]).wait()


def reorder(back_hbm, slot_hbm, less_hbm, greater_hbm, back, slot, less, greater, fetched, stored):
    fetches = [
        pltpu.make_async_copy(slot_hbm, slot, fetched.at[0]),
        pltpu.make_async_copy(back_hbm, back, fetched.at[1]),
    ]
    for fetch in fetches:
        fetch.start()
    fetches[0].wait()
    hot = one_hot(slot[...], 0, SLOTS)
    fetches[1].wait()
    value = back[...].astype(F32)
    ordered = jnp.concatenate(
        [value[:, part * MINE : (part + 1) * MINE].reshape(SLOTS, 128) for part in range(2)], axis=1
    )
    result = dot(ordered.astype(BF16), hot, ((0,), (0,))).astype(BF16)
    stores = []
    for part in range(2):
        for array, (kept, result_hbm) in enumerate(((less, less_hbm), (greater, greater_hbm))):
            kept[part] = result[(part * 2 + array) * N0 : (part * 2 + array + 1) * N0]
            stores.append(pltpu.make_async_copy(kept.at[part], result_hbm.at[part], stored.at[part, array]))
            stores[-1].start()
    for store in stores:
        store.wait()


def per_device(g_less, g_greater, pair_slot):
    coarse, fine = tables()
    hbm = pl.BlockSpec(memory_space=pltpu.HBM)
    grant = 60 * 1024 * 1024
    packets = pltpu.VMEM((OWNERS, ROWS, 128), BF16)
    back = pl.pallas_call(
        kernel,
        out_shape=jax.ShapeDtypeStruct((OWNERS, ROWS, 128), BF16),
        in_specs=[hbm] * 5,
        out_specs=hbm,
        scratch_shapes=[
            pltpu.VMEM((2, N0, SLOTS), BF16),
            pltpu.VMEM((2, N0, SLOTS), BF16),
            pltpu.VMEM((1, SLOTS), jnp.int32),
            pltpu.VMEM(coarse.shape, F32),
            pltpu.VMEM(coarse.shape, BF16),
            pltpu.VMEM(fine.shape, F32),
            pltpu.VMEM((SLOTS, SLOTS), BF16),
            packets,
            packets,
            packets,
            pltpu.VMEM((OWNERS * ROWS, 128), F32),
            pltpu.VMEM((MINE * K0, 512), BF16),
            pltpu.VMEM((MINE * K0, 512), BF16),
            pltpu.SemaphoreType.DMA((2,)),
            pltpu.SemaphoreType.DMA((2,)),
            pltpu.SemaphoreType.DMA,
            pltpu.SemaphoreType.DMA((5,)),
        ],
        compiler_params=pltpu.CompilerParams(collective_id=0, has_side_effects=True, vmem_limit_bytes=grant),
        cost_estimate=pl.CostEstimate(flops=4 * 10**9, bytes_accessed=4 * 10**6, transcendentals=0),
    )(g_less, g_greater, pair_slot, jnp.asarray(coarse), jnp.asarray(fine))
    shape = jax.ShapeDtypeStruct((2, N0, SLOTS), BF16)
    return pl.pallas_call(
        reorder,
        out_shape=(shape, shape),
        in_specs=[hbm, hbm],
        out_specs=(hbm, hbm),
        scratch_shapes=[
            packets,
            pltpu.VMEM((1, SLOTS), jnp.int32),
            pltpu.VMEM(shape.shape, BF16),
            pltpu.VMEM(shape.shape, BF16),
            pltpu.SemaphoreType.DMA((2,)),
            pltpu.SemaphoreType.DMA((2, 2)),
        ],
        compiler_params=pltpu.CompilerParams(vmem_limit_bytes=grant),
        cost_estimate=pl.CostEstimate(flops=10**9, bytes_accessed=10**6, transcendentals=0),
    )(back, pair_slot)


def solution(mesh):
    placed = (P(None, "energy", "pair"), P(None, "energy", "pair"), P("pair", None))
    return jax.shard_map(
        per_device,
        mesh=mesh,
        in_specs=placed,
        out_specs=(P(None, "energy", "pair"), P(None, "energy", "pair")),
        check_vma=False,
    )
```

```python
import functools
import math

import jax
import jax.numpy as jnp
import ml_dtypes
import numpy as np
from jax import lax
from jax.experimental import pallas as pl
from jax.experimental.pallas import tpu as pltpu
from jax.sharding import PartitionSpec as P

NE = 4096
N0 = 64
EDEV = 64
OWNERS = 2 * EDEV
SLOTS = 1024
MINE = SLOTS // OWNERS
ROWS = 2 * MINE
EARLY_Z = 2
K0 = 128
K1 = 64
LENGTH = 2 * NE
F32 = jnp.float32
BF16 = jnp.bfloat16
MESH = pl.DeviceIdType.MESH


def upper_lower(table):
    upper = table.astype(ml_dtypes.bfloat16)
    lower = (table - upper.astype(np.float64)).astype(ml_dtypes.bfloat16)
    return upper, lower


def cos_sin(rows, cols, period):
    angle = (np.arange(rows)[:, None] * np.arange(cols)[None, :] % period) * (2.0 * math.pi / period)
    return np.cos(angle), np.sin(angle)


def tables():
    lanes = lambda *parts: np.concatenate(parts, axis=1)
    both = lambda table: np.concatenate(upper_lower(table))
    straight = lambda part: np.kron(np.eye(2), part)
    crossed = lambda part: np.kron(np.eye(2)[::-1], part)
    c, s = cos_sin(K0, EDEV, K0)
    first = [lanes(*upper_lower(lanes(c, s))), lanes(*upper_lower(lanes(c, -s)))]
    c, s = cos_sin(N0, K1, K1)
    own = both(np.block([[straight(c), -straight(s)], [straight(s), straight(c)]]))
    far = both(np.block([[crossed(c), crossed(s)], [-crossed(s), crossed(c)]]))
    ahead = both(np.block([[straight(c), straight(s)], [-straight(s), straight(c)]]))
    behind = both(np.block([[crossed(c), crossed(s)], [crossed(s), -crossed(c)]]))
    c, s = cos_sin(EDEV, K0, K0)
    last = both(np.block([[c, -s], [s, c]]))
    coarse = np.concatenate(first + [own, far, ahead, behind, last])
    c, s = cos_sin(K0, N0, LENGTH)
    scale = 1.0 / (math.sqrt(NE) * LENGTH)
    fine = np.stack([lanes(c, c), lanes(s, s), lanes(s, s) * scale, -lanes(c, c) * scale])
    return coarse.reshape(-1, 128, 256).astype(np.float32), fine.astype(np.float32)


def dot(left, right, dims=((1,), (0,))):
    return lax.dot_general(left, right, (dims, ((), ())), preferred_element_type=F32)


def split(value):
    upper = value.astype(BF16)
    return upper, (value - upper.astype(F32)).astype(BF16)


def correlate(recv, send, coarse, fine, flat, y_own, y_far):
    first, own, far, ahead, behind, last = 0, 2, 6, 10, 14, 18
    flat[...] = recv[...].astype(F32).reshape(OWNERS * ROWS, 128)

    def line(side, part, slot):
        return pl.ds(side * ROWS + part * MINE + slot, EDEV, stride=2 * ROWS)

    def spectrum(side, slot, into):
        re, im = flat[line(side, 0, slot), :], flat[line(side, 1, slot), :]
        top = jnp.concatenate([re, im], axis=1).astype(BF16)
        bottom = jnp.concatenate([im, -re], axis=1).astype(BF16)
        step = dot(coarse[first + side], jnp.concatenate([top, bottom, top, bottom], axis=0))
        re, im = step[:, :128], step[:, 128:]
        c, s = fine[0], fine[1]
        if side == 0:
            re, im = re * c + im * s, im * c - re * s
        else:
            re, im = re * c - im * s, im * c + re * s
        into[pl.ds(slot * K0, K0), :] = jnp.concatenate(split(jnp.concatenate([re, im], axis=1)), axis=1)

    for slot in range(MINE):
        spectrum(0, slot, y_own)
        spectrum(1, slot, y_far)

    def triple(value, table):
        upper = coarse[table : table + 2].reshape(256, 256)
        lower = coarse[table + 2 : table + 4].reshape(256, 256)
        return dot(
            jnp.concatenate([value, value[:, :256]], axis=1), jnp.concatenate([upper, upper, lower], axis=0)
        )

    group = 4
    for step in range(MINE // group):
        rows = pl.ds(step * (group * K0), group * K0)
        left, right = triple(y_own[rows, :], own), triple(y_far[rows, :], far)
        a, b, c, d = left[:, :128], left[:, 128:], right[:, :128], right[:, 128:]
        spec = jnp.concatenate(split(jnp.concatenate([a * c - b * d, a * d + b * c], axis=1)), axis=1)
        lags = (triple(spec, ahead), triple(spec, behind))
        for member in range(group):
            tops, bottoms = [], []
            for part in lags:
                re, im = part[member * K0 : (member + 1) * K0, :128], part[member * K0 : (member + 1) * K0, 128:]
                tops.append(re * fine[2] - im * fine[3])
                bottoms.append(re * fine[3] + im * fine[2])
            upper, lower = split(
                jnp.concatenate([jnp.concatenate(tops, axis=1), jnp.concatenate(bottoms, axis=1)], axis=0)
            )
            both = dot(coarse[last : last + 2].reshape(256, 256), upper)
            result = both[:128] + both[128:] + dot(coarse[last], lower)
            slot = step * group + member
            flat[line(0, 0, slot), :] = result[:EDEV, :128]
            flat[line(0, 1, slot), :] = result[EDEV:, :128]
            flat[line(1, 0, slot), :] = -result[:EDEV, 128:]
            flat[line(1, 1, slot), :] = result[EDEV:, 128:]

    send[...] = flat[...].reshape(OWNERS, ROWS, 128).astype(BF16)


def one_hot(slot, begin, rows):
    order = lax.broadcasted_iota(jnp.int32, (rows, SLOTS), 0) + begin
    return jnp.where(order == slot, 1.0, 0.0).astype(BF16)


def kernel(
    less_hbm, greater_hbm, slot_hbm, coarse_hbm, fine_hbm,
    recv_two,
    less, greater, slot, wide, coarse, fine,
    hot, send_one, recv_one, send_two, flat, y_own, y_far,
    my_turn, left_far, left_near, sent, came, kept, fetched,
):
    e = lax.axis_index("energy")
    p = lax.axis_index("pair")
    core, z, x = lax.rem(e, 2), lax.rem(lax.div(e, 2), 16), lax.div(p, 2)
    side = lax.rem(p, 2)
    y = lax.div(e, 32) * 2 + side
    place = e * 2 + side
    owner = (1 - core) * EDEV + lax.div(e, 2) * 2 + side

    sources = (slot_hbm, less_hbm, greater_hbm, coarse_hbm, fine_hbm)
    places = (slot, less, greater, wide, fine)
    fetches = [pltpu.make_async_copy(a, b, fetched.at[i]) for i, (a, b) in enumerate(zip(sources, places))]
    for fetch in fetches:
        fetch.start()

    columns = []
    for dy in range(4):
        to_y = lax.rem(y + dy, 4)
        columns.append((lax.div(to_y, 2) * 16, lax.rem(to_y, 2)))

    def at_z(to_z, to_core, columns, act):
        for high, to_side in columns:
            chip = high + to_z
            act(
                chip * 2 + to_core,
                x * 2 + to_side,
                (chip * 2 + to_core) * 2 + to_side,
                (1 - to_core) * EDEV + chip * 2 + to_side,
            )

    def at(dz, to_core, columns, act):
        at_z(jnp.where(z + dz >= 16, z + dz - 16, z + dz), to_core, columns, act)

    def peers(cores, act, visit=at):
        def both_ways(near, carry):
            for to_core in cores:
                visit(7 - near, to_core, columns, act)
                visit(9 + near, to_core, columns, act)
            return carry

        for to_core in cores:
            visit(8, to_core, columns, act)
        lax.fori_loop(0, 7, both_ways, 0)
        for to_core in cores:
            visit(0, to_core, columns[1:], act)
            pl.when(core != to_core)(functools.partial(visit, 0, to_core, columns[:1], act))

    def far_peers(to_core, act):
        def both_ways(near, carry):
            at(7 - near, to_core, columns, act)
            at(9 + near, to_core, columns, act)
            return carry

        at(8, to_core, columns, act)
        lax.fori_loop(0, 4, both_ways, 0)

    def near_peers(to_core, act):
        def both_ways(near, carry):
            at(3 - near, to_core, columns, act)
            at(13 + near, to_core, columns, act)
            return carry

        lax.fori_loop(0, 3, both_ways, 0)
        at(0, to_core, columns[1:], act)
        pl.when(core != to_core)(functools.partial(at, 0, to_core, columns[:1], act))

    barrier = pltpu.get_barrier_semaphore()

    def greet(to_e, to_p, to_place, to_owner):
        pl.semaphore_signal(barrier, inc=1, device_id=(to_e, to_p), device_id_type=MESH)

    peers((1, 0), greet)
    fetches[0].wait()
    hot[...] = one_hot(slot[...], 0, SLOTS)

    def remote(src, dst, departure, arrival, to_e, to_p):
        pltpu.make_async_remote_copy(
            src_ref=src,
            dst_ref=dst,
            send_sem=departure,
            recv_sem=arrival,
            device_id=(to_e, to_p),
            device_id_type=MESH,
        ).start()

    def out(departure):
        return lambda to_e, to_p, to_place, to_owner: remote(
            send_one.at[to_owner], recv_one.at[place], departure, came.at[0], to_e, to_p
        )

    def back(to_e, to_p, to_place, to_owner):
        remote(send_two.at[to_place], recv_two.at[owner], sent, came.at[1], to_e, to_p)

    others = pl.ds(0, OWNERS - 1)

    def arrive(src, dst, target, turn):
        stay = pltpu.make_async_copy(src, dst, kept)
        stay.start()
        stay.wait()
        pltpu.make_async_copy(target.at[others], target.at[others], came.at[turn]).wait()

    fetches[1].wait()
    fetches[2].wait()
    value = jnp.concatenate([less[0], greater[0], less[1], greater[1]], axis=0)

    def permute(to_core):
        half = SLOTS // 2
        ordered = dot(hot[(1 - to_core) * half : (2 - to_core) * half, :], value, ((1,), (1,)))
        parts = [ordered[:, part * 128 : (part + 1) * 128].reshape(EDEV, MINE, 128) for part in range(2)]
        send_one[(1 - to_core) * EDEV : (2 - to_core) * EDEV] = jnp.concatenate(parts, axis=1).astype(BF16)

    def hand_over(to_core):
        far = pl.ds(0, 36)
        pltpu.make_async_copy(send_one.at[far], send_one.at[far], left_far.at[to_core]).wait()
        sibling = e + 1 - 2 * core
        pl.semaphore_signal(my_turn, inc=1, device_id=(sibling, p), device_id_type=MESH)

    def take_over():
        pl.semaphore_wait(my_turn, 1)

    permute(1)
    pl.semaphore_wait(barrier, OWNERS - 1)
    pl.when(core == 0)(take_over)
    far_peers(1, out(left_far.at[1]))
    near_peers(1, out(left_near.at[1]))
    permute(0)
    hand_over(1)
    take_over()
    far_peers(0, out(left_far.at[0]))
    near_peers(0, out(left_near.at[0]))
    pl.when(core == 1)(functools.partial(hand_over, 0))

    fetches[3].wait()
    fetches[4].wait()
    coarse[...] = wide[...].astype(BF16)
    arrive(send_one.at[owner], recv_one.at[place], recv_one, 0)
    correlate(recv_one, send_two, coarse, fine, flat, y_own, y_far)
    peers((1,), back)
    for to_z in range(EARLY_Z):
        at_z(to_z, 0, columns[1:], back)
        pl.when(jnp.logical_or(z != to_z, core != 0))(functools.partial(at_z, to_z, 0, columns[:1], back))

    def later(dz, to_core, columns, act):
        to_z = jnp.where(z + dz >= 16, z + dz - 16, z + dz)
        pl.when(to_z >= EARLY_Z)(functools.partial(at_z, to_z, to_core, columns, act))

    peers((0,), back, later)
    arrive(send_two.at[place], recv_two.at[owner], recv_two, 1)

    def drain(source, count, departure):
        some = source.at[pl.ds(0, count)]
        pltpu.make_async_copy(some, some, departure).wait()

    pl.when(core == 0)(functools.partial(drain, send_one, 36, left_far.at[0]))
    for to_core in (1, 0):
        pl.when(core == to_core)(functools.partial(drain, send_one, 27, left_near.at[to_core]))
        pl.when(core != to_core)(functools.partial(drain, send_one, 28, left_near.at[to_core]))
    drain(send_two, OWNERS - 1, sent)


def reorder(back_hbm, slot_hbm, less_hbm, greater_hbm, back, slot, less, greater, fetched, stored):
    fetches = [
        pltpu.make_async_copy(slot_hbm, slot, fetched.at[0]),
        pltpu.make_async_copy(back_hbm, back, fetched.at[1]),
    ]
    for fetch in fetches:
        fetch.start()
    fetches[0].wait()
    hot = one_hot(slot[...], 0, SLOTS)
    fetches[1].wait()
    value = back[...].astype(F32)
    ordered = jnp.concatenate(
        [value[:, part * MINE : (part + 1) * MINE].reshape(SLOTS, 128) for part in range(2)], axis=1
    )
    result = dot(ordered.astype(BF16), hot, ((0,), (0,))).astype(BF16)
    stores = []
    for part in range(2):
        for array, (kept, result_hbm) in enumerate(((less, less_hbm), (greater, greater_hbm))):
            kept[part] = result[(part * 2 + array) * N0 : (part * 2 + array + 1) * N0]
            stores.append(pltpu.make_async_copy(kept.at[part], result_hbm.at[part], stored.at[part, array]))
            stores[-1].start()
    for store in stores:
        store.wait()


def per_device(g_less, g_greater, pair_slot):
    coarse, fine = tables()
    hbm = pl.BlockSpec(memory_space=pltpu.HBM)
    grant = 60 * 1024 * 1024
    packets = pltpu.VMEM((OWNERS, ROWS, 128), BF16)
    back = pl.pallas_call(
        kernel,
        out_shape=jax.ShapeDtypeStruct((OWNERS, ROWS, 128), BF16),
        in_specs=[hbm] * 5,
        out_specs=hbm,
        scratch_shapes=[
            pltpu.VMEM((2, N0, SLOTS), BF16),
            pltpu.VMEM((2, N0, SLOTS), BF16),
            pltpu.VMEM((1, SLOTS), jnp.int32),
            pltpu.VMEM(coarse.shape, F32),
            pltpu.VMEM(coarse.shape, BF16),
            pltpu.VMEM(fine.shape, F32),
            pltpu.VMEM((SLOTS, SLOTS), BF16),
            packets,
            packets,
            packets,
            pltpu.VMEM((OWNERS * ROWS, 128), F32),
            pltpu.VMEM((MINE * K0, 512), BF16),
            pltpu.VMEM((MINE * K0, 512), BF16),
            pltpu.SemaphoreType.REGULAR,
            pltpu.SemaphoreType.DMA((2,)),
            pltpu.SemaphoreType.DMA((2,)),
            pltpu.SemaphoreType.DMA,
            pltpu.SemaphoreType.DMA((2,)),
            pltpu.SemaphoreType.DMA,
            pltpu.SemaphoreType.DMA((5,)),
        ],
        compiler_params=pltpu.CompilerParams(collective_id=0, has_side_effects=True, vmem_limit_bytes=grant),
        cost_estimate=pl.CostEstimate(flops=4 * 10**9, bytes_accessed=4 * 10**6, transcendentals=0),
    )(g_less, g_greater, pair_slot, jnp.asarray(coarse), jnp.asarray(fine))
    shape = jax.ShapeDtypeStruct((2, N0, SLOTS), BF16)
    return pl.pallas_call(
        reorder,
        out_shape=(shape, shape),
        in_specs=[hbm, hbm],
        out_specs=(hbm, hbm),
        scratch_shapes=[
            packets,
            pltpu.VMEM((1, SLOTS), jnp.int32),
            pltpu.VMEM(shape.shape, BF16),
            pltpu.VMEM(shape.shape, BF16),
            pltpu.SemaphoreType.DMA((2,)),
            pltpu.SemaphoreType.DMA((2, 2)),
        ],
        compiler_params=pltpu.CompilerParams(vmem_limit_bytes=grant),
        cost_estimate=pl.CostEstimate(flops=10**9, bytes_accessed=10**6, transcendentals=0),
    )(back, pair_slot)


def solution(mesh):
    placed = (P(None, "energy", "pair"), P(None, "energy", "pair"), P("pair", None))
    return jax.shard_map(
        per_device,
        mesh=mesh,
        in_specs=placed,
        out_specs=(P(None, "energy", "pair"), P(None, "energy", "pair")),
        check_vma=False,
    )
```

```python
import functools
import math

import jax
import jax.numpy as jnp
import ml_dtypes
import numpy as np
from jax import lax
from jax.experimental import pallas as pl
from jax.experimental.pallas import tpu as pltpu
from jax.sharding import PartitionSpec as P

NE = 4096
N0 = 64
EDEV = 64
OWNERS = 2 * EDEV
SLOTS = 1024
MINE = SLOTS // OWNERS
ROWS = 2 * MINE
EARLY_Z = 2
K0 = 128
K1 = 64
LENGTH = 2 * NE
F32 = jnp.float32
BF16 = jnp.bfloat16
MESH = pl.DeviceIdType.MESH


def upper_lower(table):
    upper = table.astype(ml_dtypes.bfloat16)
    lower = (table - upper.astype(np.float64)).astype(ml_dtypes.bfloat16)
    return upper, lower


def cos_sin(rows, cols, period):
    angle = (np.arange(rows)[:, None] * np.arange(cols)[None, :] % period) * (2.0 * math.pi / period)
    return np.cos(angle), np.sin(angle)


def tables():
    lanes = lambda *parts: np.concatenate(parts, axis=1)
    both = lambda table: np.concatenate(upper_lower(table))
    straight = lambda part: np.kron(np.eye(2), part)
    crossed = lambda part: np.kron(np.eye(2)[::-1], part)
    c, s = cos_sin(K0, EDEV, K0)
    first = [lanes(*upper_lower(lanes(c, s))), lanes(*upper_lower(lanes(c, -s)))]
    c, s = cos_sin(N0, K1, K1)
    own = both(np.block([[straight(c), -straight(s)], [straight(s), straight(c)]]))
    far = both(np.block([[crossed(c), crossed(s)], [-crossed(s), crossed(c)]]))
    ahead = both(np.block([[straight(c), straight(s)], [-straight(s), straight(c)]]))
    behind = both(np.block([[crossed(c), crossed(s)], [crossed(s), -crossed(c)]]))
    c, s = cos_sin(EDEV, K0, K0)
    last = both(np.block([[c, -s], [s, c]]))
    coarse = np.concatenate(first + [own, far, ahead, behind, last])
    c, s = cos_sin(K0, N0, LENGTH)
    scale = 1.0 / (math.sqrt(NE) * LENGTH)
    fine = np.stack([lanes(c, c), lanes(s, s), lanes(s, s) * scale, -lanes(c, c) * scale])
    return coarse.reshape(-1, 128, 256).astype(np.float32), fine.astype(np.float32)


def dot(left, right, dims=((1,), (0,))):
    return lax.dot_general(left, right, (dims, ((), ())), preferred_element_type=F32)


def split(value):
    upper = value.astype(BF16)
    return upper, (value - upper.astype(F32)).astype(BF16)


def correlate(recv, send, coarse, fine, flat, y_own, y_far):
    first, own, far, ahead, behind, last = 0, 2, 6, 10, 14, 18
    flat[...] = recv[...].astype(F32).reshape(OWNERS * ROWS, 128)

    def line(side, part, slot):
        return pl.ds(side * ROWS + part * MINE + slot, EDEV, stride=2 * ROWS)

    def spectrum(side, slot, into):
        re, im = flat[line(side, 0, slot), :], flat[line(side, 1, slot), :]
        top = jnp.concatenate([re, im], axis=1).astype(BF16)
        bottom = jnp.concatenate([im, -re], axis=1).astype(BF16)
        step = dot(coarse[first + side], jnp.concatenate([top, bottom, top, bottom], axis=0))
        re, im = step[:, :128], step[:, 128:]
        c, s = fine[0], fine[1]
        if side == 0:
            re, im = re * c + im * s, im * c - re * s
        else:
            re, im = re * c - im * s, im * c + re * s
        into[pl.ds(slot * K0, K0), :] = jnp.concatenate(split(jnp.concatenate([re, im], axis=1)), axis=1)

    for slot in range(MINE):
        spectrum(0, slot, y_own)
        spectrum(1, slot, y_far)

    def triple(value, table):
        upper = coarse[table : table + 2].reshape(256, 256)
        lower = coarse[table + 2 : table + 4].reshape(256, 256)
        return dot(
            jnp.concatenate([value, value[:, :256]], axis=1), jnp.concatenate([upper, upper, lower], axis=0)
        )

    group = 4
    for step in range(MINE // group):
        rows = pl.ds(step * (group * K0), group * K0)
        left, right = triple(y_own[rows, :], own), triple(y_far[rows, :], far)
        a, b, c, d = left[:, :128], left[:, 128:], right[:, :128], right[:, 128:]
        spec = jnp.concatenate(split(jnp.concatenate([a * c - b * d, a * d + b * c], axis=1)), axis=1)
        lags = (triple(spec, ahead), triple(spec, behind))
        for member in range(group):
            tops, bottoms = [], []
            for part in lags:
                re, im = part[member * K0 : (member + 1) * K0, :128], part[member * K0 : (member + 1) * K0, 128:]
                tops.append(re * fine[2] - im * fine[3])
                bottoms.append(re * fine[3] + im * fine[2])
            upper, lower = split(
                jnp.concatenate([jnp.concatenate(tops, axis=1), jnp.concatenate(bottoms, axis=1)], axis=0)
            )
            both = dot(coarse[last : last + 2].reshape(256, 256), upper)
            result = both[:128] + both[128:] + dot(coarse[last], lower)
            slot = step * group + member
            flat[line(0, 0, slot), :] = result[:EDEV, :128]
            flat[line(0, 1, slot), :] = result[EDEV:, :128]
            flat[line(1, 0, slot), :] = -result[:EDEV, 128:]
            flat[line(1, 1, slot), :] = result[EDEV:, 128:]

    send[...] = flat[...].reshape(OWNERS, ROWS, 128).astype(BF16)


def one_hot(slot, begin, rows):
    order = lax.broadcasted_iota(jnp.int32, (rows, SLOTS), 0) + begin
    return jnp.where(order == slot, 1.0, 0.0).astype(BF16)


def kernel(
    less_hbm, greater_hbm, slot_hbm, coarse_hbm, fine_hbm,
    recv_two,
    less, greater, slot, wide, coarse, fine,
    hot, send_one, recv_one, send_two, flat, y_own, y_far,
    sent, came, kept, fetched,
):
    e = lax.axis_index("energy")
    p = lax.axis_index("pair")
    core, z, x = lax.rem(e, 2), lax.rem(lax.div(e, 2), 16), lax.div(p, 2)
    side = lax.rem(p, 2)
    y = lax.div(e, 32) * 2 + side
    place = e * 2 + side
    owner = (1 - core) * EDEV + lax.div(e, 2) * 2 + side

    columns = []
    for dy in range(4):
        to_y = lax.rem(y + dy, 4)
        columns.append((lax.div(to_y, 2) * 16, lax.rem(to_y, 2)))

    def at_z(to_z, to_core, columns, act):
        for high, to_side in columns:
            chip = high + to_z
            act(
                chip * 2 + to_core,
                x * 2 + to_side,
                (chip * 2 + to_core) * 2 + to_side,
                (1 - to_core) * EDEV + chip * 2 + to_side,
            )

    def at(dz, to_core, columns, act):
        at_z(jnp.where(z + dz >= 16, z + dz - 16, z + dz), to_core, columns, act)

    def peers(cores, act, visit=at):
        def both_ways(near, carry):
            for to_core in cores:
                visit(7 - near, to_core, columns, act)
                visit(9 + near, to_core, columns, act)
            return carry

        for to_core in cores:
            visit(8, to_core, columns, act)
        lax.fori_loop(0, 7, both_ways, 0)
        for to_core in cores:
            visit(0, to_core, columns[1:], act)
            pl.when(core != to_core)(functools.partial(visit, 0, to_core, columns[:1], act))

    def some_peers(to_core, odd, act):
        even = 1 - lax.rem(odd + z, 2)

        def both_ways(near, carry):
            at(7 + even - 2 * near, to_core, columns, act)
            at(9 + even + 2 * near, to_core, columns, act)
            return carry

        lax.fori_loop(0, 3, both_ways, 0)
        at(1 + even, to_core, columns, act)
        at(15 + even, to_core, columns[1:], act)
        pl.when(jnp.logical_or(even == 0, core != to_core))(
            functools.partial(at, 15 + even, to_core, columns[:1], act)
        )

    barrier = pltpu.get_barrier_semaphore()

    def greet(to_e, to_p, to_place, to_owner):
        pl.semaphore_signal(barrier, inc=1, device_id=(to_e, to_p), device_id_type=MESH)

    peers((1, 0), greet)

    sources = (slot_hbm, less_hbm, greater_hbm, coarse_hbm, fine_hbm)
    places = (slot, less, greater, wide, fine)
    fetches = [pltpu.make_async_copy(a, b, fetched.at[i]) for i, (a, b) in enumerate(zip(sources, places))]
    for fetch in fetches:
        fetch.start()
    fetches[0].wait()
    hot[...] = one_hot(slot[...], 0, SLOTS)

    def remote(src, dst, turn, to_e, to_p):
        pltpu.make_async_remote_copy(
            src_ref=src,
            dst_ref=dst,
            send_sem=sent.at[turn],
            recv_sem=came.at[turn],
            device_id=(to_e, to_p),
            device_id_type=MESH,
        ).start()

    def out(to_e, to_p, to_place, to_owner):
        remote(send_one.at[to_owner], recv_one.at[place], 0, to_e, to_p)

    def back(to_e, to_p, to_place, to_owner):
        remote(send_two.at[to_place], recv_two.at[owner], 1, to_e, to_p)

    others = pl.ds(0, OWNERS - 1)

    def arrive(src, dst, target, turn):
        stay = pltpu.make_async_copy(src, dst, kept)
        stay.start()
        stay.wait()
        pltpu.make_async_copy(target.at[others], target.at[others], came.at[turn]).wait()

    fetches[1].wait()
    fetches[2].wait()
    value = jnp.concatenate([less[0], greater[0], less[1], greater[1]], axis=0)
    for to_core in (1, 0):
        half = SLOTS // 2
        ordered = dot(hot[(1 - to_core) * half : (2 - to_core) * half, :], value, ((1,), (1,)))
        parts = [ordered[:, part * 128 : (part + 1) * 128].reshape(EDEV, MINE, 128) for part in range(2)]
        send_one[(1 - to_core) * EDEV : (2 - to_core) * EDEV] = jnp.concatenate(parts, axis=1).astype(BF16)
        if to_core == 1:
            pl.semaphore_wait(barrier, OWNERS - 1)
        for odd in (1, 0):
            some_peers(to_core, odd, out)

    fetches[3].wait()
    fetches[4].wait()
    coarse[...] = wide[...].astype(BF16)
    arrive(send_one.at[owner], recv_one.at[place], recv_one, 0)
    correlate(recv_one, send_two, coarse, fine, flat, y_own, y_far)
    peers((1,), back)
    for to_z in range(EARLY_Z):
        at_z(to_z, 0, columns[1:], back)
        pl.when(jnp.logical_or(z != to_z, core != 0))(functools.partial(at_z, to_z, 0, columns[:1], back))

    def later(dz, to_core, columns, act):
        to_z = jnp.where(z + dz >= 16, z + dz - 16, z + dz)
        pl.when(to_z >= EARLY_Z)(functools.partial(at_z, to_z, to_core, columns, act))

    peers((0,), back, later)
    arrive(send_two.at[place], recv_two.at[owner], recv_two, 1)

    for turn, source in enumerate((send_one, send_two)):
        pltpu.make_async_copy(source.at[others], source.at[others], sent.at[turn]).wait()


def reorder(back_hbm, slot_hbm, less_hbm, greater_hbm, back, slot, less, greater, fetched, stored):
    fetches = [
        pltpu.make_async_copy(slot_hbm, slot, fetched.at[0]),
        pltpu.make_async_copy(back_hbm, back, fetched.at[1]),
    ]
    for fetch in fetches:
        fetch.start()
    fetches[0].wait()
    half = SLOTS // 2
    hot = one_hot(slot[...], 0, half)
    fetches[1].wait()
    result = None
    for part in range(2):
        value = back[part * EDEV : (part + 1) * EDEV].astype(F32)
        ordered = jnp.concatenate([value[:, :MINE].reshape(half, 128), value[:, MINE:].reshape(half, 128)], axis=1)
        term = dot(ordered.astype(BF16), hot, ((0,), (0,)))
        if part == 0:
            hot = one_hot(slot[...], half, half)
            result = term
        else:
            result = (result + term).astype(BF16)
    stores = []
    for part in range(2):
        for array, (kept, result_hbm) in enumerate(((less, less_hbm), (greater, greater_hbm))):
            kept[part] = result[(part * 2 + array) * N0 : (part * 2 + array + 1) * N0]
            stores.append(pltpu.make_async_copy(kept.at[part], result_hbm.at[part], stored.at[part, array]))
            stores[-1].start()
    for store in stores:
        store.wait()


def per_device(g_less, g_greater, pair_slot):
    coarse, fine = tables()
    hbm = pl.BlockSpec(memory_space=pltpu.HBM)
    grant = 60 * 1024 * 1024
    packets = pltpu.VMEM((OWNERS, ROWS, 128), BF16)
    back = pl.pallas_call(
        kernel,
        out_shape=jax.ShapeDtypeStruct((OWNERS, ROWS, 128), BF16),
        in_specs=[hbm] * 5,
        out_specs=hbm,
        scratch_shapes=[
            pltpu.VMEM((2, N0, SLOTS), BF16),
            pltpu.VMEM((2, N0, SLOTS), BF16),
            pltpu.VMEM((1, SLOTS), jnp.int32),
            pltpu.VMEM(coarse.shape, F32),
            pltpu.VMEM(coarse.shape, BF16),
            pltpu.VMEM(fine.shape, F32),
            pltpu.VMEM((SLOTS, SLOTS), BF16),
            packets,
            packets,
            packets,
            pltpu.VMEM((OWNERS * ROWS, 128), F32),
            pltpu.VMEM((MINE * K0, 512), BF16),
            pltpu.VMEM((MINE * K0, 512), BF16),
            pltpu.SemaphoreType.DMA((2,)),
            pltpu.SemaphoreType.DMA((2,)),
            pltpu.SemaphoreType.DMA,
            pltpu.SemaphoreType.DMA((5,)),
        ],
        compiler_params=pltpu.CompilerParams(collective_id=0, has_side_effects=True, vmem_limit_bytes=grant),
        cost_estimate=pl.CostEstimate(flops=4 * 10**9, bytes_accessed=4 * 10**6, transcendentals=0),
    )(g_less, g_greater, pair_slot, jnp.asarray(coarse), jnp.asarray(fine))
    shape = jax.ShapeDtypeStruct((2, N0, SLOTS), BF16)
    return pl.pallas_call(
        reorder,
        out_shape=(shape, shape),
        in_specs=[hbm, hbm],
        out_specs=(hbm, hbm),
        scratch_shapes=[
            packets,
            pltpu.VMEM((1, SLOTS), jnp.int32),
            pltpu.VMEM(shape.shape, BF16),
            pltpu.VMEM(shape.shape, BF16),
            pltpu.SemaphoreType.DMA((2,)),
            pltpu.SemaphoreType.DMA((2, 2)),
        ],
        compiler_params=pltpu.CompilerParams(vmem_limit_bytes=grant),
        cost_estimate=pl.CostEstimate(flops=10**9, bytes_accessed=10**6, transcendentals=0),
    )(back, pair_slot)


def solution(mesh):
    placed = (P(None, "energy", "pair"), P(None, "energy", "pair"), P("pair", None))
    return jax.shard_map(
        per_device,
        mesh=mesh,
        in_specs=placed,
        out_specs=(P(None, "energy", "pair"), P(None, "energy", "pair")),
        check_vma=False,
    )
```

```python
import functools
import math

import jax
import jax.numpy as jnp
import ml_dtypes
import numpy as np
from jax import lax
from jax.experimental import pallas as pl
from jax.experimental.pallas import tpu as pltpu
from jax.sharding import PartitionSpec as P

NE = 4096
N0 = 64
EDEV = 64
OWNERS = 2 * EDEV
SLOTS = 1024
MINE = SLOTS // OWNERS
ROWS = 2 * MINE
EARLY_Z = 4
K0 = 128
K1 = 64
LENGTH = 2 * NE
F32 = jnp.float32
BF16 = jnp.bfloat16
MESH = pl.DeviceIdType.MESH


def upper_lower(table):
    upper = table.astype(ml_dtypes.bfloat16)
    lower = (table - upper.astype(np.float64)).astype(ml_dtypes.bfloat16)
    return upper, lower


def cos_sin(rows, cols, period):
    angle = (np.arange(rows)[:, None] * np.arange(cols)[None, :] % period) * (2.0 * math.pi / period)
    return np.cos(angle), np.sin(angle)


def tables():
    lanes = lambda *parts: np.concatenate(parts, axis=1)
    both = lambda table: np.concatenate(upper_lower(table))
    straight = lambda part: np.kron(np.eye(2), part)
    crossed = lambda part: np.kron(np.eye(2)[::-1], part)
    c, s = cos_sin(K0, EDEV, K0)
    first = [lanes(*upper_lower(lanes(c, s))), lanes(*upper_lower(lanes(c, -s)))]
    c, s = cos_sin(N0, K1, K1)
    own = both(np.block([[straight(c), -straight(s)], [straight(s), straight(c)]]))
    far = both(np.block([[crossed(c), crossed(s)], [-crossed(s), crossed(c)]]))
    ahead = both(np.block([[straight(c), straight(s)], [-straight(s), straight(c)]]))
    behind = both(np.block([[crossed(c), crossed(s)], [crossed(s), -crossed(c)]]))
    c, s = cos_sin(EDEV, K0, K0)
    last = both(np.block([[c, -s], [s, c]]))
    coarse = np.concatenate(first + [own, far, ahead, behind, last])
    c, s = cos_sin(K0, N0, LENGTH)
    scale = 1.0 / (math.sqrt(NE) * LENGTH)
    fine = np.stack([lanes(c, c), lanes(s, s), lanes(s, s) * scale, -lanes(c, c) * scale])
    return coarse.reshape(-1, 128, 256).astype(np.float32), fine.astype(np.float32)


def dot(left, right, dims=((1,), (0,))):
    return lax.dot_general(left, right, (dims, ((), ())), preferred_element_type=F32)


def split(value):
    upper = value.astype(BF16)
    return upper, (value - upper.astype(F32)).astype(BF16)


def correlate(recv, send, coarse, fine, flat, y_own, y_far):
    first, own, far, ahead, behind, last = 0, 2, 6, 10, 14, 18
    flat[...] = recv[...].astype(F32).reshape(OWNERS * ROWS, 128)

    def line(side, part, slot):
        return pl.ds(side * ROWS + part * MINE + slot, EDEV, stride=2 * ROWS)

    def spectrum(side, slot, into):
        re, im = flat[line(side, 0, slot), :], flat[line(side, 1, slot), :]
        top = jnp.concatenate([re, im], axis=1).astype(BF16)
        bottom = jnp.concatenate([im, -re], axis=1).astype(BF16)
        step = dot(coarse[first + side], jnp.concatenate([top, bottom, top, bottom], axis=0))
        re, im = step[:, :128], step[:, 128:]
        c, s = fine[0], fine[1]
        if side == 0:
            re, im = re * c + im * s, im * c - re * s
        else:
            re, im = re * c - im * s, im * c + re * s
        into[pl.ds(slot * K0, K0), :] = jnp.concatenate(split(jnp.concatenate([re, im], axis=1)), axis=1)

    for slot in range(MINE):
        spectrum(0, slot, y_own)
        spectrum(1, slot, y_far)

    def triple(value, table):
        upper = coarse[table : table + 2].reshape(256, 256)
        lower = coarse[table + 2 : table + 4].reshape(256, 256)
        return dot(
            jnp.concatenate([value, value[:, :256]], axis=1), jnp.concatenate([upper, upper, lower], axis=0)
        )

    group = 4
    for step in range(MINE // group):
        rows = pl.ds(step * (group * K0), group * K0)
        left, right = triple(y_own[rows, :], own), triple(y_far[rows, :], far)
        a, b, c, d = left[:, :128], left[:, 128:], right[:, :128], right[:, 128:]
        spec = jnp.concatenate(split(jnp.concatenate([a * c - b * d, a * d + b * c], axis=1)), axis=1)
        lags = (triple(spec, ahead), triple(spec, behind))
        for member in range(group):
            tops, bottoms = [], []
            for part in lags:
                re, im = part[member * K0 : (member + 1) * K0, :128], part[member * K0 : (member + 1) * K0, 128:]
                tops.append(re * fine[2] - im * fine[3])
                bottoms.append(re * fine[3] + im * fine[2])
            upper, lower = split(
                jnp.concatenate([jnp.concatenate(tops, axis=1), jnp.concatenate(bottoms, axis=1)], axis=0)
            )
            both = dot(coarse[last : last + 2].reshape(256, 256), upper)
            result = both[:128] + both[128:] + dot(coarse[last], lower)
            slot = step * group + member
            flat[line(0, 0, slot), :] = result[:EDEV, :128]
            flat[line(0, 1, slot), :] = result[EDEV:, :128]
            flat[line(1, 0, slot), :] = -result[:EDEV, 128:]
            flat[line(1, 1, slot), :] = result[EDEV:, 128:]

    send[...] = flat[...].reshape(OWNERS, ROWS, 128).astype(BF16)


def one_hot(slot, begin, rows):
    order = lax.broadcasted_iota(jnp.int32, (rows, SLOTS), 0) + begin
    return jnp.where(order == slot, 1.0, 0.0).astype(BF16)


def kernel(
    less_hbm, greater_hbm, slot_hbm, coarse_hbm, fine_hbm,
    recv_two,
    less, greater, slot, wide, coarse, fine,
    hot, send_one, recv_one, send_two, flat, y_own, y_far,
    sent, came, kept, fetched,
):
    e = lax.axis_index("energy")
    p = lax.axis_index("pair")
    core, z, x = lax.rem(e, 2), lax.rem(lax.div(e, 2), 16), lax.div(p, 2)
    side = lax.rem(p, 2)
    y = lax.div(e, 32) * 2 + side
    place = e * 2 + side
    owner = (1 - core) * EDEV + lax.div(e, 2) * 2 + side

    columns = []
    for dy in range(4):
        to_y = lax.rem(y + dy, 4)
        columns.append((lax.div(to_y, 2) * 16, lax.rem(to_y, 2)))

    def at_z(to_z, to_core, columns, act):
        for high, to_side in columns:
            chip = high + to_z
            act(
                chip * 2 + to_core,
                x * 2 + to_side,
                (chip * 2 + to_core) * 2 + to_side,
                (1 - to_core) * EDEV + chip * 2 + to_side,
            )

    def at(dz, to_core, columns, act):
        at_z(jnp.where(z + dz >= 16, z + dz - 16, z + dz), to_core, columns, act)

    def peers(cores, act, visit=at):
        def both_ways(near, carry):
            for to_core in cores:
                visit(7 - near, to_core, columns, act)
                visit(9 + near, to_core, columns, act)
            return carry

        for to_core in cores:
            visit(8, to_core, columns, act)
        lax.fori_loop(0, 7, both_ways, 0)
        for to_core in cores:
            visit(0, to_core, columns[1:], act)
            pl.when(core != to_core)(functools.partial(visit, 0, to_core, columns[:1], act))

    def some_peers(to_core, odd, act):
        even = 1 - lax.rem(odd + z, 2)

        def both_ways(near, carry):
            at(7 + even - 2 * near, to_core, columns, act)
            at(9 + even + 2 * near, to_core, columns, act)
            return carry

        lax.fori_loop(0, 3, both_ways, 0)
        at(1 + even, to_core, columns, act)
        at(15 + even, to_core, columns[1:], act)
        pl.when(jnp.logical_or(even == 0, core != to_core))(
            functools.partial(at, 15 + even, to_core, columns[:1], act)
        )

    barrier = pltpu.get_barrier_semaphore()

    def greet(to_e, to_p, to_place, to_owner):
        pl.semaphore_signal(barrier, inc=1, device_id=(to_e, to_p), device_id_type=MESH)

    peers((1, 0), greet)

    sources = (slot_hbm, less_hbm, greater_hbm, coarse_hbm, fine_hbm)
    places = (slot, less, greater, wide, fine)
    fetches = [pltpu.make_async_copy(a, b, fetched.at[i]) for i, (a, b) in enumerate(zip(sources, places))]
    for fetch in fetches:
        fetch.start()
    fetches[0].wait()
    hot[...] = one_hot(slot[...], 0, SLOTS)

    def remote(src, dst, turn, to_e, to_p):
        pltpu.make_async_remote_copy(
            src_ref=src,
            dst_ref=dst,
            send_sem=sent.at[turn],
            recv_sem=came.at[turn],
            device_id=(to_e, to_p),
            device_id_type=MESH,
        ).start()

    def out(to_e, to_p, to_place, to_owner):
        remote(send_one.at[to_owner], recv_one.at[place], 0, to_e, to_p)

    def back(to_e, to_p, to_place, to_owner):
        remote(send_two.at[to_place], recv_two.at[owner], 1, to_e, to_p)

    others = pl.ds(0, OWNERS - 1)

    def arrive(src, dst, target, turn):
        stay = pltpu.make_async_copy(src, dst, kept)
        stay.start()
        stay.wait()
        pltpu.make_async_copy(target.at[others], target.at[others], came.at[turn]).wait()

    fetches[1].wait()
    fetches[2].wait()
    value = jnp.concatenate([less[0], greater[0], less[1], greater[1]], axis=0)
    for to_core in (1, 0):
        half = SLOTS // 2
        ordered = dot(hot[(1 - to_core) * half : (2 - to_core) * half, :], value, ((1,), (1,)))
        parts = [ordered[:, part * 128 : (part + 1) * 128].reshape(EDEV, MINE, 128) for part in range(2)]
        send_one[(1 - to_core) * EDEV : (2 - to_core) * EDEV] = jnp.concatenate(parts, axis=1).astype(BF16)
        if to_core == 1:
            pl.semaphore_wait(barrier, OWNERS - 1)
        for odd in (1, 0):
            some_peers(to_core, odd, out)

    fetches[3].wait()
    fetches[4].wait()
    coarse[...] = wide[...].astype(BF16)
    arrive(send_one.at[owner], recv_one.at[place], recv_one, 0)
    correlate(recv_one, send_two, coarse, fine, flat, y_own, y_far)
    def lowest(dz, to_core, columns, act):
        to_z = jnp.where(z + dz >= 16, z + dz - 16, z + dz)
        pl.when(to_z < EARLY_Z)(functools.partial(at_z, to_z, to_core, columns, act))

    def rest(dz, to_core, columns, act):
        to_z = jnp.where(z + dz >= 16, z + dz - 16, z + dz)
        pl.when(to_z >= EARLY_Z)(functools.partial(at_z, to_z, to_core, columns, act))

    peers((1,), back)
    peers((0,), back, lowest)
    peers((0,), back, rest)
    arrive(send_two.at[place], recv_two.at[owner], recv_two, 1)

    for turn, source in enumerate((send_one, send_two)):
        pltpu.make_async_copy(source.at[others], source.at[others], sent.at[turn]).wait()


def reorder(back_hbm, slot_hbm, less_hbm, greater_hbm, back, slot, less, greater, fetched, stored):
    fetches = [
        pltpu.make_async_copy(slot_hbm, slot, fetched.at[0]),
        pltpu.make_async_copy(back_hbm, back, fetched.at[1]),
    ]
    for fetch in fetches:
        fetch.start()
    fetches[0].wait()
    half = SLOTS // 2
    hot = one_hot(slot[...], 0, half)
    fetches[1].wait()
    result = None
    for part in range(2):
        value = back[part * EDEV : (part + 1) * EDEV].astype(F32)
        ordered = jnp.concatenate([value[:, :MINE].reshape(half, 128), value[:, MINE:].reshape(half, 128)], axis=1)
        term = dot(ordered.astype(BF16), hot, ((0,), (0,)))
        if part == 0:
            hot = one_hot(slot[...], half, half)
            result = term
        else:
            result = (result + term).astype(BF16)
    stores = []
    for part in range(2):
        for array, (kept, result_hbm) in enumerate(((less, less_hbm), (greater, greater_hbm))):
            kept[part] = result[(part * 2 + array) * N0 : (part * 2 + array + 1) * N0]
            stores.append(pltpu.make_async_copy(kept.at[part], result_hbm.at[part], stored.at[part, array]))
            stores[-1].start()
    for store in stores:
        store.wait()


def per_device(g_less, g_greater, pair_slot):
    coarse, fine = tables()
    hbm = pl.BlockSpec(memory_space=pltpu.HBM)
    grant = 60 * 1024 * 1024
    packets = pltpu.VMEM((OWNERS, ROWS, 128), BF16)
    back = pl.pallas_call(
        kernel,
        out_shape=jax.ShapeDtypeStruct((OWNERS, ROWS, 128), BF16),
        in_specs=[hbm] * 5,
        out_specs=hbm,
        scratch_shapes=[
            pltpu.VMEM((2, N0, SLOTS), BF16),
            pltpu.VMEM((2, N0, SLOTS), BF16),
            pltpu.VMEM((1, SLOTS), jnp.int32),
            pltpu.VMEM(coarse.shape, F32),
            pltpu.VMEM(coarse.shape, BF16),
            pltpu.VMEM(fine.shape, F32),
            pltpu.VMEM((SLOTS, SLOTS), BF16),
            packets,
            packets,
            packets,
            pltpu.VMEM((OWNERS * ROWS, 128), F32),
            pltpu.VMEM((MINE * K0, 512), BF16),
            pltpu.VMEM((MINE * K0, 512), BF16),
            pltpu.SemaphoreType.DMA((2,)),
            pltpu.SemaphoreType.DMA((2,)),
            pltpu.SemaphoreType.DMA,
            pltpu.SemaphoreType.DMA((5,)),
        ],
        compiler_params=pltpu.CompilerParams(collective_id=0, has_side_effects=True, vmem_limit_bytes=grant),
        cost_estimate=pl.CostEstimate(flops=4 * 10**9, bytes_accessed=4 * 10**6, transcendentals=0),
    )(g_less, g_greater, pair_slot, jnp.asarray(coarse), jnp.asarray(fine))
    shape = jax.ShapeDtypeStruct((2, N0, SLOTS), BF16)
    return pl.pallas_call(
        reorder,
        out_shape=(shape, shape),
        in_specs=[hbm, hbm],
        out_specs=(hbm, hbm),
        scratch_shapes=[
            packets,
            pltpu.VMEM((1, SLOTS), jnp.int32),
            pltpu.VMEM(shape.shape, BF16),
            pltpu.VMEM(shape.shape, BF16),
            pltpu.SemaphoreType.DMA((2,)),
            pltpu.SemaphoreType.DMA((2, 2)),
        ],
        compiler_params=pltpu.CompilerParams(vmem_limit_bytes=grant),
        cost_estimate=pl.CostEstimate(flops=10**9, bytes_accessed=10**6, transcendentals=0),
    )(back, pair_slot)


def solution(mesh):
    placed = (P(None, "energy", "pair"), P(None, "energy", "pair"), P("pair", None))
    return jax.shard_map(
        per_device,
        mesh=mesh,
        in_specs=placed,
        out_specs=(P(None, "energy", "pair"), P(None, "energy", "pair")),
        check_vma=False,
    )
```

```python
import functools
import math

import jax
import jax.numpy as jnp
import ml_dtypes
import numpy as np
from jax import lax
from jax.experimental import pallas as pl
from jax.experimental.pallas import tpu as pltpu
from jax.sharding import PartitionSpec as P

NE = 4096
N0 = 64
EDEV = 64
OWNERS = 2 * EDEV
SLOTS = 1024
MINE = SLOTS // OWNERS
ROWS = 2 * MINE
EARLY_Z = 2
K0 = 128
K1 = 64
LENGTH = 2 * NE
F32 = jnp.float32
BF16 = jnp.bfloat16
MESH = pl.DeviceIdType.MESH


def upper_lower(table):
    upper = table.astype(ml_dtypes.bfloat16)
    lower = (table - upper.astype(np.float64)).astype(ml_dtypes.bfloat16)
    return upper, lower


def cos_sin(rows, cols, period):
    angle = (np.arange(rows)[:, None] * np.arange(cols)[None, :] % period) * (2.0 * math.pi / period)
    return np.cos(angle), np.sin(angle)


def tables():
    lanes = lambda *parts: np.concatenate(parts, axis=1)
    both = lambda table: np.concatenate(upper_lower(table))
    straight = lambda part: np.kron(np.eye(2), part)
    crossed = lambda part: np.kron(np.eye(2)[::-1], part)
    c, s = cos_sin(K0, EDEV, K0)
    first = [lanes(*upper_lower(lanes(c, s))), lanes(*upper_lower(lanes(c, -s)))]
    c, s = cos_sin(N0, K1, K1)
    own = both(np.block([[straight(c), -straight(s)], [straight(s), straight(c)]]))
    far = both(np.block([[crossed(c), crossed(s)], [-crossed(s), crossed(c)]]))
    ahead = both(np.block([[straight(c), straight(s)], [-straight(s), straight(c)]]))
    behind = both(np.block([[crossed(c), crossed(s)], [crossed(s), -crossed(c)]]))
    c, s = cos_sin(EDEV, K0, K0)
    last = both(np.block([[c, -s], [s, c]]))
    coarse = np.concatenate(first + [own, far, ahead, behind, last])
    c, s = cos_sin(K0, N0, LENGTH)
    scale = 1.0 / (math.sqrt(NE) * LENGTH)
    fine = np.stack([lanes(c, c), lanes(s, s), lanes(s, s) * scale, -lanes(c, c) * scale])
    return coarse.reshape(-1, 128, 256).astype(np.float32), fine.astype(np.float32)


def dot(left, right, dims=((1,), (0,))):
    return lax.dot_general(left, right, (dims, ((), ())), preferred_element_type=F32)


def split(value):
    upper = value.astype(BF16)
    return upper, (value - upper.astype(F32)).astype(BF16)


def correlate(recv, send, coarse, fine, flat, y_own, y_far):
    first, own, far, ahead, behind, last = 0, 2, 6, 10, 14, 18
    flat[...] = recv[...].astype(F32).reshape(OWNERS * ROWS, 128)

    def line(side, part, slot):
        return pl.ds(side * ROWS + part * MINE + slot, EDEV, stride=2 * ROWS)

    def spectrum(side, slot, into):
        re, im = flat[line(side, 0, slot), :], flat[line(side, 1, slot), :]
        top = jnp.concatenate([re, im], axis=1).astype(BF16)
        bottom = jnp.concatenate([im, -re], axis=1).astype(BF16)
        step = dot(coarse[first + side], jnp.concatenate([top, bottom, top, bottom], axis=0))
        re, im = step[:, :128], step[:, 128:]
        c, s = fine[0], fine[1]
        if side == 0:
            re, im = re * c + im * s, im * c - re * s
        else:
            re, im = re * c - im * s, im * c + re * s
        into[pl.ds(slot * K0, K0), :] = jnp.concatenate(split(jnp.concatenate([re, im], axis=1)), axis=1)

    for slot in range(MINE):
        spectrum(0, slot, y_own)
        spectrum(1, slot, y_far)

    def triple(value, table):
        upper = coarse[table : table + 2].reshape(256, 256)
        lower = coarse[table + 2 : table + 4].reshape(256, 256)
        return dot(
            jnp.concatenate([value, value[:, :256]], axis=1), jnp.concatenate([upper, upper, lower], axis=0)
        )

    group = MINE
    for step in range(MINE // group):
        rows = pl.ds(step * (group * K0), group * K0)
        left, right = triple(y_own[rows, :], own), triple(y_far[rows, :], far)
        a, b, c, d = left[:, :128], left[:, 128:], right[:, :128], right[:, 128:]
        spec = jnp.concatenate(split(jnp.concatenate([a * c - b * d, a * d + b * c], axis=1)), axis=1)
        lags = (triple(spec, ahead), triple(spec, behind))
        for member in range(group):
            tops, bottoms = [], []
            for part in lags:
                re, im = part[member * K0 : (member + 1) * K0, :128], part[member * K0 : (member + 1) * K0, 128:]
                tops.append(re * fine[2] - im * fine[3])
                bottoms.append(re * fine[3] + im * fine[2])
            upper, lower = split(
                jnp.concatenate([jnp.concatenate(tops, axis=1), jnp.concatenate(bottoms, axis=1)], axis=0)
            )
            both = dot(coarse[last : last + 2].reshape(256, 256), upper)
            result = both[:128] + both[128:] + dot(coarse[last], lower)
            slot = step * group + member
            flat[line(0, 0, slot), :] = result[:EDEV, :128]
            flat[line(0, 1, slot), :] = result[EDEV:, :128]
            flat[line(1, 0, slot), :] = -result[:EDEV, 128:]
            flat[line(1, 1, slot), :] = result[EDEV:, 128:]

    send[...] = flat[...].reshape(OWNERS, ROWS, 128).astype(BF16)


def one_hot(slot, begin, rows):
    order = lax.broadcasted_iota(jnp.int32, (rows, SLOTS), 0) + begin
    return jnp.where(order == slot, 1.0, 0.0).astype(BF16)


def kernel(
    less_hbm, greater_hbm, slot_hbm, coarse_hbm, fine_hbm,
    recv_two,
    less, greater, slot, wide, coarse, fine,
    hot, send_one, recv_one, send_two, flat, y_own, y_far,
    sent, came, kept, fetched,
):
    e = lax.axis_index("energy")
    p = lax.axis_index("pair")
    core, z, x = lax.rem(e, 2), lax.rem(lax.div(e, 2), 16), lax.div(p, 2)
    side = lax.rem(p, 2)
    y = lax.div(e, 32) * 2 + side
    place = e * 2 + side
    owner = (1 - core) * EDEV + lax.div(e, 2) * 2 + side

    columns = []
    for dy in range(4):
        to_y = lax.rem(y + dy, 4)
        columns.append((lax.div(to_y, 2) * 16, lax.rem(to_y, 2)))

    def at_z(to_z, to_core, columns, act):
        for high, to_side in columns:
            chip = high + to_z
            act(
                chip * 2 + to_core,
                x * 2 + to_side,
                (chip * 2 + to_core) * 2 + to_side,
                (1 - to_core) * EDEV + chip * 2 + to_side,
            )

    def at(dz, to_core, columns, act):
        at_z(jnp.where(z + dz >= 16, z + dz - 16, z + dz), to_core, columns, act)

    def peers(cores, act, visit=at):
        def both_ways(near, carry):
            for to_core in cores:
                visit(7 - near, to_core, columns, act)
                visit(9 + near, to_core, columns, act)
            return carry

        for to_core in cores:
            visit(8, to_core, columns, act)
        lax.fori_loop(0, 7, both_ways, 0)
        for to_core in cores:
            visit(0, to_core, columns[1:], act)
            pl.when(core != to_core)(functools.partial(visit, 0, to_core, columns[:1], act))

    def some_peers(to_core, odd, act):
        even = 1 - lax.rem(odd + z, 2)

        def both_ways(near, carry):
            at(7 + even - 2 * near, to_core, columns, act)
            at(9 + even + 2 * near, to_core, columns, act)
            return carry

        lax.fori_loop(0, 3, both_ways, 0)
        at(1 + even, to_core, columns, act)
        at(15 + even, to_core, columns[1:], act)
        pl.when(jnp.logical_or(even == 0, core != to_core))(
            functools.partial(at, 15 + even, to_core, columns[:1], act)
        )

    barrier = pltpu.get_barrier_semaphore()

    def greet(to_e, to_p, to_place, to_owner):
        pl.semaphore_signal(barrier, inc=1, device_id=(to_e, to_p), device_id_type=MESH)

    peers((1, 0), greet)

    sources = (slot_hbm, less_hbm, greater_hbm, coarse_hbm, fine_hbm)
    places = (slot, less, greater, wide, fine)
    fetches = [pltpu.make_async_copy(a, b, fetched.at[i]) for i, (a, b) in enumerate(zip(sources, places))]
    for fetch in fetches:
        fetch.start()
    fetches[0].wait()
    hot[...] = one_hot(slot[...], 0, SLOTS)

    def remote(src, dst, turn, to_e, to_p):
        pltpu.make_async_remote_copy(
            src_ref=src,
            dst_ref=dst,
            send_sem=sent.at[turn],
            recv_sem=came.at[turn],
            device_id=(to_e, to_p),
            device_id_type=MESH,
        ).start()

    def out(to_e, to_p, to_place, to_owner):
        remote(send_one.at[to_owner], recv_one.at[place], 0, to_e, to_p)

    def back(to_e, to_p, to_place, to_owner):
        remote(send_two.at[to_place], recv_two.at[owner], 1, to_e, to_p)

    others = pl.ds(0, OWNERS - 1)

    def arrive(src, dst, target, turn):
        stay = pltpu.make_async_copy(src, dst, kept)
        stay.start()
        stay.wait()
        pltpu.make_async_copy(target.at[others], target.at[others], came.at[turn]).wait()

    fetches[1].wait()
    fetches[2].wait()
    value = jnp.concatenate([less[0], greater[0], less[1], greater[1]], axis=0)
    for to_core in (1, 0):
        half = SLOTS // 2
        ordered = dot(hot[(1 - to_core) * half : (2 - to_core) * half, :], value, ((1,), (1,)))
        parts = [ordered[:, part * 128 : (part + 1) * 128].reshape(EDEV, MINE, 128) for part in range(2)]
        send_one[(1 - to_core) * EDEV : (2 - to_core) * EDEV] = jnp.concatenate(parts, axis=1).astype(BF16)
        if to_core == 1:
            pl.semaphore_wait(barrier, OWNERS - 1)
        for odd in (1, 0):
            some_peers(to_core, odd, out)

    fetches[3].wait()
    fetches[4].wait()
    coarse[...] = wide[...].astype(BF16)
    arrive(send_one.at[owner], recv_one.at[place], recv_one, 0)
    correlate(recv_one, send_two, coarse, fine, flat, y_own, y_far)
    peers((1,), back)
    for to_z in range(EARLY_Z):
        at_z(to_z, 0, columns[1:], back)
        pl.when(jnp.logical_or(z != to_z, core != 0))(functools.partial(at_z, to_z, 0, columns[:1], back))

    def later(dz, to_core, columns, act):
        to_z = jnp.where(z + dz >= 16, z + dz - 16, z + dz)
        pl.when(to_z >= EARLY_Z)(functools.partial(at_z, to_z, to_core, columns, act))

    peers((0,), back, later)
    arrive(send_two.at[place], recv_two.at[owner], recv_two, 1)

    for turn, source in enumerate((send_one, send_two)):
        pltpu.make_async_copy(source.at[others], source.at[others], sent.at[turn]).wait()


def reorder(back_hbm, slot_hbm, less_hbm, greater_hbm, back, slot, less, greater, fetched, stored):
    fetches = [
        pltpu.make_async_copy(slot_hbm, slot, fetched.at[0]),
        pltpu.make_async_copy(back_hbm, back, fetched.at[1]),
    ]
    for fetch in fetches:
        fetch.start()
    fetches[0].wait()
    half = SLOTS // 2
    hot = one_hot(slot[...], 0, half)
    fetches[1].wait()
    result = None
    for part in range(2):
        value = back[part * EDEV : (part + 1) * EDEV].astype(F32)
        ordered = jnp.concatenate([value[:, :MINE].reshape(half, 128), value[:, MINE:].reshape(half, 128)], axis=1)
        term = dot(ordered.astype(BF16), hot, ((0,), (0,)))
        if part == 0:
            hot = one_hot(slot[...], half, half)
            result = term
        else:
            result = (result + term).astype(BF16)
    stores = []
    for part in range(2):
        for array, (kept, result_hbm) in enumerate(((less, less_hbm), (greater, greater_hbm))):
            kept[part] = result[(part * 2 + array) * N0 : (part * 2 + array + 1) * N0]
            stores.append(pltpu.make_async_copy(kept.at[part], result_hbm.at[part], stored.at[part, array]))
            stores[-1].start()
    for store in stores:
        store.wait()


def per_device(g_less, g_greater, pair_slot):
    coarse, fine = tables()
    hbm = pl.BlockSpec(memory_space=pltpu.HBM)
    grant = 60 * 1024 * 1024
    packets = pltpu.VMEM((OWNERS, ROWS, 128), BF16)
    back = pl.pallas_call(
        kernel,
        out_shape=jax.ShapeDtypeStruct((OWNERS, ROWS, 128), BF16),
        in_specs=[hbm] * 5,
        out_specs=hbm,
        scratch_shapes=[
            pltpu.VMEM((2, N0, SLOTS), BF16),
            pltpu.VMEM((2, N0, SLOTS), BF16),
            pltpu.VMEM((1, SLOTS), jnp.int32),
            pltpu.VMEM(coarse.shape, F32),
            pltpu.VMEM(coarse.shape, BF16),
            pltpu.VMEM(fine.shape, F32),
            pltpu.VMEM((SLOTS, SLOTS), BF16),
            packets,
            packets,
            packets,
            pltpu.VMEM((OWNERS * ROWS, 128), F32),
            pltpu.VMEM((MINE * K0, 512), BF16),
            pltpu.VMEM((MINE * K0, 512), BF16),
            pltpu.SemaphoreType.DMA((2,)),
            pltpu.SemaphoreType.DMA((2,)),
            pltpu.SemaphoreType.DMA,
            pltpu.SemaphoreType.DMA((5,)),
        ],
        compiler_params=pltpu.CompilerParams(collective_id=0, has_side_effects=True, vmem_limit_bytes=grant),
        cost_estimate=pl.CostEstimate(flops=4 * 10**9, bytes_accessed=4 * 10**6, transcendentals=0),
    )(g_less, g_greater, pair_slot, jnp.asarray(coarse), jnp.asarray(fine))
    shape = jax.ShapeDtypeStruct((2, N0, SLOTS), BF16)
    return pl.pallas_call(
        reorder,
        out_shape=(shape, shape),
        in_specs=[hbm, hbm],
        out_specs=(hbm, hbm),
        scratch_shapes=[
            packets,
            pltpu.VMEM((1, SLOTS), jnp.int32),
            pltpu.VMEM(shape.shape, BF16),
            pltpu.VMEM(shape.shape, BF16),
            pltpu.SemaphoreType.DMA((2,)),
            pltpu.SemaphoreType.DMA((2, 2)),
        ],
        compiler_params=pltpu.CompilerParams(vmem_limit_bytes=grant),
        cost_estimate=pl.CostEstimate(flops=10**9, bytes_accessed=10**6, transcendentals=0),
    )(back, pair_slot)


def solution(mesh):
    placed = (P(None, "energy", "pair"), P(None, "energy", "pair"), P("pair", None))
    return jax.shard_map(
        per_device,
        mesh=mesh,
        in_specs=placed,
        out_specs=(P(None, "energy", "pair"), P(None, "energy", "pair")),
        check_vma=False,
    )
```

```python
import functools
import math

import jax
import jax.numpy as jnp
import ml_dtypes
import numpy as np
from jax import lax
from jax.experimental import pallas as pl
from jax.experimental.pallas import tpu as pltpu
from jax.sharding import PartitionSpec as P

NE = 4096
N0 = 64
EDEV = 64
OWNERS = 2 * EDEV
SLOTS = 1024
MINE = SLOTS // OWNERS
ROWS = 2 * MINE
EARLY_Z = 2
K0 = 128
K1 = 64
LENGTH = 2 * NE
F32 = jnp.float32
BF16 = jnp.bfloat16
MESH = pl.DeviceIdType.MESH


def upper_lower(table):
    upper = table.astype(ml_dtypes.bfloat16)
    lower = (table - upper.astype(np.float64)).astype(ml_dtypes.bfloat16)
    return upper, lower


def cos_sin(rows, cols, period):
    angle = (np.arange(rows)[:, None] * np.arange(cols)[None, :] % period) * (2.0 * math.pi / period)
    return np.cos(angle), np.sin(angle)


def tables():
    lanes = lambda *parts: np.concatenate(parts, axis=1)
    both = lambda table: np.concatenate(upper_lower(table))
    straight = lambda part: np.kron(np.eye(2), part)
    crossed = lambda part: np.kron(np.eye(2)[::-1], part)
    c, s = cos_sin(K0, EDEV, K0)
    first = [lanes(*upper_lower(lanes(c, s))), lanes(*upper_lower(lanes(c, -s)))]
    c, s = cos_sin(N0, K1, K1)
    own = both(np.block([[straight(c), -straight(s)], [straight(s), straight(c)]]))
    far = both(np.block([[crossed(c), crossed(s)], [-crossed(s), crossed(c)]]))
    ahead = both(np.block([[straight(c), straight(s)], [-straight(s), straight(c)]]))
    behind = both(np.block([[crossed(c), crossed(s)], [crossed(s), -crossed(c)]]))
    c, s = cos_sin(EDEV, K0, K0)
    last = both(np.block([[c, -s], [s, c]]))
    coarse = np.concatenate(first + [own, far, ahead, behind, last])
    c, s = cos_sin(K0, N0, LENGTH)
    scale = 1.0 / (math.sqrt(NE) * LENGTH)
    fine = np.stack([lanes(c, c), lanes(s, s), lanes(s, s) * scale, -lanes(c, c) * scale])
    return coarse.reshape(-1, 128, 256).astype(np.float32), fine.astype(np.float32)


def dot(left, right, dims=((1,), (0,))):
    return lax.dot_general(left, right, (dims, ((), ())), preferred_element_type=F32)


def split(value):
    upper = value.astype(BF16)
    return upper, (value - upper.astype(F32)).astype(BF16)


def correlate(recv, send, coarse, fine, flat, y_own, y_far):
    first, own, far, ahead, behind, last = 0, 2, 6, 10, 14, 18
    flat[...] = recv[...].astype(F32).reshape(OWNERS * ROWS, 128)

    def line(side, part, slot):
        return pl.ds(side * ROWS + part * MINE + slot, EDEV, stride=2 * ROWS)

    def spectrum(side, slot, into):
        re, im = flat[line(side, 0, slot), :], flat[line(side, 1, slot), :]
        top = jnp.concatenate([re, im], axis=1).astype(BF16)
        bottom = jnp.concatenate([im, -re], axis=1).astype(BF16)
        step = dot(coarse[first + side], jnp.concatenate([top, bottom, top, bottom], axis=0))
        re, im = step[:, :128], step[:, 128:]
        c, s = fine[0], fine[1]
        if side == 0:
            re, im = re * c + im * s, im * c - re * s
        else:
            re, im = re * c - im * s, im * c + re * s
        into[pl.ds(slot * K0, K0), :] = jnp.concatenate(split(jnp.concatenate([re, im], axis=1)), axis=1)

    for slot in range(MINE):
        spectrum(0, slot, y_own)
        spectrum(1, slot, y_far)

    def triple(value, table):
        upper = coarse[table : table + 2].reshape(256, 256)
        lower = coarse[table + 2 : table + 4].reshape(256, 256)
        return dot(
            jnp.concatenate([value, value[:, :256]], axis=1), jnp.concatenate([upper, upper, lower], axis=0)
        )

    group = MINE
    for step in range(MINE // group):
        rows = pl.ds(step * (group * K0), group * K0)
        left, right = triple(y_own[rows, :], own), triple(y_far[rows, :], far)
        a, b, c, d = left[:, :128], left[:, 128:], right[:, :128], right[:, 128:]
        spec = jnp.concatenate(split(jnp.concatenate([a * c - b * d, a * d + b * c], axis=1)), axis=1)
        lags = (triple(spec, ahead), triple(spec, behind))
        for member in range(group):
            tops, bottoms = [], []
            for part in lags:
                re, im = part[member * K0 : (member + 1) * K0, :128], part[member * K0 : (member + 1) * K0, 128:]
                tops.append(re * fine[2] - im * fine[3])
                bottoms.append(re * fine[3] + im * fine[2])
            upper, lower = split(
                jnp.concatenate([jnp.concatenate(tops, axis=1), jnp.concatenate(bottoms, axis=1)], axis=0)
            )
            both = dot(coarse[last : last + 2].reshape(256, 256), upper)
            result = both[:128] + both[128:] + dot(coarse[last], lower)
            slot = step * group + member
            flat[line(0, 0, slot), :] = result[:EDEV, :128]
            flat[line(0, 1, slot), :] = result[EDEV:, :128]
            flat[line(1, 0, slot), :] = -result[:EDEV, 128:]
            flat[line(1, 1, slot), :] = result[EDEV:, 128:]

    send[...] = flat[...].reshape(OWNERS, ROWS, 128).astype(BF16)


def one_hot(slot, begin, rows):
    order = lax.broadcasted_iota(jnp.int32, (rows, SLOTS), 0) + begin
    return jnp.where(order == slot, 1.0, 0.0).astype(BF16)


def kernel(
    less_hbm, greater_hbm, slot_hbm, coarse_hbm, fine_hbm,
    recv_two,
    less, greater, slot, wide, coarse, fine,
    send_one, recv_one, send_two, flat, y_own, y_far,
    sent, came, kept, fetched,
):
    e = lax.axis_index("energy")
    p = lax.axis_index("pair")
    core, z, x = lax.rem(e, 2), lax.rem(lax.div(e, 2), 16), lax.div(p, 2)
    side = lax.rem(p, 2)
    y = lax.div(e, 32) * 2 + side
    place = e * 2 + side
    owner = (1 - core) * EDEV + lax.div(e, 2) * 2 + side

    columns = []
    for dy in (0, 2, 1, 3):
        to_y = lax.rem(y + dy, 4)
        columns.append((lax.div(to_y, 2) * 16, lax.rem(to_y, 2)))

    def at_z(to_z, to_core, columns, act):
        for high, to_side in columns:
            chip = high + to_z
            act(
                chip * 2 + to_core,
                x * 2 + to_side,
                (chip * 2 + to_core) * 2 + to_side,
                (1 - to_core) * EDEV + chip * 2 + to_side,
            )

    def at(dz, to_core, columns, act):
        at_z(jnp.where(z + dz >= 16, z + dz - 16, z + dz), to_core, columns, act)

    def peers(cores, act, visit=at):
        def both_ways(near, carry):
            for to_core in cores:
                visit(7 - near, to_core, columns, act)
                visit(9 + near, to_core, columns, act)
            return carry

        for to_core in cores:
            visit(8, to_core, columns, act)
        lax.fori_loop(0, 7, both_ways, 0)
        for to_core in cores:
            visit(0, to_core, columns[1:], act)
            pl.when(core != to_core)(functools.partial(visit, 0, to_core, columns[:1], act))

    def some_peers(to_core, odd, act):
        even = 1 - lax.rem(odd + z, 2)

        def both_ways(near, carry):
            at(7 + even - 2 * near, to_core, columns, act)
            at(9 + even + 2 * near, to_core, columns, act)
            return carry

        lax.fori_loop(0, 3, both_ways, 0)
        at(1 + even, to_core, columns, act)
        at(15 + even, to_core, columns[1:], act)
        pl.when(jnp.logical_or(even == 0, core != to_core))(
            functools.partial(at, 15 + even, to_core, columns[:1], act)
        )

    barrier = pltpu.get_barrier_semaphore()

    def greet(to_e, to_p, to_place, to_owner):
        pl.semaphore_signal(barrier, inc=1, device_id=(to_e, to_p), device_id_type=MESH)

    peers((1, 0), greet)

    sources = (slot_hbm, less_hbm, greater_hbm, coarse_hbm, fine_hbm)
    places = (slot, less, greater, wide, fine)
    fetches = [pltpu.make_async_copy(a, b, fetched.at[i]) for i, (a, b) in enumerate(zip(sources, places))]
    for fetch in fetches:
        fetch.start()
    fetches[0].wait()

    def remote(src, dst, turn, to_e, to_p):
        pltpu.make_async_remote_copy(
            src_ref=src,
            dst_ref=dst,
            send_sem=sent.at[turn],
            recv_sem=came.at[turn],
            device_id=(to_e, to_p),
            device_id_type=MESH,
        ).start()

    def out(to_e, to_p, to_place, to_owner):
        remote(send_one.at[to_owner], recv_one.at[place], 0, to_e, to_p)

    def back(to_e, to_p, to_place, to_owner):
        remote(send_two.at[to_place], recv_two.at[owner], 1, to_e, to_p)

    others = pl.ds(0, OWNERS - 1)

    def arrive(src, dst, target, turn):
        stay = pltpu.make_async_copy(src, dst, kept)
        stay.start()
        stay.wait()
        pltpu.make_async_copy(target.at[others], target.at[others], came.at[turn]).wait()

    fetches[1].wait()
    fetches[2].wait()
    value = jnp.concatenate([less[0], greater[0], less[1], greater[1]], axis=0)
    for to_core in (1, 0):
        half = SLOTS // 2
        ordered = dot(one_hot(slot[...], (1 - to_core) * half, half), value, ((1,), (1,)))
        parts = [ordered[:, part * 128 : (part + 1) * 128].reshape(EDEV, MINE, 128) for part in range(2)]
        send_one[(1 - to_core) * EDEV : (2 - to_core) * EDEV] = jnp.concatenate(parts, axis=1).astype(BF16)
        if to_core == 1:
            pl.semaphore_wait(barrier, OWNERS - 1)
        for odd in (1, 0):
            some_peers(to_core, odd, out)

    fetches[3].wait()
    fetches[4].wait()
    coarse[...] = wide[...].astype(BF16)
    arrive(send_one.at[owner], recv_one.at[place], recv_one, 0)
    correlate(recv_one, send_two, coarse, fine, flat, y_own, y_far)
    peers((1,), back)
    for to_z in range(EARLY_Z):
        at_z(to_z, 0, columns[1:], back)
        pl.when(jnp.logical_or(z != to_z, core != 0))(functools.partial(at_z, to_z, 0, columns[:1], back))

    def later(dz, to_core, columns, act):
        to_z = jnp.where(z + dz >= 16, z + dz - 16, z + dz)
        pl.when(to_z >= EARLY_Z)(functools.partial(at_z, to_z, to_core, columns, act))

    peers((0,), back, later)
    arrive(send_two.at[place], recv_two.at[owner], recv_two, 1)

    for turn, source in enumerate((send_one, send_two)):
        pltpu.make_async_copy(source.at[others], source.at[others], sent.at[turn]).wait()


def reorder(back_hbm, slot_hbm, less_hbm, greater_hbm, back, slot, less, greater, fetched, stored):
    fetches = [
        pltpu.make_async_copy(slot_hbm, slot, fetched.at[0]),
        pltpu.make_async_copy(back_hbm, back, fetched.at[1]),
    ]
    for fetch in fetches:
        fetch.start()
    fetches[0].wait()
    half = SLOTS // 2
    hot = one_hot(slot[...], 0, half)
    fetches[1].wait()
    result = None
    for part in range(2):
        value = back[part * EDEV : (part + 1) * EDEV].astype(F32)
        ordered = jnp.concatenate([value[:, :MINE].reshape(half, 128), value[:, MINE:].reshape(half, 128)], axis=1)
        term = dot(ordered.astype(BF16), hot, ((0,), (0,)))
        if part == 0:
            hot = one_hot(slot[...], half, half)
            result = term
        else:
            result = (result + term).astype(BF16)
    stores = []
    for part in range(2):
        for array, (kept, result_hbm) in enumerate(((less, less_hbm), (greater, greater_hbm))):
            kept[part] = result[(part * 2 + array) * N0 : (part * 2 + array + 1) * N0]
            stores.append(pltpu.make_async_copy(kept.at[part], result_hbm.at[part], stored.at[part, array]))
            stores[-1].start()
    for store in stores:
        store.wait()


def per_device(g_less, g_greater, pair_slot):
    coarse, fine = tables()
    hbm = pl.BlockSpec(memory_space=pltpu.HBM)
    grant = 60 * 1024 * 1024
    packets = pltpu.VMEM((OWNERS, ROWS, 128), BF16)
    back = pl.pallas_call(
        kernel,
        out_shape=jax.ShapeDtypeStruct((OWNERS, ROWS, 128), BF16),
        in_specs=[hbm] * 5,
        out_specs=hbm,
        scratch_shapes=[
            pltpu.VMEM((2, N0, SLOTS), BF16),
            pltpu.VMEM((2, N0, SLOTS), BF16),
            pltpu.VMEM((1, SLOTS), jnp.int32),
            pltpu.VMEM(coarse.shape, F32),
            pltpu.VMEM(coarse.shape, BF16),
            pltpu.VMEM(fine.shape, F32),
            packets,
            packets,
            packets,
            pltpu.VMEM((OWNERS * ROWS, 128), F32),
            pltpu.VMEM((MINE * K0, 512), BF16),
            pltpu.VMEM((MINE * K0, 512), BF16),
            pltpu.SemaphoreType.DMA((2,)),
            pltpu.SemaphoreType.DMA((2,)),
            pltpu.SemaphoreType.DMA,
            pltpu.SemaphoreType.DMA((5,)),
        ],
        compiler_params=pltpu.CompilerParams(collective_id=0, has_side_effects=True, vmem_limit_bytes=grant),
        cost_estimate=pl.CostEstimate(flops=4 * 10**9, bytes_accessed=4 * 10**6, transcendentals=0),
    )(g_less, g_greater, pair_slot, jnp.asarray(coarse), jnp.asarray(fine))
    shape = jax.ShapeDtypeStruct((2, N0, SLOTS), BF16)
    return pl.pallas_call(
        reorder,
        out_shape=(shape, shape),
        in_specs=[hbm, hbm],
        out_specs=(hbm, hbm),
        scratch_shapes=[
            packets,
            pltpu.VMEM((1, SLOTS), jnp.int32),
            pltpu.VMEM(shape.shape, BF16),
            pltpu.VMEM(shape.shape, BF16),
            pltpu.SemaphoreType.DMA((2,)),
            pltpu.SemaphoreType.DMA((2, 2)),
        ],
        compiler_params=pltpu.CompilerParams(vmem_limit_bytes=grant),
        cost_estimate=pl.CostEstimate(flops=10**9, bytes_accessed=10**6, transcendentals=0),
    )(back, pair_slot)


def solution(mesh):
    placed = (P(None, "energy", "pair"), P(None, "energy", "pair"), P("pair", None))
    return jax.shard_map(
        per_device,
        mesh=mesh,
        in_specs=placed,
        out_specs=(P(None, "energy", "pair"), P(None, "energy", "pair")),
        check_vma=False,
    )
```

```python
import functools
import math

import jax
import jax.numpy as jnp
import ml_dtypes
import numpy as np
from jax import lax
from jax.experimental import pallas as pl
from jax.experimental.pallas import tpu as pltpu
from jax.sharding import PartitionSpec as P

NE = 4096
N0 = 64
EDEV = 64
OWNERS = 2 * EDEV
SLOTS = 1024
MINE = SLOTS // OWNERS
ROWS = 2 * MINE
EARLY_Z = 3
K0 = 128
K1 = 64
LENGTH = 2 * NE
F32 = jnp.float32
BF16 = jnp.bfloat16
MESH = pl.DeviceIdType.MESH


def upper_lower(table):
    upper = table.astype(ml_dtypes.bfloat16)
    lower = (table - upper.astype(np.float64)).astype(ml_dtypes.bfloat16)
    return upper, lower


def cos_sin(rows, cols, period):
    angle = (np.arange(rows)[:, None] * np.arange(cols)[None, :] % period) * (2.0 * math.pi / period)
    return np.cos(angle), np.sin(angle)


def tables():
    lanes = lambda *parts: np.concatenate(parts, axis=1)
    both = lambda table: np.concatenate(upper_lower(table))
    straight = lambda part: np.kron(np.eye(2), part)
    crossed = lambda part: np.kron(np.eye(2)[::-1], part)
    c, s = cos_sin(K0, EDEV, K0)
    first = [lanes(*upper_lower(lanes(c, s))), lanes(*upper_lower(lanes(c, -s)))]
    c, s = cos_sin(N0, K1, K1)
    own = both(np.block([[straight(c), -straight(s)], [straight(s), straight(c)]]))
    far = both(np.block([[crossed(c), crossed(s)], [-crossed(s), crossed(c)]]))
    ahead = both(np.block([[straight(c), straight(s)], [-straight(s), straight(c)]]))
    behind = both(np.block([[crossed(c), crossed(s)], [crossed(s), -crossed(c)]]))
    c, s = cos_sin(EDEV, K0, K0)
    last = both(np.block([[c, -s], [s, c]]))
    coarse = np.concatenate(first + [own, far, ahead, behind, last])
    c, s = cos_sin(K0, N0, LENGTH)
    scale = 1.0 / (math.sqrt(NE) * LENGTH)
    fine = np.stack([lanes(c, c), lanes(s, s), lanes(s, s) * scale, -lanes(c, c) * scale])
    return coarse.reshape(-1, 128, 256).astype(np.float32), fine.astype(np.float32)


def dot(left, right, dims=((1,), (0,))):
    return lax.dot_general(left, right, (dims, ((), ())), preferred_element_type=F32)


def split(value):
    upper = value.astype(BF16)
    return upper, (value - upper.astype(F32)).astype(BF16)


def correlate(recv, send, coarse, fine, flat, y_own, y_far):
    first, own, far, ahead, behind, last = 0, 2, 6, 10, 14, 18
    flat[...] = recv[...].astype(F32).reshape(OWNERS * ROWS, 128)

    def line(side, part, slot):
        return pl.ds(side * ROWS + part * MINE + slot, EDEV, stride=2 * ROWS)

    def spectrum(side, slot, into):
        re, im = flat[line(side, 0, slot), :], flat[line(side, 1, slot), :]
        top = jnp.concatenate([re, im], axis=1).astype(BF16)
        bottom = jnp.concatenate([im, -re], axis=1).astype(BF16)
        step = dot(coarse[first + side], jnp.concatenate([top, bottom, top, bottom], axis=0))
        re, im = step[:, :128], step[:, 128:]
        c, s = fine[0], fine[1]
        if side == 0:
            re, im = re * c + im * s, im * c - re * s
        else:
            re, im = re * c - im * s, im * c + re * s
        into[pl.ds(slot * K0, K0), :] = jnp.concatenate(split(jnp.concatenate([re, im], axis=1)), axis=1)

    for slot in range(MINE):
        spectrum(0, slot, y_own)
        spectrum(1, slot, y_far)

    def triple(value, table):
        upper = coarse[table : table + 2].reshape(256, 256)
        lower = coarse[table + 2 : table + 4].reshape(256, 256)
        return dot(
            jnp.concatenate([value, value[:, :256]], axis=1), jnp.concatenate([upper, upper, lower], axis=0)
        )

    group = MINE
    for step in range(MINE // group):
        rows = pl.ds(step * (group * K0), group * K0)
        left, right = triple(y_own[rows, :], own), triple(y_far[rows, :], far)
        a, b, c, d = left[:, :128], left[:, 128:], right[:, :128], right[:, 128:]
        spec = jnp.concatenate(split(jnp.concatenate([a * c - b * d, a * d + b * c], axis=1)), axis=1)
        lags = (triple(spec, ahead), triple(spec, behind))
        for member in range(group):
            tops, bottoms = [], []
            for part in lags:
                re, im = part[member * K0 : (member + 1) * K0, :128], part[member * K0 : (member + 1) * K0, 128:]
                tops.append(re * fine[2] - im * fine[3])
                bottoms.append(re * fine[3] + im * fine[2])
            upper, lower = split(
                jnp.concatenate([jnp.concatenate(tops, axis=1), jnp.concatenate(bottoms, axis=1)], axis=0)
            )
            both = dot(coarse[last : last + 2].reshape(256, 256), upper)
            result = both[:128] + both[128:] + dot(coarse[last], lower)
            slot = step * group + member
            flat[line(0, 0, slot), :] = result[:EDEV, :128]
            flat[line(0, 1, slot), :] = result[EDEV:, :128]
            flat[line(1, 0, slot), :] = -result[:EDEV, 128:]
            flat[line(1, 1, slot), :] = result[EDEV:, 128:]

    send[...] = flat[...].reshape(OWNERS, ROWS, 128).astype(BF16)


def one_hot(slot, begin, rows):
    order = lax.broadcasted_iota(jnp.int32, (rows, SLOTS), 0) + begin
    return jnp.where(order == slot, 1.0, 0.0).astype(BF16)


def kernel(
    less_hbm, greater_hbm, slot_hbm, coarse_hbm, fine_hbm,
    recv_two,
    less, greater, slot, wide, coarse, fine,
    send_one, recv_one, send_two, flat, y_own, y_far,
    sent, came, kept, fetched,
):
    e = lax.axis_index("energy")
    p = lax.axis_index("pair")
    core, z, x = lax.rem(e, 2), lax.rem(lax.div(e, 2), 16), lax.div(p, 2)
    side = lax.rem(p, 2)
    y = lax.div(e, 32) * 2 + side
    place = e * 2 + side
    owner = (1 - core) * EDEV + lax.div(e, 2) * 2 + side

    columns = []
    for dy in (0, 2, 1, 3):
        to_y = lax.rem(y + dy, 4)
        columns.append((lax.div(to_y, 2) * 16, lax.rem(to_y, 2)))

    def at_z(to_z, to_core, columns, act):
        for high, to_side in columns:
            chip = high + to_z
            act(
                chip * 2 + to_core,
                x * 2 + to_side,
                (chip * 2 + to_core) * 2 + to_side,
                (1 - to_core) * EDEV + chip * 2 + to_side,
            )

    def at(dz, to_core, columns, act):
        at_z(jnp.where(z + dz >= 16, z + dz - 16, z + dz), to_core, columns, act)

    def peers(cores, act, visit=at):
        def both_ways(near, carry):
            for to_core in cores:
                visit(7 - near, to_core, columns, act)
                visit(9 + near, to_core, columns, act)
            return carry

        for to_core in cores:
            visit(8, to_core, columns, act)
        lax.fori_loop(0, 7, both_ways, 0)
        for to_core in cores:
            visit(0, to_core, columns[1:], act)
            pl.when(core != to_core)(functools.partial(visit, 0, to_core, columns[:1], act))

    def some_peers(to_core, odd, act):
        even = 1 - lax.rem(odd + z, 2)

        def both_ways(near, carry):
            at(7 + even - 2 * near, to_core, columns, act)
            at(9 + even + 2 * near, to_core, columns, act)
            return carry

        lax.fori_loop(0, 3, both_ways, 0)
        at(1 + even, to_core, columns, act)
        at(15 + even, to_core, columns[1:], act)
        pl.when(jnp.logical_or(even == 0, core != to_core))(
            functools.partial(at, 15 + even, to_core, columns[:1], act)
        )

    barrier = pltpu.get_barrier_semaphore()

    def greet(to_e, to_p, to_place, to_owner):
        pl.semaphore_signal(barrier, inc=1, device_id=(to_e, to_p), device_id_type=MESH)

    peers((1, 0), greet)

    sources = (slot_hbm, less_hbm, greater_hbm, coarse_hbm, fine_hbm)
    places = (slot, less, greater, wide, fine)
    fetches = [pltpu.make_async_copy(a, b, fetched.at[i]) for i, (a, b) in enumerate(zip(sources, places))]
    for fetch in fetches:
        fetch.start()
    fetches[0].wait()

    def remote(src, dst, turn, to_e, to_p):
        pltpu.make_async_remote_copy(
            src_ref=src,
            dst_ref=dst,
            send_sem=sent.at[turn],
            recv_sem=came.at[turn],
            device_id=(to_e, to_p),
            device_id_type=MESH,
        ).start()

    def out(to_e, to_p, to_place, to_owner):
        remote(send_one.at[to_owner], recv_one.at[place], 0, to_e, to_p)

    def back(to_e, to_p, to_place, to_owner):
        remote(send_two.at[to_place], recv_two.at[owner], 1, to_e, to_p)

    others = pl.ds(0, OWNERS - 1)

    def arrive(src, dst, target, turn):
        stay = pltpu.make_async_copy(src, dst, kept)
        stay.start()
        stay.wait()
        pltpu.make_async_copy(target.at[others], target.at[others], came.at[turn]).wait()

    fetches[1].wait()
    fetches[2].wait()
    value = jnp.concatenate([less[0], greater[0], less[1], greater[1]], axis=0)
    for to_core in (1, 0):
        half = SLOTS // 2
        ordered = dot(one_hot(slot[...], (1 - to_core) * half, half), value, ((1,), (1,)))
        parts = [ordered[:, part * 128 : (part + 1) * 128].reshape(EDEV, MINE, 128) for part in range(2)]
        send_one[(1 - to_core) * EDEV : (2 - to_core) * EDEV] = jnp.concatenate(parts, axis=1).astype(BF16)
        if to_core == 1:
            pl.semaphore_wait(barrier, OWNERS - 1)
        for odd in (1, 0):
            some_peers(to_core, odd, out)

    fetches[3].wait()
    fetches[4].wait()
    coarse[...] = wide[...].astype(BF16)
    arrive(send_one.at[owner], recv_one.at[place], recv_one, 0)
    correlate(recv_one, send_two, coarse, fine, flat, y_own, y_far)
    peers((1,), back)
    for to_z in range(EARLY_Z):
        at_z(to_z, 0, columns[1:], back)
        pl.when(jnp.logical_or(z != to_z, core != 0))(functools.partial(at_z, to_z, 0, columns[:1], back))

    def later(dz, to_core, columns, act):
        to_z = jnp.where(z + dz >= 16, z + dz - 16, z + dz)
        pl.when(to_z >= EARLY_Z)(functools.partial(at_z, to_z, to_core, columns, act))

    peers((0,), back, later)
    arrive(send_two.at[place], recv_two.at[owner], recv_two, 1)

    for turn, source in enumerate((send_one, send_two)):
        pltpu.make_async_copy(source.at[others], source.at[others], sent.at[turn]).wait()


def reorder(back_hbm, slot_hbm, less_hbm, greater_hbm, back, slot, less, greater, fetched, stored):
    fetches = [
        pltpu.make_async_copy(slot_hbm, slot, fetched.at[0]),
        pltpu.make_async_copy(back_hbm, back, fetched.at[1]),
    ]
    for fetch in fetches:
        fetch.start()
    fetches[0].wait()
    half = SLOTS // 2
    hot = one_hot(slot[...], 0, half)
    fetches[1].wait()
    result = None
    for part in range(2):
        value = back[part * EDEV : (part + 1) * EDEV].astype(F32)
        ordered = jnp.concatenate([value[:, :MINE].reshape(half, 128), value[:, MINE:].reshape(half, 128)], axis=1)
        term = dot(ordered.astype(BF16), hot, ((0,), (0,)))
        if part == 0:
            hot = one_hot(slot[...], half, half)
            result = term
        else:
            result = (result + term).astype(BF16)
    stores = []
    for part in range(2):
        for array, (kept, result_hbm) in enumerate(((less, less_hbm), (greater, greater_hbm))):
            kept[part] = result[(part * 2 + array) * N0 : (part * 2 + array + 1) * N0]
            stores.append(pltpu.make_async_copy(kept.at[part], result_hbm.at[part], stored.at[part, array]))
            stores[-1].start()
    for store in stores:
        store.wait()


def per_device(g_less, g_greater, pair_slot):
    coarse, fine = tables()
    hbm = pl.BlockSpec(memory_space=pltpu.HBM)
    grant = 60 * 1024 * 1024
    packets = pltpu.VMEM((OWNERS, ROWS, 128), BF16)
    back = pl.pallas_call(
        kernel,
        out_shape=jax.ShapeDtypeStruct((OWNERS, ROWS, 128), BF16),
        in_specs=[hbm] * 5,
        out_specs=hbm,
        scratch_shapes=[
            pltpu.VMEM((2, N0, SLOTS), BF16),
            pltpu.VMEM((2, N0, SLOTS), BF16),
            pltpu.VMEM((1, SLOTS), jnp.int32),
            pltpu.VMEM(coarse.shape, F32),
            pltpu.VMEM(coarse.shape, BF16),
            pltpu.VMEM(fine.shape, F32),
            packets,
            packets,
            packets,
            pltpu.VMEM((OWNERS * ROWS, 128), F32),
            pltpu.VMEM((MINE * K0, 512), BF16),
            pltpu.VMEM((MINE * K0, 512), BF16),
            pltpu.SemaphoreType.DMA((2,)),
            pltpu.SemaphoreType.DMA((2,)),
            pltpu.SemaphoreType.DMA,
            pltpu.SemaphoreType.DMA((5,)),
        ],
        compiler_params=pltpu.CompilerParams(collective_id=0, has_side_effects=True, vmem_limit_bytes=grant),
        cost_estimate=pl.CostEstimate(flops=4 * 10**9, bytes_accessed=4 * 10**6, transcendentals=0),
    )(g_less, g_greater, pair_slot, jnp.asarray(coarse), jnp.asarray(fine))
    shape = jax.ShapeDtypeStruct((2, N0, SLOTS), BF16)
    return pl.pallas_call(
        reorder,
        out_shape=(shape, shape),
        in_specs=[hbm, hbm],
        out_specs=(hbm, hbm),
        scratch_shapes=[
            packets,
            pltpu.VMEM((1, SLOTS), jnp.int32),
            pltpu.VMEM(shape.shape, BF16),
            pltpu.VMEM(shape.shape, BF16),
            pltpu.SemaphoreType.DMA((2,)),
            pltpu.SemaphoreType.DMA((2, 2)),
        ],
        compiler_params=pltpu.CompilerParams(vmem_limit_bytes=grant),
        cost_estimate=pl.CostEstimate(flops=10**9, bytes_accessed=10**6, transcendentals=0),
    )(back, pair_slot)


def solution(mesh):
    placed = (P(None, "energy", "pair"), P(None, "energy", "pair"), P("pair", None))
    return jax.shard_map(
        per_device,
        mesh=mesh,
        in_specs=placed,
        out_specs=(P(None, "energy", "pair"), P(None, "energy", "pair")),
        check_vma=False,
    )
```
